32 devices in a mesh: ctx: 16 (over z, x, core), tp: 2 (over y).
Axes of the slice: x: 2, y: 2, z: 4, core: 2. Of those that a mesh axis runs over, the one named last changes fastest.
Arguments:
- record_lengths: int32 [16], replicated, may hold values from 1 to 1728, 3072 in all
- query_heads: bfloat16 [3072, 8192], P(('ctx', 'tp')), may hold values from -36 to 36
- key_heads: bfloat16 [3072, 1024], P(('ctx', 'tp')), may hold values from -36 to 36
- value_heads: bfloat16 [3072, 1024], P(('ctx', 'tp')), may hold values from -5 to 5
- out_grad: bfloat16 [3072, 8192], P(('ctx', 'tp')), may hold values from -5 to 5
- gate_input: bfloat16 [3072, 8192], P('ctx', 'tp'), may hold values from -5 to 5
- key_input: bfloat16 [3072, 8192], P('ctx', 'tp'), may hold values from -5 to 5
- value_input: bfloat16 [3072, 8192], P('ctx', 'tp'), may hold values from -5 to 5
- hyena_grad: bfloat16 [3072, 8192], P('ctx', 'tp'), may hold values from -5 to 5
- short_filter: float32 [3, 3, 8192], P(None, None, 'tp'), may hold values from -3 to 3
- long_filter: float32 [7, 512], P(None, 'tp'), may hold values from -3 to 3
Outputs:
- attn_out: bfloat16 [3072, 8192], P('ctx', 'tp')
- grad_query: bfloat16 [3072, 8192], P('ctx', 'tp')
- grad_key: bfloat16 [3072, 1024], P('ctx', 'tp')
- grad_value: bfloat16 [3072, 1024], P('ctx', 'tp')
- hyena_out: bfloat16 [3072, 8192], P('ctx', 'tp')
- grad_gate_in: bfloat16 [3072, 8192], P('ctx', 'tp')
- grad_key_in: bfloat16 [3072, 8192], P('ctx', 'tp')
- grad_value_in: bfloat16 [3072, 8192], P('ctx', 'tp')
The draws below stay inside these ranges and needn't reach their ends.
Inputs may be any that keep to these rules, and one draw needn't show every extreme that they name: `record_lengths`: the 16 records lie end to end and fill the 3072 tokens; the longest has exactly 1728 tokens.
All inputs are finite; a program needn't handle non-finite values.
Results may differ from the reference program's by a relative error of at most 0.035.
Values may be sent and summed in bfloat16 or wider, within the bound.
No kernel may reach another device: no remote copies, remote signals or barrier semaphores. Data moves between devices by JAX's collectives and lax.ppermute only.
A program may use at most 128 MiB of HBM per device.

```python
import math
from functools import partial
import jax
import jax.numpy as jnp
import numpy as np
from jax import lax

HD = 128
QH = 64
KVH = 8
CH = 8192
GROUP = 16
TAPS = 7
SHORT = 3
TOK_DEV = 192
NREC = 16
LEN = 3072
MOST = 1728


def paired_heads(key):
    base = jax.random.fold_in(key, 11)
    parts = jax.random.split(base, 2)
    group = QH // KVH
    raw_keys = jax.random.truncated_normal(parts[0], -4.0, 4.0, (LEN, KVH, HD), jnp.float32)
    raw_queries = jax.random.truncated_normal(parts[1], -4.0, 4.0, (LEN, KVH, group, HD), jnp.float32)
    key_rows = raw_keys
    query_rows = raw_queries
    return (query_rows.reshape(LEN, QH * HD), key_rows.reshape(LEN, KVH * HD))


def draw_query_heads(key, part):
    return paired_heads(key)[0].astype(jnp.bfloat16)


def draw_key_heads(key, part):
    return paired_heads(key)[1].astype(jnp.bfloat16)


def shard_levels(own_key, extent, cuts, smallest, high):
    level = 1.0
    for position, shards_of in cuts:
        draws = jax.random.uniform(jax.random.fold_in(jax.random.fold_in(own_key, 6), position), (shards_of,), jnp.float32, smallest / len(cuts), high / len(cuts))
        level = level * jnp.repeat(jnp.exp(draws), extent[position] // shards_of).reshape((-1,) + (1,) * (len(extent) - 1 - position))
    return level


def split_up(number_of, total, reach, skew):
    weights = [(1 << 20) // math.isqrt(standing ** skew) + 1 for standing in range(2, number_of + 1)]
    rest, given = total - reach - (number_of - 1), [1] * (number_of - 1)
    while rest > 0:
        free = [i for i in range(number_of - 1) if given[i] < reach]
        whole, left = sum([weights[i] for i in free]), rest
        for i in free:
            extra = min(reach - given[i], max(1, left * weights[i] // whole), rest)
            given[i] = given[i] + extra
            rest = rest - extra
    return np.array([reach] + given)


def uneven_parts(rng, count, total, reach, lean):
    if count == 2:
        one = jax.random.randint(rng, (), max(1, total - reach), min(reach, total - 1) + 1)
        return jnp.stack([one, total - one])
    tallies = jnp.asarray(split_up(count, total, reach, lean), jnp.int32)
    pairs = (count - 1) // 2
    source_of, taker = tallies[1:1 + 2 * pairs:2], tallies[2:2 + 2 * pairs:2]
    margin = jnp.minimum(source_of - 1, reach - taker)
    moved = jax.random.randint(jax.random.fold_in(rng, 1), (pairs,), 0, 1 << 20) % (margin + 1)
    tallies = tallies.at[1:1 + 2 * pairs:2].set(source_of - moved).at[2:2 + 2 * pairs:2].set(taker + moved)
    return tallies[jax.random.permutation(jax.random.fold_in(rng, 2), count)]


def noise(own_key, dims, scale, bound, cuts=(), kind=jnp.bfloat16):
    gain = shard_levels(own_key, dims, cuts, -0.22, 0.18) if cuts else 1.0
    values = jax.random.normal(own_key, dims, jnp.float32) * scale * gain
    return jnp.minimum(jnp.maximum(values, -bound), bound).astype(kind)


def setup_inputs(seed: int = 0) -> dict:
    keys = jax.random.split(jax.random.key(seed), 12)
    record_lengths = uneven_parts(keys[0], NREC, LEN, MOST, 2).astype(jnp.int32)
    query_heads = draw_query_heads(jax.random.fold_in(keys[11], 71), 0)
    key_heads = draw_key_heads(jax.random.fold_in(keys[11], 71), 0)
    value_heads = noise(keys[3], (LEN, KVH * HD), 1.0, 5.0, ((0, 32),))
    out_grad = noise(keys[4], (LEN, QH * HD), 1.0, 5.0, ((0, 32),))
    gate_input = noise(keys[5], (LEN, CH), 1.0, 5.0, ((0, 16), (1, 2)))
    key_input = noise(keys[6], (LEN, CH), 1.0, 5.0, ((0, 16), (1, 2)))
    value_input = noise(keys[7], (LEN, CH), 1.0, 5.0, ((0, 16), (1, 2)))
    hyena_grad = noise(keys[8], (LEN, CH), 1.0, 5.0, ((0, 16), (1, 2)))
    short_filter = noise(keys[9], (3, SHORT, CH), 0.6, 3.0, ((2, 2),), jnp.float32)
    long_filter = noise(keys[10], (TAPS, CH // GROUP), 0.4, 3.0, ((1, 2),), jnp.float32)
    return dict(record_lengths=record_lengths, query_heads=query_heads, key_heads=key_heads, value_heads=value_heads, out_grad=out_grad, gate_input=gate_input, key_input=key_input, value_input=value_input, hyena_grad=hyena_grad, short_filter=short_filter, long_filter=long_filter)


def segment_ids(record_lengths, positions):
    ends = jnp.cumsum(record_lengths)
    starts = ends - record_lengths
    return lax.optimization_barrier(jnp.sum((starts[None, :] <= positions[:, None]).astype(jnp.int32), axis=1)) - 1

def bf16_round(values):
    return lax.optimization_barrier(values.astype(jnp.bfloat16)).astype(jnp.float32)

def attention(record_lengths, query_heads, key_heads, value_heads, out_grad):
    group = QH // KVH
    scale = HD ** (-0.5)
    blocks = LEN // TOK_DEV
    positions = jnp.arange(LEN, dtype=jnp.int32)
    segs = segment_ids(record_lengths, positions)
    q_all = query_heads.reshape(blocks, TOK_DEV, KVH, group, HD).transpose(2, 0, 1, 3, 4)
    g_all = out_grad.reshape(blocks, TOK_DEV, KVH, group, HD).transpose(2, 0, 1, 3, 4)
    k_all = key_heads.reshape(LEN, KVH, HD).transpose(1, 0, 2)
    v_all = value_heads.reshape(LEN, KVH, HD).transpose(1, 0, 2)
    q_pos = positions.reshape(blocks, TOK_DEV)
    q_seg = segs.reshape(blocks, TOK_DEV)

    def one_head(operands):
        q_head, g_head, k_head, v_head = operands
        key32 = k_head.astype(jnp.float32)
        val32 = v_head.astype(jnp.float32)

        def one_block(carry, block):
            dk_sum, dv_sum = carry
            q_blk, g_blk, pos_blk, seg_blk = block
            q32 = q_blk.astype(jnp.float32)
            g32 = g_blk.astype(jnp.float32)
            allowed = (positions[None, :] <= pos_blk[:, None]) & (segs[None, :] == seg_blk[:, None])
            allowed = allowed[None]
            scores = jnp.einsum('tgd,sd->gts', q32, key32) * scale
            peak = lax.optimization_barrier(jnp.max(jnp.where(allowed, scores, -jnp.inf), axis=2))
            weights = jnp.where(allowed, jnp.exp(scores - peak[:, :, None]), 0.0)
            total = lax.optimization_barrier(jnp.sum(weights, axis=2))
            mixed = jnp.einsum('gts,sd->gtd', bf16_round(weights), val32) / total[:, :, None]
            out_b = mixed.astype(jnp.bfloat16)
            lse = peak + jnp.log(total)
            delta = lax.optimization_barrier(jnp.sum(g32.transpose(1, 0, 2) * out_b.astype(jnp.float32), axis=2))
            probs = jnp.where(allowed, jnp.exp(scores - lse[:, :, None]), 0.0)
            probs_b = bf16_round(probs)
            dv_sum = dv_sum + jnp.einsum('gts,tgd->sd', probs_b, g32)
            dprobs = jnp.einsum('tgd,sd->gts', g32, val32)
            dscores = bf16_round(probs * (dprobs - delta[:, :, None]))
            dq_blk = scale * jnp.einsum('gts,sd->tgd', dscores, key32)
            dk_sum = dk_sum + scale * jnp.einsum('gts,tgd->sd', dscores, q32)
            return ((dk_sum, dv_sum), (out_b.transpose(1, 0, 2), dq_blk.astype(jnp.bfloat16)))
        zeros = jnp.zeros((LEN, HD), jnp.float32)
        sums, stacked = lax.scan(one_block, (zeros, zeros), (q_head, g_head, q_pos, q_seg))
        return (stacked[0], stacked[1], sums[0].astype(jnp.bfloat16), sums[1].astype(jnp.bfloat16))
    outs, dqs, dks, dvs = lax.map(one_head, (q_all, g_all, k_all, v_all))
    attn_out = outs.transpose(1, 2, 0, 3, 4).reshape(LEN, QH * HD)
    grad_query = dqs.transpose(1, 2, 0, 3, 4).reshape(LEN, QH * HD)
    grad_key = dks.transpose(1, 0, 2).reshape(LEN, KVH * HD)
    grad_value = dvs.transpose(1, 0, 2).reshape(LEN, KVH * HD)
    return (attn_out, grad_query, grad_key, grad_value)

def shifted(values, amount):
    return jnp.pad(values, ((amount, 0), (0, 0)))[:values.shape[0]]

def hyena_forward(short_filter, long_filter, gate_in, key_in, value_in):

    def featurize(values, taps):
        result = taps[0] * values
        for index in range(1, SHORT):
            result = result + taps[index] * shifted(values, index)
        return result
    gate_f = featurize(gate_in, short_filter[0])
    key_f = featurize(key_in, short_filter[1])
    value_f = featurize(value_in, short_filter[2])
    mixed = key_f * value_f
    per_channel = jnp.repeat(long_filter, GROUP, axis=1)
    conv = per_channel[0] * mixed
    for index in range(1, TAPS):
        conv = conv + per_channel[index] * shifted(mixed, index)
    return gate_f * conv

def reference(record_lengths, query_heads, key_heads, value_heads, out_grad, gate_input, key_input, value_input, hyena_grad, short_filter, long_filter):
    attn_out, grad_query, grad_key, grad_value = attention(record_lengths, query_heads, key_heads, value_heads, out_grad)
    forward = partial(hyena_forward, short_filter, long_filter)
    hyena_val, pullback = jax.vjp(forward, gate_input.astype(jnp.float32), key_input.astype(jnp.float32), value_input.astype(jnp.float32))
    grads = pullback(hyena_grad.astype(jnp.float32))
    return (attn_out, grad_query, grad_key, grad_value, hyena_val.astype(jnp.bfloat16), grads[0].astype(jnp.bfloat16), grads[1].astype(jnp.bfloat16), grads[2].astype(jnp.bfloat16))
```

```python
import functools

import jax
import jax.numpy as jnp
import numpy as np
from jax import lax
from jax.experimental import pallas as pl
from jax.experimental.pallas import tpu as pltpu
from jax.sharding import PartitionSpec as P

HD = 128
QH = 64
KVH = 8
GROUP = 16
TAPS = 7
SHORT = 3
HALO = 8
PLANE = 4
KB = 192
NEG = -1e30
SCALE = HD ** (-0.5)
TO_EXP2 = SCALE * 1.4426950408889634
VMEM = 48 * 1024 * 1024


def hyena_kernel(
    gate_ref,
    key_ref,
    value_ref,
    grad_ref,
    before_ref,
    after_ref,
    short_ref,
    long_ref,
    out_ref,
    dgate_ref,
    dkey_ref,
    dvalue_ref,
):
    tokens, width = gate_ref.shape
    rows = tokens + 2 * HALO

    def chunk(index, carry):
        lanes = pl.ds(pl.multiple_of(index * HD, HD), HD)
        before = before_ref[:, lanes].astype(jnp.float32)
        after = after_ref[:, lanes].astype(jnp.float32)

        def padded(ref, which):
            part = slice(which * HALO, (which + 1) * HALO)
            return jnp.concatenate(
                [before[part], ref[:, lanes].astype(jnp.float32), after[part]], axis=0
            )

        def earlier(values, amount):
            return pltpu.roll(values, amount, 0) if amount else values

        def later(values, amount):
            return pltpu.roll(values, rows - amount, 0) if amount else values

        short = short_ref[:, lanes]
        long = long_ref[:, lanes]

        def featurize(values, which):
            result = short[which * SHORT][None] * values
            for tap in range(1, SHORT):
                result = result + short[which * SHORT + tap][None] * earlier(values, tap)
            return result

        def unfeaturize(grads, which):
            result = short[which * SHORT][None] * grads
            for tap in range(1, SHORT):
                result = result + short[which * SHORT + tap][None] * later(grads, tap)
            return result[HALO : HALO + tokens].astype(jnp.bfloat16)

        key_f = featurize(padded(key_ref, 1), 1)
        value_f = featurize(padded(value_ref, 2), 2)
        mixed = key_f * value_f
        conv = long[0][None] * mixed
        for tap in range(1, TAPS):
            conv = conv + long[tap][None] * earlier(mixed, tap)
        gate_f = featurize(padded(gate_ref, 0), 0)
        out_ref[:, lanes] = (gate_f * conv)[HALO : HALO + tokens].astype(jnp.bfloat16)
        grad = padded(grad_ref, 3)
        dgate_ref[:, lanes] = unfeaturize(grad * conv, 0)
        dconv = grad * gate_f
        dmixed = long[0][None] * dconv
        for tap in range(1, TAPS):
            dmixed = dmixed + long[tap][None] * later(dconv, tap)
        dkey_ref[:, lanes] = unfeaturize(dmixed * value_f, 1)
        dvalue_ref[:, lanes] = unfeaturize(dmixed * key_f, 2)
        return carry

    lax.fori_loop(0, width // HD, chunk, 0)


def hyena(streams, before, after, short_filter, long_filter):
    tokens, channels = streams[0].shape
    width = min(512, channels)
    block = pl.BlockSpec((tokens, width), lambda i: (0, i))
    edge = pl.BlockSpec((4 * HALO, width), lambda i: (0, i))
    taps = long_filter.shape[0]
    return pl.pallas_call(
        hyena_kernel,
        grid=(channels // width,),
        in_specs=[block] * 4
        + [edge, edge]
        + [
            pl.BlockSpec((3 * SHORT, width), lambda i: (0, i)),
            pl.BlockSpec((taps, width), lambda i: (0, i)),
        ],
        out_specs=[block] * 4,
        out_shape=[jax.ShapeDtypeStruct((tokens, channels), jnp.bfloat16)] * 4,
        compiler_params=pltpu.CompilerParams(vmem_limit_bytes=VMEM),
        cost_estimate=pl.CostEstimate(
            flops=100 * tokens * channels, bytes_accessed=16 * tokens * channels, transcendentals=0
        ),
        name="hyena",
    )(*streams, before, after, short_filter, long_filter)


def attention_kernel(
    bases_ref,
    bounds_ref,
    q_ref,
    g_ref,
    kv_ref,
    pos_ref,
    low_ref,
    out_ref,
    dq_ref,
    dkv_ref,
    k_t,
    v_t,
    dk_sum,
    dv_sum,
    scores,
    weights,
    q_rows,
    q_t,
    g_rows,
    g_t,
    peak8,
    total8,
    out_t,
    dq_t,
):
    step = pl.program_id(1)
    blocks = dk_sum.shape[0]
    size = q_ref.shape[0]
    heads = q_ref.shape[1] // HD
    rows = size * heads
    f32 = jnp.float32
    bf16 = jnp.bfloat16

    @pl.when(step == 0)
    def _():
        def prepare(b, carry):
            part = pl.ds(pl.multiple_of(b * KB, KB), KB)
            k_t[b] = kv_ref[part, :HD].T
            v_t[b] = kv_ref[part, HD:].T
            dk_sum[b] = jnp.zeros((KB, HD), f32)
            dv_sum[b] = jnp.zeros((KB, HD), f32)
            return carry

        lax.fori_loop(0, blocks, prepare, 0)

    for h in range(heads):
        part = slice(h * size, (h + 1) * size)
        q_rows[part] = q_ref[:, h * HD : (h + 1) * HD]
        g_rows[part] = g_ref[:, h * HD : (h + 1) * HD]
    q_t[...] = q_rows[...].T
    g_t[...] = g_rows[...].T
    peak8[...] = jnp.full((8, rows), NEG, f32)
    total8[...] = jnp.zeros((8, rows), f32)
    out_t[...] = jnp.zeros((HD, rows), f32)
    dq_t[...] = jnp.zeros((HD, rows), f32)

    q_first = bounds_ref[step, 0]
    low_first = bounds_ref[step, 1]
    low_last = bounds_ref[step, 2]

    def live(b):
        base = bases_ref[b]
        return (base <= q_first + (size - 1)) & (base + (KB - 1) >= low_first)

    def whole(b):
        base = bases_ref[b]
        return (base + (KB - 1) <= q_first) & (base >= low_last)

    def key_block(b):
        return kv_ref[pl.ds(pl.multiple_of(b * KB, KB), KB), :HD]

    def value_block(b):
        return kv_ref[pl.ds(pl.multiple_of(b * KB, KB), KB), HD:]

    def fold(values, combine):
        result = values[0:8]
        for start in range(8, values.shape[0], 8):
            result = combine(result, values[start : start + 8])
        return result

    def score_pass(b, carry):
        @pl.when(live(b))
        def _():
            s = jnp.dot(key_block(b), q_t[...], preferred_element_type=f32)

            @pl.when(whole(b))
            def _():
                scores[b] = s
                peak8[...] = jnp.maximum(peak8[...], fold(s, jnp.maximum))

            @pl.when(jnp.logical_not(whole(b)))
            def _():
                key_pos = bases_ref[b] + lax.broadcasted_iota(jnp.int32, (KB, rows), 0)
                allowed = (key_pos <= pos_ref[0]) & (key_pos >= low_ref[0])
                masked = jnp.where(allowed, s, NEG)
                scores[b] = masked
                peak8[...] = jnp.maximum(peak8[...], fold(masked, jnp.maximum))

        return carry

    lax.fori_loop(0, blocks, score_pass, 0)
    peak = jnp.max(peak8[...], axis=0, keepdims=True) * TO_EXP2

    def weight_pass(b, carry):
        @pl.when(live(b))
        def _():
            w = jnp.exp2(scores[b] * TO_EXP2 - peak)
            total8[...] += fold(w, jnp.add)
            w_b = w.astype(bf16)
            weights[b] = w_b
            out_t[...] += jnp.dot(v_t[b], w_b, preferred_element_type=f32)

        return carry

    lax.fori_loop(0, blocks, weight_pass, 0)
    inverse = 1.0 / jnp.sum(total8[...], axis=0, keepdims=True)
    out_b = (out_t[...] * inverse).astype(bf16)
    g_wide = g_t[...].astype(f32)
    delta = jnp.sum(g_wide * out_b.astype(f32), axis=0, keepdims=True) * inverse
    g_scaled = (g_wide * inverse).astype(bf16)
    g_t[...] = g_scaled
    g_rows[...] = g_scaled.T
    out_rows = out_b.T
    for h in range(heads):
        out_ref[:, h * HD : (h + 1) * HD] = out_rows[h * size : (h + 1) * size]

    def grad_pass(b, carry):
        @pl.when(live(b))
        def _():
            dp = jnp.dot(value_block(b), g_t[...], preferred_element_type=f32)
            w_b = weights[b]
            ds = (w_b.astype(f32) * (dp - delta)).astype(bf16)
            dv_sum[b] += jnp.dot(w_b, g_rows[...], preferred_element_type=f32)
            dk_sum[b] += jnp.dot(ds, q_rows[...], preferred_element_type=f32)
            dq_t[...] += jnp.dot(k_t[b], ds, preferred_element_type=f32)

        return carry

    lax.fori_loop(0, blocks, grad_pass, 0)
    dq_rows = (dq_t[...] * SCALE).astype(bf16).T
    for h in range(heads):
        dq_ref[:, h * HD : (h + 1) * HD] = dq_rows[h * size : (h + 1) * size]

    @pl.when(step == pl.num_programs(1) - 1)
    def _():
        def finish(b, carry):
            part = pl.ds(pl.multiple_of(b * KB, KB), KB)
            dkv_ref[part, :HD] = (dk_sum[b] * SCALE).astype(bf16)
            dkv_ref[part, HD:] = dv_sum[b].astype(bf16)
            return carry

        lax.fori_loop(0, blocks, finish, 0)


def attention(q, g, kv, bases, bounds, pos, low, size, token_block):
    tokens, width = q.shape
    keys, kv_width = kv.shape
    kv_local = kv_width // (2 * HD)
    heads = width // HD // kv_local
    rows = size * heads
    blocks = keys // KB
    steps = tokens // size
    bf16 = jnp.bfloat16
    f32 = jnp.float32
    taken = pl.BlockSpec((size, heads * HD), lambda h, i, *_: (i, h))
    given = pl.BlockSpec((size, heads * HD), lambda h, i, *_: (token_block(i), h))
    window = pl.BlockSpec((keys, 2 * HD), lambda h, i, *_: (0, h))
    lanes = pl.BlockSpec((1, 1, rows), lambda h, i, *_: (i, 0, 0))
    pairs = tokens * width // HD * keys
    return pl.pallas_call(
        attention_kernel,
        grid_spec=pltpu.PrefetchScalarGridSpec(
            num_scalar_prefetch=2,
            grid=(kv_local, steps),
            in_specs=[taken, taken, window, lanes, lanes],
            out_specs=[given, given, window],
            scratch_shapes=[
                pltpu.VMEM((blocks, HD, KB), bf16),
                pltpu.VMEM((blocks, HD, KB), bf16),
                pltpu.VMEM((blocks, KB, HD), f32),
                pltpu.VMEM((blocks, KB, HD), f32),
                pltpu.VMEM((blocks, KB, rows), f32),
                pltpu.VMEM((blocks, KB, rows), bf16),
                pltpu.VMEM((rows, HD), bf16),
                pltpu.VMEM((HD, rows), bf16),
                pltpu.VMEM((rows, HD), bf16),
                pltpu.VMEM((HD, rows), bf16),
                pltpu.VMEM((8, rows), f32),
                pltpu.VMEM((8, rows), f32),
                pltpu.VMEM((HD, rows), f32),
                pltpu.VMEM((HD, rows), f32),
            ],
        ),
        out_shape=[
            jax.ShapeDtypeStruct((tokens, width), bf16),
            jax.ShapeDtypeStruct((tokens, width), bf16),
            jax.ShapeDtypeStruct((keys, kv_width), bf16),
        ],
        compiler_params=pltpu.CompilerParams(vmem_limit_bytes=VMEM),
        cost_estimate=pl.CostEstimate(
            flops=12 * HD * pairs, bytes_accessed=8 * tokens * width, transcendentals=pairs
        ),
        name="attention",
    )(bases, bounds, q, g, kv, pos, low)


def body(
    record_lengths,
    query_heads,
    key_heads,
    value_heads,
    out_grad,
    gate_input,
    key_input,
    value_input,
    hyena_grad,
    short_filter,
    long_filter,
):
    ctx = lax.axis_size("ctx")
    tp = lax.axis_size("tp")
    own_ctx = lax.axis_index("ctx")
    own_tp = lax.axis_index("tp")
    piece = query_heads.shape[0]
    tokens = piece * tp
    window = tokens * ctx
    most = window // 2 + 192
    split = 2 if (KVH // tp) % 2 == 0 else 1
    kv_local = KVH // tp // split
    unit = tokens * split
    lanes = PLANE // split
    plane = unit * lanes
    reach = (most - 1) // plane
    tail = -(-(most - 1 - reach * plane) // KB) * KB

    members = [
        [t * ctx + n * split + c for t in range(tp) for c in range(split)]
        for n in range(ctx // split)
    ]

    def share(values):
        return lax.all_to_all(
            values, ("tp", "ctx"), 1, 0, axis_index_groups=members, tiled=True
        )

    pairs_of = functools.partial(lax.ppermute, axis_name="ctx")

    def token_order(index):
        return index % split * tp + index // split

    kv = jnp.concatenate(
        [key_heads.reshape(piece, KVH, HD), value_heads.reshape(piece, KVH, HD)], axis=2
    ).reshape(piece, KVH * 2 * HD)
    kv = share(kv)
    own_kv = (
        kv.reshape(tp, split, piece, -1).transpose(1, 0, 2, 3).reshape(unit, kv_local * 2 * HD)
    )
    q = share(query_heads)
    g = share(out_grad)

    lane = own_ctx // split % lanes
    level = own_ctx // PLANE

    def across(values, distance):
        return pairs_of(values, perm=[(i, i ^ (distance * split)) for i in range(ctx)])

    def up(values):
        return pairs_of(values, perm=[(i, i + PLANE) for i in range(ctx - PLANE)])

    def down(values):
        return pairs_of(values, perm=[(i + PLANE, i) for i in range(ctx - PLANE)])

    far = (reach + 1) * PLANE - (lanes - 1) * split
    far_pairs = [
        (i, i + far) for i in range(ctx - far) if i // split % lanes == lanes - 1
    ]

    columns = [own_kv]
    for _ in range(reach):
        columns.append(up(columns[-1]))
    tail_kv = pairs_of(own_kv[unit - tail :], perm=far_pairs)
    pieces = [tail_kv]
    starts_at = [jnp.where(lane == 0, (level - reach) * plane - tail, -window)]
    for back in range(reach + 1):
        for distance in range(lanes):
            held = columns[back]
            pieces.append(held if distance == 0 else across(held, distance))
            starts_at.append((level - back) * plane + (lane ^ distance) * unit)
    keys = jnp.concatenate(pieces, axis=0)
    bases = jnp.concatenate(
        [
            start + np.arange(0, part.shape[0], KB, dtype=np.int32)
            for start, part in zip(starts_at, pieces)
        ]
    )

    ends = jnp.cumsum(record_lengths)
    size = 96
    steps = unit // size
    q_first = level * plane + lane * unit
    order = np.concatenate(
        [np.arange(piece) + token_order(i) * piece for i in range(tp * split)]
    ).astype(np.int32)
    if piece < size:
        q = q.reshape(tp, split, piece, -1).transpose(1, 0, 2, 3).reshape(unit, -1)
        g = g.reshape(tp, split, piece, -1).transpose(1, 0, 2, 3).reshape(unit, -1)
        order = np.arange(unit, dtype=np.int32)
    firsts = order.reshape(steps, size)[:, 0]
    pos = q_first + order
    low = jnp.max(
        jnp.where(ends[None, :] <= pos[:, None], ends[None, :], 0), axis=1
    ).reshape(steps, size)
    pos = pos.reshape(steps, size)
    group = QH // KVH
    bounds = jnp.stack([pos[:, 0], low[:, 0], low[:, -1]], axis=1)
    pos_rows = jnp.tile(pos, (1, group)).reshape(steps, 1, size * group)
    low_rows = jnp.tile(low, (1, group)).reshape(steps, 1, size * group)

    if piece < size:
        token_block = lambda i: i
    else:
        per = piece // size
        token_block = lambda i: token_order(i // per) * per + i % per

    attn, dq, terms = attention(
        q, g, keys, bases, bounds, pos_rows, low_rows, size, token_block
    )

    tail_term = pairs_of(terms[:tail], perm=[(j, i) for i, j in far_pairs])
    offset = tail
    sums = []
    for back in range(reach + 1):
        total = terms[offset : offset + unit].astype(jnp.float32)
        for distance in range(1, lanes):
            sent = terms[offset + distance * unit : offset + (distance + 1) * unit]
            total = total + across(sent, distance).astype(jnp.float32)
        sums.append(total)
        offset = offset + plane
    running = sums[reach]
    for back in range(reach - 1, -1, -1):
        running = sums[back] + down(running.astype(jnp.bfloat16)).astype(jnp.float32)
    owned = jnp.concatenate(
        [running[: unit - tail], running[unit - tail :] + tail_term.astype(jnp.float32)], axis=0
    ).astype(jnp.bfloat16)

    def settle(values):
        if split == 1:
            return values
        return lax.all_to_all(
            values,
            "ctx",
            0,
            1,
            axis_index_groups=[[n * split + c for c in range(split)] for n in range(ctx // split)],
            tiled=True,
        )

    attn_out = settle(attn)
    grad_query = settle(dq)
    grads = settle(owned).reshape(tokens, split * kv_local, 2, HD)
    grad_key = grads[:, :, 0].reshape(tokens, -1)
    grad_value = grads[:, :, 1].reshape(tokens, -1)

    streams = (gate_input, key_input, value_input, hyena_grad)
    heads = jnp.concatenate([s[:HALO] for s in streams], axis=0)
    tails = jnp.concatenate([s[tokens - HALO :] for s in streams], axis=0)
    before = pairs_of(tails, perm=[(i, i + 1) for i in range(ctx - 1)])
    after = pairs_of(heads, perm=[(i + 1, i) for i in range(ctx - 1)])
    hyena_val, grad_gate, grad_keyx, grad_valuex = hyena(
        streams,
        before,
        after,
        short_filter.reshape(3 * SHORT, -1),
        jnp.repeat(long_filter, GROUP, axis=1),
    )
    return (
        attn_out,
        grad_query,
        grad_key,
        grad_value,
        hyena_val,
        grad_gate,
        grad_keyx,
        grad_valuex,
    )


def solution(mesh):
    rows = P(("ctx", "tp"), None)
    both = P("ctx", "tp")
    return jax.shard_map(
        body,
        mesh=mesh,
        in_specs=(P(), rows, rows, rows, rows, both, both, both, both)
        + (P(None, None, "tp"), P(None, "tp")),
        out_specs=(both,) * 8,
        check_vma=False,
    )
```

```python
import functools

import jax
import jax.numpy as jnp
import numpy as np
from jax import lax
from jax.experimental import pallas as pl
from jax.experimental.pallas import tpu as pltpu
from jax.sharding import PartitionSpec as P

HD = 128
QH = 64
KVH = 8
GROUP = 16
TAPS = 7
SHORT = 3
HALO = 8
PLANE = 4
KB = 256
NEG = -1e30
SCALE = HD ** (-0.5)
TO_EXP2 = SCALE * 1.4426950408889634
VMEM = 48 * 1024 * 1024


def hyena_kernel(
    gate_ref,
    key_ref,
    value_ref,
    grad_ref,
    before_ref,
    after_ref,
    short_ref,
    long_ref,
    out_ref,
    dgate_ref,
    dkey_ref,
    dvalue_ref,
):
    first = pl.program_id(0)
    tokens, width = gate_ref.shape
    rows = tokens + 2 * HALO

    def chunk(index, carry):
        lanes = pl.ds(pl.multiple_of(index * HD, HD), HD)
        before = before_ref[:, lanes].astype(jnp.float32)
        after = after_ref[:, lanes].astype(jnp.float32)

        def padded(ref, which):
            part = slice(which * HALO, (which + 1) * HALO)
            return jnp.concatenate(
                [before[part], ref[:, lanes].astype(jnp.float32), after[part]], axis=0
            )

        def earlier(values, amount):
            return pltpu.roll(values, amount, 0) if amount else values

        def later(values, amount):
            return pltpu.roll(values, rows - amount, 0) if amount else values

        group = lax.broadcasted_iota(jnp.int32, (long_ref.shape[1], HD), 0)
        channel = first * width + index * HD
        channel = channel + lax.broadcasted_iota(jnp.int32, (long_ref.shape[1], HD), 1)
        long = jnp.dot(
            long_ref[...],
            (group == channel // GROUP).astype(jnp.float32),
            precision=lax.Precision.HIGHEST,
            preferred_element_type=jnp.float32,
        )

        def short(which, tap):
            return short_ref[which, tap : tap + 1, lanes]

        def featurize(values, which):
            result = short(which, 0) * values
            for tap in range(1, SHORT):
                result = result + short(which, tap) * earlier(values, tap)
            return result

        def unfeaturize(grads, which):
            result = short(which, 0) * grads
            for tap in range(1, SHORT):
                result = result + short(which, tap) * later(grads, tap)
            return result[HALO : HALO + tokens].astype(jnp.bfloat16)

        key_f = featurize(padded(key_ref, 1), 1)
        value_f = featurize(padded(value_ref, 2), 2)
        mixed = key_f * value_f
        conv = long[0:1] * mixed
        for tap in range(1, TAPS):
            conv = conv + long[tap : tap + 1] * earlier(mixed, tap)
        gate_f = featurize(padded(gate_ref, 0), 0)
        out_ref[:, lanes] = (gate_f * conv)[HALO : HALO + tokens].astype(jnp.bfloat16)
        grad = padded(grad_ref, 3)
        dgate_ref[:, lanes] = unfeaturize(grad * conv, 0)
        dconv = grad * gate_f
        dmixed = long[0:1] * dconv
        for tap in range(1, TAPS):
            dmixed = dmixed + long[tap : tap + 1] * later(dconv, tap)
        dkey_ref[:, lanes] = unfeaturize(dmixed * value_f, 1)
        dvalue_ref[:, lanes] = unfeaturize(dmixed * key_f, 2)
        return carry

    lax.fori_loop(0, width // HD, chunk, 0)


def hyena(streams, before, after, short_filter, long_filter):
    tokens, channels = streams[0].shape
    width = min(512, channels)
    block = pl.BlockSpec((tokens, width), lambda i: (0, i))
    edge = pl.BlockSpec((4 * HALO, width), lambda i: (0, i))
    return pl.pallas_call(
        hyena_kernel,
        grid=(channels // width,),
        in_specs=[block] * 4
        + [edge, edge]
        + [
            pl.BlockSpec((3, SHORT, width), lambda i: (0, 0, i)),
            pl.BlockSpec(long_filter.shape, lambda i: (0, 0)),
        ],
        out_specs=[block] * 4,
        out_shape=[jax.ShapeDtypeStruct((tokens, channels), jnp.bfloat16)] * 4,
        compiler_params=pltpu.CompilerParams(vmem_limit_bytes=VMEM),
        cost_estimate=pl.CostEstimate(
            flops=100 * tokens * channels, bytes_accessed=16 * tokens * channels, transcendentals=0
        ),
        name="hyena",
    )(*streams, before, after, short_filter, long_filter)


def pack_kernel(stacked, *refs):
    sources, target = refs[:-1], refs[-1]
    for index, ref in enumerate(sources):
        if stacked:
            target[0, index] = ref[...]
        else:
            width = ref.shape[1]
            target[0, :, index * width : (index + 1) * width] = ref[...]


def pack(parts, slots, stacked):
    rows, columns = parts[0].shape
    width = columns // slots
    count = len(parts)
    if stacked:
        shape = (slots, count, rows, width)
        target = pl.BlockSpec((1, count, rows, width), lambda i: (i, 0, 0, 0))
    else:
        shape = (slots, rows, count * width)
        target = pl.BlockSpec((1, rows, count * width), lambda i: (i, 0, 0))
    return pl.pallas_call(
        functools.partial(pack_kernel, stacked),
        grid=(slots,),
        in_specs=[pl.BlockSpec((rows, width), lambda i: (0, i))] * count,
        out_specs=target,
        out_shape=jax.ShapeDtypeStruct(shape, parts[0].dtype),
        name="pack",
    )(*parts)


def attention_kernel(pieces, steps, *refs):
    (info_ref, bounds_ref, q_ref, g_ref), refs = refs[:4], refs[4:]
    piece_refs, refs = refs[:pieces], refs[pieces:]
    (pos_ref, low_ref), refs = refs[:2], refs[2:]
    out_refs, refs = refs[:steps], refs[steps:]
    dq_refs, refs = refs[:steps], refs[steps:]
    term_refs, refs = refs[:pieces], refs[pieces:]
    kv, k_t, v_t, dk_sum, dv_sum, scores, weights, dscores = refs[:8]
    q_rows, q_t, g_rows, g_t, peak8, total8, out_t, dq_t = refs[8:]
    step = pl.program_id(1)
    blocks = k_t.shape[0]
    heads = q_ref.shape[2] // HD
    size = q_ref.shape[0] * q_ref.shape[1]
    rows = size * heads
    f32 = jnp.float32
    bf16 = jnp.bfloat16
    chunks = [slice(start, min(start + 256, rows)) for start in range(0, rows, 256)]
    origin = info_ref[0]

    def rows_of(b):
        return pl.ds(pl.multiple_of(b * KB, KB), KB)

    def piece_rows(index):
        count = piece_refs[index].shape[1]
        return pl.ds(pl.multiple_of(info_ref[2 + index], 64), count)

    @pl.when(step == 0)
    def _():
        filled = sum(ref.shape[1] for ref in piece_refs)
        if filled < kv.shape[0]:
            kv[filled:] = jnp.zeros((kv.shape[0] - filled, 2 * HD), bf16)
        for index in range(pieces):
            kv[piece_rows(index), :HD] = piece_refs[index][0]
            kv[piece_rows(index), HD:] = piece_refs[index][1]
        dk_sum[...] = jnp.zeros(dk_sum.shape, f32)
        dv_sum[...] = jnp.zeros(dv_sum.shape, f32)

        def prepare(b, carry):
            k_t[b] = kv[rows_of(b), :HD].T
            v_t[b] = kv[rows_of(b), HD:].T
            return carry

        lax.fori_loop(0, blocks, prepare, 0)

    for h in range(heads):
        part = slice(h * size, (h + 1) * size)
        q_rows[part] = q_ref[:, :, h * HD : (h + 1) * HD].reshape(size, HD)
        g_rows[part] = g_ref[:, :, h * HD : (h + 1) * HD].reshape(size, HD)
    q_t[...] = q_rows[...].T
    g_t[...] = g_rows[...].T
    peak8[...] = jnp.full((8, rows), NEG, f32)
    total8[...] = jnp.zeros((8, rows), f32)
    out_t[...] = jnp.zeros((HD, rows), f32)
    dq_t[...] = jnp.zeros((HD, rows), f32)

    q_first = bounds_ref[step, 0]
    low_first = bounds_ref[step, 1]
    low_last = bounds_ref[step, 2]
    first = (low_first - origin) // KB
    last = (q_first + (size - 1) - origin) // KB + 1

    def fold(values, combine):
        result = values[0:8]
        for start in range(8, values.shape[0], 8):
            result = combine(result, values[start : start + 8])
        return result

    def score_pass(b, carry):
        base = origin + b * KB
        whole = (base + (KB - 1) <= q_first) & (base >= low_last)

        @pl.when(whole)
        def _():
            for part in chunks:
                s = jnp.dot(kv[rows_of(b), :HD], q_t[:, part], preferred_element_type=f32)
                scores[b - first, :, part] = s
                peak8[:, part] = jnp.maximum(peak8[:, part], fold(s, jnp.maximum))

        @pl.when(jnp.logical_not(whole))
        def _():
            for part in chunks:
                s = jnp.dot(kv[rows_of(b), :HD], q_t[:, part], preferred_element_type=f32)
                key_pos = base + lax.broadcasted_iota(jnp.int32, s.shape, 0)
                allowed = (key_pos <= pos_ref[0, :, part]) & (key_pos >= low_ref[0, :, part])
                s = jnp.where(allowed, s, NEG)
                scores[b - first, :, part] = s
                peak8[:, part] = jnp.maximum(peak8[:, part], fold(s, jnp.maximum))

        return carry

    lax.fori_loop(first, last, score_pass, 0)
    peak = jnp.max(peak8[...], axis=0, keepdims=True) * TO_EXP2

    def weight_pass(b, carry):
        for part in chunks:
            w = jnp.exp2(scores[b - first, :, part] * TO_EXP2 - peak[:, part])
            total8[:, part] += fold(w, jnp.add)
            w_b = w.astype(bf16)
            weights[b - first, :, part] = w_b
            out_t[:, part] += jnp.dot(v_t[b], w_b, preferred_element_type=f32)
        return carry

    lax.fori_loop(first, last, weight_pass, 0)
    inverse = 1.0 / jnp.sum(total8[...], axis=0, keepdims=True)
    out_b = (out_t[...] * inverse).astype(bf16)
    g_wide = g_t[...].astype(f32)
    delta = jnp.sum(g_wide * out_b.astype(f32), axis=0, keepdims=True) * inverse
    g_scaled = (g_wide * inverse).astype(bf16)
    g_t[...] = g_scaled
    g_rows[...] = g_scaled.T

    def give(refs, wide):
        for which in range(steps):

            @pl.when(step == which)
            def _():
                for h in range(heads):
                    refs[which][:, h * HD : (h + 1) * HD] = wide[h * size : (h + 1) * size]

    give(out_refs, out_b.T)

    def grad_pass(b, carry):
        for part in chunks:
            dp = jnp.dot(kv[rows_of(b), HD:], g_t[:, part], preferred_element_type=f32)
            w = weights[b - first, :, part].astype(f32)
            dscores[:, part] = (w * (dp - delta[:, part])).astype(bf16)
        dv_sum[rows_of(b)] += jnp.dot(weights[b - first], g_rows[...], preferred_element_type=f32)
        dk_sum[rows_of(b)] += jnp.dot(dscores[...], q_rows[...], preferred_element_type=f32)
        dq_t[...] += jnp.dot(k_t[b], dscores[...], preferred_element_type=f32)
        return carry

    lax.fori_loop(first, last, grad_pass, 0)
    give(dq_refs, (dq_t[...] * SCALE).astype(bf16).T)

    @pl.when(step == steps - 1)
    def _():
        for index in range(pieces):
            term_refs[index][0] = (dk_sum[piece_rows(index)] * SCALE).astype(bf16)
            term_refs[index][1] = dv_sum[piece_rows(index)].astype(bf16)


def attention(qg, kv_pieces, info, bounds, pos, low, out_width, most):
    groups, run, width = qg.shape
    width = width // 2
    steps, _, rows = pos.shape
    kv_local = kv_pieces[0].shape[2] // HD
    columns = width // kv_local
    heads = columns // HD
    size = rows // heads
    pieces = len(kv_pieces)
    keys = -(-sum(part.shape[1] for part in kv_pieces) // KB) * KB
    blocks = keys // KB
    live = min(blocks, (most + size - 3) // KB + 2)
    bf16 = jnp.bfloat16
    f32 = jnp.float32

    def taken(first):
        return pl.BlockSpec(
            (groups, run // steps, columns), lambda h, i, info, bounds: (0, bounds[i, 3], first + h)
        )

    kv_specs = [
        pl.BlockSpec((2, part.shape[1], HD), lambda h, i, *_: (0, 0, h)) for part in kv_pieces
    ]
    lanes = pl.BlockSpec((1, 1, rows), lambda h, i, *_: (i, 0, 0))
    sent = pl.BlockSpec((size, columns), lambda h, i, *_: (0, h))
    kept = pl.BlockSpec((size, columns), lambda h, i, info, bounds: (0, info[1] * kv_local + h))
    out_specs = [sent] * (steps - 1) + [kept]
    out_shape = [jax.ShapeDtypeStruct((size, width), bf16)] * (steps - 1)
    out_shape = out_shape + [jax.ShapeDtypeStruct((size, out_width), bf16)]
    pairs = size * steps * heads * kv_local * keys
    results = pl.pallas_call(
        functools.partial(attention_kernel, pieces, steps),
        grid_spec=pltpu.PrefetchScalarGridSpec(
            num_scalar_prefetch=2,
            grid=(kv_local, steps),
            in_specs=[taken(0), taken(kv_local)] + kv_specs + [lanes, lanes],
            out_specs=out_specs + out_specs + kv_specs,
            scratch_shapes=[
                pltpu.VMEM((keys, 2 * HD), bf16),
                pltpu.VMEM((blocks, HD, KB), bf16),
                pltpu.VMEM((blocks, HD, KB), bf16),
                pltpu.VMEM((keys, HD), f32),
                pltpu.VMEM((keys, HD), f32),
                pltpu.VMEM((live, KB, rows), f32),
                pltpu.VMEM((live, KB, rows), bf16),
                pltpu.VMEM((KB, rows), bf16),
                pltpu.VMEM((rows, HD), bf16),
                pltpu.VMEM((HD, rows), bf16),
                pltpu.VMEM((rows, HD), bf16),
                pltpu.VMEM((HD, rows), bf16),
                pltpu.VMEM((8, rows), f32),
                pltpu.VMEM((8, rows), f32),
                pltpu.VMEM((HD, rows), f32),
                pltpu.VMEM((HD, rows), f32),
            ],
        ),
        out_shape=out_shape
        + out_shape
        + [jax.ShapeDtypeStruct(part.shape, bf16) for part in kv_pieces],
        compiler_params=pltpu.CompilerParams(vmem_limit_bytes=VMEM),
        cost_estimate=pl.CostEstimate(
            flops=48 * HD * pairs, bytes_accessed=16 * qg.size, transcendentals=pairs
        ),
        name="attention",
    )(info, bounds, qg, qg, *kv_pieces, pos, low)
    return results[:steps], results[steps : 2 * steps], results[2 * steps :]


def body(
    record_lengths,
    query_heads,
    key_heads,
    value_heads,
    out_grad,
    gate_input,
    key_input,
    value_input,
    hyena_grad,
    short_filter,
    long_filter,
):
    ctx = lax.axis_size("ctx")
    tp = lax.axis_size("tp")
    own_ctx = lax.axis_index("ctx")
    piece = query_heads.shape[0]
    tokens = piece * tp
    window = tokens * ctx
    most = window // 2 + 192
    split = 2 if (KVH // tp) % 2 == 0 else 1
    slots = tp * split
    kv_local = KVH // slots
    unit = tokens * split
    lanes = PLANE // split
    plane = unit * lanes
    reach = (most - 1) // plane
    tail = -(-(most - 1 - reach * plane) // 192) * 192
    core = own_ctx % split
    lane = own_ctx // split % lanes
    level = own_ctx // PLANE
    f32 = jnp.float32
    bf16 = jnp.bfloat16

    members = [
        [t * ctx + n * split + c for t in range(tp) for c in range(split)]
        for n in range(ctx // split)
    ]

    def share(laid):
        return lax.all_to_all(
            laid, ("tp", "ctx"), 0, 0, axis_index_groups=members, tiled=True
        )

    permute = functools.partial(lax.ppermute, axis_name="ctx")

    def across(values, distance):
        return permute(values, perm=[(i, i ^ (distance * split)) for i in range(ctx)])

    def up(values):
        return permute(values, perm=[(i, i + PLANE) for i in range(ctx - PLANE)])

    def down(values, flip=0):
        return permute(values, perm=[(i + PLANE, i ^ flip) for i in range(ctx - PLANE)])

    def partner(values):
        return permute(values, perm=[(i, i ^ 1) for i in range(ctx)])

    far = (reach + 1) * PLANE - (lanes - 1) * split
    far_pairs = [
        (i, i + far) for i in range(ctx - far) if i // split % lanes == lanes - 1
    ]

    kv = share(pack([key_heads, value_heads], slots, True))
    qg = share(pack([query_heads, out_grad], slots, False))
    own_kv = kv.reshape(tp, split, 2, piece, kv_local * HD)
    own_kv = own_kv.transpose(2, 1, 0, 3, 4).reshape(2, unit, kv_local * HD)

    columns = [own_kv]
    for _ in range(reach):
        columns.append(up(columns[-1]))
    tail_kv = permute(own_kv[:, unit - tail :], perm=far_pairs)
    pieces = [tail_kv]
    places = [jnp.int32(0)]
    for back in range(reach + 1):
        for distance in range(lanes):
            held = columns[back]
            pieces.append(held if distance == 0 else across(held, distance))
            places.append(tail + (reach - back) * plane + (lane ^ distance) * unit)
    origin = (level - reach) * plane - tail
    info = jnp.stack([origin, core] + places).astype(jnp.int32)

    ends = jnp.cumsum(record_lengths)
    half = (core + 1 + np.arange(split, dtype=np.int32)) % split
    start = own_ctx // split * unit + half * tokens
    pos = start[:, None] + np.arange(tokens, dtype=np.int32)
    low = jnp.max(jnp.where(ends <= pos[..., None], ends, 0), axis=-1)
    bounds = jnp.stack([pos[:, 0], low[:, 0], low[:, -1], half], axis=1).astype(jnp.int32)
    group = QH // KVH
    pos_rows = jnp.tile(pos, (1, group)).reshape(split, 1, -1)
    low_rows = jnp.tile(low, (1, group)).reshape(split, 1, -1)

    streams = (gate_input, key_input, value_input, hyena_grad)
    heads = jnp.concatenate([s[:HALO] for s in streams], axis=0)
    tails = jnp.concatenate([s[tokens - HALO :] for s in streams], axis=0)
    before = permute(tails, perm=[(i, i + 1) for i in range(ctx - 1)])
    after = permute(heads, perm=[(i + 1, i) for i in range(ctx - 1)])
    hyena_outs = hyena(
        streams,
        before,
        after,
        short_filter,
        long_filter,
    )
    hyena_outs, info = lax.optimization_barrier((hyena_outs, info))

    shape = (1, unit, -1) if split == 1 else (tp, split * piece, -1)
    outs, dqs, terms = attention(
        qg.reshape(shape), pieces, info, bounds, pos_rows, low_rows, split * qg.shape[2] // 2, most
    )

    def settle(parts):
        if split == 1:
            return parts[-1]
        width = parts[0].shape[1]
        return lax.dynamic_update_slice(
            parts[-1], partner(parts[0]), (jnp.int32(0), (1 - core) * width)
        )

    def plane_sum(back):
        at = 1 + back * lanes
        total = terms[at].astype(f32)
        for distance in range(1, lanes):
            total = total + across(terms[at + distance], distance).astype(f32)
        return total

    def halves(values):
        if split == 1:
            return values, None
        low_half, high_half = values[:, :tokens], values[:, tokens:]
        mine = jnp.where(core == 0, low_half, high_half)
        return mine, jnp.where(core == 0, high_half, low_half)

    running = plane_sum(reach).astype(bf16)
    for back in range(reach - 1, 0, -1):
        running = (plane_sum(back) + down(running).astype(f32)).astype(bf16)
    tail_term = permute(terms[0], perm=[(j, i) for i, j in far_pairs]).astype(f32)
    own_sum = plane_sum(0)
    own_sum = jnp.concatenate(
        [own_sum[:, : unit - tail], own_sum[:, unit - tail :] + tail_term], axis=1
    )
    mine, others = halves(own_sum)
    coming, crossing = halves(running)
    mine = mine + down(coming).astype(f32)
    if split == 2:
        theirs = partner(others.astype(bf16)).astype(f32) + down(crossing, 1).astype(f32)
        mine = jnp.where(
            core == 0,
            jnp.concatenate([mine, theirs], axis=2),
            jnp.concatenate([theirs, mine], axis=2),
        )
    grad_key, grad_value = mine[0].astype(bf16), mine[1].astype(bf16)
    return (settle(outs), settle(dqs), grad_key, grad_value) + tuple(hyena_outs)


def solution(mesh):
    rows = P(("ctx", "tp"), None)
    both = P("ctx", "tp")
    return jax.shard_map(
        body,
        mesh=mesh,
        in_specs=(P(), rows, rows, rows, rows, both, both, both, both)
        + (P(None, None, "tp"), P(None, "tp")),
        out_specs=(both,) * 8,
        check_vma=False,
    )
```

```python
import functools

import jax
import jax.numpy as jnp
import numpy as np
from jax import lax
from jax.experimental import pallas as pl
from jax.experimental.pallas import tpu as pltpu
from jax.sharding import PartitionSpec as P

HD = 128
QH = 64
KVH = 8
GROUP = 16
TAPS = 7
SHORT = 3
HALO = 8
PLANE = 4
KB = 256
NEG = -1e30
SCALE = HD ** (-0.5)
TO_EXP2 = SCALE * 1.4426950408889634
VMEM = 48 * 1024 * 1024


def hyena_kernel(
    part,
    gate_ref,
    key_ref,
    value_ref,
    grad_ref,
    before_ref,
    after_ref,
    short_ref,
    long_ref,
    *refs,
):
    out_ref, dgate_ref, dkey_ref, dvalue_ref, taps = refs[-5:]
    tokens, width = gate_ref.shape
    own = pl.program_id(0)

    @pl.when(own == 0)
    def _():
        shape = (long_ref.shape[1], taps.shape[1])
        group = lax.broadcasted_iota(jnp.int32, shape, 0)
        channel = part * taps.shape[1] + lax.broadcasted_iota(jnp.int32, shape, 1)
        taps[...] = jnp.dot(
            long_ref[...],
            (group == channel // GROUP).astype(jnp.float32),
            precision=lax.Precision.HIGHEST,
            preferred_element_type=jnp.float32,
        )

    rows = tokens + 2 * HALO

    def chunk(index, carry):
        lanes = pl.ds(pl.multiple_of(index * HD, HD), HD)
        before = before_ref[:, lanes].astype(jnp.float32)
        after = after_ref[:, lanes].astype(jnp.float32)

        def padded(ref, which):
            part = slice(which * HALO, (which + 1) * HALO)
            return jnp.concatenate(
                [before[part], ref[:, lanes].astype(jnp.float32), after[part]], axis=0
            )

        def earlier(values, amount):
            return pltpu.roll(values, amount, 0) if amount else values

        def later(values, amount):
            return pltpu.roll(values, rows - amount, 0) if amount else values

        long = taps[:, pl.ds(pl.multiple_of(own * width + index * HD, HD), HD)]

        def short(which, tap):
            return short_ref[which, tap : tap + 1, lanes]

        def featurize(values, which):
            result = short(which, 0) * values
            for tap in range(1, SHORT):
                result = result + short(which, tap) * earlier(values, tap)
            return result

        def unfeaturize(grads, which):
            result = short(which, 0) * grads
            for tap in range(1, SHORT):
                result = result + short(which, tap) * later(grads, tap)
            return result[HALO : HALO + tokens].astype(jnp.bfloat16)

        key_f = featurize(padded(key_ref, 1), 1)
        value_f = featurize(padded(value_ref, 2), 2)
        mixed = key_f * value_f
        conv = long[0:1] * mixed
        for tap in range(1, TAPS):
            conv = conv + long[tap : tap + 1] * earlier(mixed, tap)
        gate_f = featurize(padded(gate_ref, 0), 0)
        out_ref[:, lanes] = (gate_f * conv)[HALO : HALO + tokens].astype(jnp.bfloat16)
        grad = padded(grad_ref, 3)
        dgate_ref[:, lanes] = unfeaturize(grad * conv, 0)
        dconv = grad * gate_f
        dmixed = long[0:1] * dconv
        for tap in range(1, TAPS):
            dmixed = dmixed + long[tap : tap + 1] * later(dconv, tap)
        dkey_ref[:, lanes] = unfeaturize(dmixed * value_f, 1)
        dvalue_ref[:, lanes] = unfeaturize(dmixed * key_f, 2)
        return carry

    lax.fori_loop(0, width // HD, chunk, 0)


def hyena(streams, before, after, short_filter, long_filter, part, parts, filled=()):
    tokens, channels = streams[0].shape
    own = channels // parts
    width = min(512, own)
    steps = own // width
    block = pl.BlockSpec((tokens, width), lambda i: (0, part * steps + i))
    edge = pl.BlockSpec((4 * HALO, width), lambda i: (0, part * steps + i))
    return pl.pallas_call(
        functools.partial(hyena_kernel, part),
        grid=(steps,),
        in_specs=[block] * 4
        + [edge, edge]
        + [
            pl.BlockSpec((3, SHORT, width), lambda i: (0, 0, part * steps + i)),
            pl.BlockSpec(long_filter.shape, lambda i: (0, 0)),
        ]
        + [pl.BlockSpec(memory_space=pl.ANY)] * len(filled),
        out_specs=[block] * 4,
        out_shape=[jax.ShapeDtypeStruct((tokens, channels), jnp.bfloat16)] * 4,
        scratch_shapes=[pltpu.VMEM((TAPS, own), jnp.float32)],
        input_output_aliases={8 + i: i for i in range(len(filled))},
        compiler_params=pltpu.CompilerParams(vmem_limit_bytes=VMEM),
        cost_estimate=pl.CostEstimate(
            flops=14000 * tokens * own, bytes_accessed=16 * tokens * own, transcendentals=0
        ),
        name="hyena",
    )(*streams, before, after, short_filter, long_filter, *filled)


def pack_kernel(stacked, *refs):
    sources, target = refs[:-1], refs[-1]
    for index, ref in enumerate(sources):
        if stacked:
            target[0, index] = ref[...]
        else:
            width = ref.shape[1]
            target[0, :, index * width : (index + 1) * width] = ref[...]


def pack(parts, slots, stacked, cut=0, cuts=1):
    rows, columns = parts[0].shape
    width = columns // slots // cuts
    count = len(parts)
    if stacked:
        shape = (slots, count, rows, width)
        target = pl.BlockSpec((1, count, rows, width), lambda i: (i, 0, 0, 0))
    else:
        shape = (slots, rows, count * width)
        target = pl.BlockSpec((1, rows, count * width), lambda i: (i, 0, 0))
    return pl.pallas_call(
        functools.partial(pack_kernel, stacked),
        grid=(slots,),
        in_specs=[pl.BlockSpec((rows, width), lambda i: (0, i * cuts + cut))] * count,
        out_specs=target,
        out_shape=jax.ShapeDtypeStruct(shape, parts[0].dtype),
        name="pack",
    )(*parts)


def attention_kernel(pieces, split, *refs):
    (info_ref, bounds_ref, q_ref, g_ref), refs = refs[:4], refs[4:]
    piece_refs, refs = refs[:pieces], refs[pieces:]
    (pos_ref, low_ref), refs = refs[:2], refs[2:]
    out_refs, refs = refs[:split], refs[split:]
    term_refs, refs = refs[:pieces], refs[pieces:]
    kv, k_t, v_t, dk_sum, dv_sum, scores, weights, dscores = refs[:8]
    q_rows, q_t, g_rows, g_t, peak8, total8, out_t, dq_t = refs[8:]
    step = pl.program_id(0)
    steps = pl.num_programs(0)
    blocks = k_t.shape[0]
    heads = q_ref.shape[2] // HD
    size = q_ref.shape[0] * q_ref.shape[1]
    rows = size * heads
    f32 = jnp.float32
    bf16 = jnp.bfloat16
    chunks = [slice(start, min(start + 256, rows)) for start in range(0, rows, 256)]
    origin = info_ref[0]

    def rows_of(b):
        return pl.ds(pl.multiple_of(b * KB, KB), KB)

    def piece_rows(index):
        count = piece_refs[index].shape[1]
        return pl.ds(pl.multiple_of(info_ref[2 + index], 64), count)

    @pl.when(step == 0)
    def _():
        filled = sum(ref.shape[1] for ref in piece_refs)
        if filled < kv.shape[0]:
            kv[filled:] = jnp.zeros((kv.shape[0] - filled, 2 * HD), bf16)
        for index in range(pieces):
            kv[piece_rows(index), :HD] = piece_refs[index][0]
            kv[piece_rows(index), HD:] = piece_refs[index][1]
        dk_sum[...] = jnp.zeros(dk_sum.shape, f32)
        dv_sum[...] = jnp.zeros(dv_sum.shape, f32)

        def prepare(b, carry):
            k_t[b] = kv[rows_of(b), :HD].T
            v_t[b] = kv[rows_of(b), HD:].T
            return carry

        lax.fori_loop(0, blocks, prepare, 0)

    for h in range(heads):
        part = slice(h * size, (h + 1) * size)
        q_rows[part] = q_ref[:, :, h * HD : (h + 1) * HD].reshape(size, HD)
        g_rows[part] = g_ref[:, :, h * HD : (h + 1) * HD].reshape(size, HD)
    q_t[...] = q_rows[...].T
    g_t[...] = g_rows[...].T
    peak8[...] = jnp.full((8, rows), NEG, f32)
    total8[...] = jnp.zeros((8, rows), f32)
    out_t[...] = jnp.zeros((HD, rows), f32)
    dq_t[...] = jnp.zeros((HD, rows), f32)

    q_first = bounds_ref[step, 0]
    low_first = bounds_ref[step, 1]
    low_last = bounds_ref[step, 2]
    first = (low_first - origin) // KB
    last = (q_first + (size - 1) - origin) // KB + 1

    def fold(values, combine):
        result = values[0:8]
        for start in range(8, values.shape[0], 8):
            result = combine(result, values[start : start + 8])
        return result

    def score_pass(b, carry):
        base = origin + b * KB
        whole = (base + (KB - 1) <= q_first) & (base >= low_last)

        @pl.when(whole)
        def _():
            for part in chunks:
                s = jnp.dot(kv[rows_of(b), :HD], q_t[:, part], preferred_element_type=f32)
                scores[b - first, :, part] = s
                peak8[:, part] = jnp.maximum(peak8[:, part], fold(s, jnp.maximum))

        @pl.when(jnp.logical_not(whole))
        def _():
            for part in chunks:
                s = jnp.dot(kv[rows_of(b), :HD], q_t[:, part], preferred_element_type=f32)
                key_pos = base + lax.broadcasted_iota(jnp.int32, s.shape, 0)
                allowed = (key_pos <= pos_ref[0, :, part]) & (key_pos >= low_ref[0, :, part])
                s = jnp.where(allowed, s, NEG)
                scores[b - first, :, part] = s
                peak8[:, part] = jnp.maximum(peak8[:, part], fold(s, jnp.maximum))

        return carry

    lax.fori_loop(first, last, score_pass, 0)
    peak = jnp.max(peak8[...], axis=0, keepdims=True) * TO_EXP2

    def weight_pass(b, carry):
        for part in chunks:
            w = jnp.exp2(scores[b - first, :, part] * TO_EXP2 - peak[:, part])
            total8[:, part] += fold(w, jnp.add)
            w_b = w.astype(bf16)
            weights[b - first, :, part] = w_b
            out_t[:, part] += jnp.dot(v_t[b], w_b, preferred_element_type=f32)
        return carry

    lax.fori_loop(first, last, weight_pass, 0)
    inverse = 1.0 / jnp.sum(total8[...], axis=0, keepdims=True)
    out_b = (out_t[...] * inverse).astype(bf16)
    g_wide = g_t[...].astype(f32)
    delta = jnp.sum(g_wide * out_b.astype(f32), axis=0, keepdims=True) * inverse
    g_scaled = (g_wide * inverse).astype(bf16)
    g_t[...] = g_scaled
    g_rows[...] = g_scaled.T

    groups, run = q_ref.shape[:2]
    inside = split // bounds_ref.shape[0]
    single = run // inside

    def give(wide, first):
        for cell in range(inside):
            owner = step * inside + cell
            for distance in range(split):

                @pl.when((owner ^ info_ref[1]) == distance)
                def _():
                    for h in range(heads):
                        for a in range(groups):
                            start = h * size + a * run + cell * single
                            out_refs[distance][
                                a * single : (a + 1) * single,
                                first + h * HD : first + (h + 1) * HD,
                            ] = wide[start : start + single]

    give(out_b.T, 0)

    def grad_pass(b, carry):
        for part in chunks:
            dp = jnp.dot(kv[rows_of(b), HD:], g_t[:, part], preferred_element_type=f32)
            w = weights[b - first, :, part].astype(f32)
            dscores[:, part] = (w * (dp - delta[:, part])).astype(bf16)
        dv_sum[rows_of(b)] += jnp.dot(weights[b - first], g_rows[...], preferred_element_type=f32)
        dk_sum[rows_of(b)] += jnp.dot(dscores[...], q_rows[...], preferred_element_type=f32)
        dq_t[...] += jnp.dot(k_t[b], dscores[...], preferred_element_type=f32)
        return carry

    lax.fori_loop(first, last, grad_pass, 0)
    give((dq_t[...] * SCALE).astype(bf16).T, heads * HD)

    @pl.when(step == steps - 1)
    def _():
        for index in range(pieces):
            term_refs[index][0] = (dk_sum[piece_rows(index)] * SCALE).astype(bf16)
            term_refs[index][1] = dv_sum[piece_rows(index)].astype(bf16)


def attention(qg, kv_pieces, info, bounds, pos, low, split, most):
    groups, run, columns = qg.shape
    columns = columns // 2
    steps, _, rows = pos.shape
    heads = columns // HD
    size = rows // heads
    pieces = len(kv_pieces)
    keys = -(-sum(part.shape[1] for part in kv_pieces) // KB) * KB
    blocks = keys // KB
    live = min(blocks, (most + size - 3) // KB + 2)
    bf16 = jnp.bfloat16
    f32 = jnp.float32

    def taken(which):
        return pl.BlockSpec((groups, run // steps, columns), lambda i, *_: (0, i, which))

    def still(shape):
        return pl.BlockSpec(shape, lambda i, *_: (0,) * len(shape))

    kv_specs = [still(part.shape) for part in kv_pieces]
    lanes = pl.BlockSpec((1, 1, rows), lambda i, *_: (i, 0, 0))
    given = (size * steps // split, 2 * columns)
    pairs = size * steps * heads * keys
    results = pl.pallas_call(
        functools.partial(attention_kernel, pieces, split),
        grid_spec=pltpu.PrefetchScalarGridSpec(
            num_scalar_prefetch=2,
            grid=(steps,),
            in_specs=[taken(0), taken(1)] + kv_specs + [lanes, lanes],
            out_specs=[still(given)] * split + kv_specs,
            scratch_shapes=[
                pltpu.VMEM((keys, 2 * HD), bf16),
                pltpu.VMEM((blocks, HD, KB), bf16),
                pltpu.VMEM((blocks, HD, KB), bf16),
                pltpu.VMEM((keys, HD), f32),
                pltpu.VMEM((keys, HD), f32),
                pltpu.VMEM((live, KB, rows), f32),
                pltpu.VMEM((live, KB, rows), bf16),
                pltpu.VMEM((KB, rows), bf16),
                pltpu.VMEM((rows, HD), bf16),
                pltpu.VMEM((HD, rows), bf16),
                pltpu.VMEM((rows, HD), bf16),
                pltpu.VMEM((HD, rows), bf16),
                pltpu.VMEM((8, rows), f32),
                pltpu.VMEM((8, rows), f32),
                pltpu.VMEM((HD, rows), f32),
                pltpu.VMEM((HD, rows), f32),
            ],
        ),
        out_shape=[jax.ShapeDtypeStruct(given, bf16)] * split
        + [jax.ShapeDtypeStruct(part.shape, bf16) for part in kv_pieces],
        compiler_params=pltpu.CompilerParams(vmem_limit_bytes=VMEM),
        cost_estimate=pl.CostEstimate(
            flops=48 * HD * pairs, bytes_accessed=16 * qg.size, transcendentals=pairs
        ),
        name="attention",
    )(info, bounds, qg, qg, *kv_pieces, pos, low)
    return results[:split], results[split:]


def settle_kernel(split, info_ref, *refs):
    piece_refs, (out_ref, dq_ref) = refs[:split], refs[-2:]
    width = out_ref.shape[1]
    for distance in range(split):

        @pl.when(pl.program_id(0) == distance)
        def _():
            out_ref[...] = piece_refs[distance][:, :width]
            dq_ref[...] = piece_refs[distance][:, width:]


def settle(info, parts, cut, cuts, filled=()):
    split = len(parts)
    rows, width = parts[0].shape
    width = width // 2
    block = pl.BlockSpec(
        (rows, width), lambda i, info_ref: (0, jnp.bitwise_xor(info_ref[1], i) * cuts + cut)
    )
    whole = pl.BlockSpec((rows, 2 * width), lambda i, info_ref: (0, 0))
    return pl.pallas_call(
        functools.partial(settle_kernel, split),
        grid_spec=pltpu.PrefetchScalarGridSpec(
            num_scalar_prefetch=1,
            grid=(split,),
            in_specs=[whole] * split + [pl.BlockSpec(memory_space=pl.ANY)] * len(filled),
            out_specs=[block] * 2,
        ),
        out_shape=[jax.ShapeDtypeStruct((rows, width * split * cuts), parts[0].dtype)] * 2,
        input_output_aliases={1 + split + i: i for i in range(len(filled))},
        name="settle",
    )(info, *parts, *filled)


def body(
    record_lengths,
    query_heads,
    key_heads,
    value_heads,
    out_grad,
    gate_input,
    key_input,
    value_input,
    hyena_grad,
    short_filter,
    long_filter,
):
    ctx = lax.axis_size("ctx")
    tp = lax.axis_size("tp")
    own_ctx = lax.axis_index("ctx")
    piece = query_heads.shape[0]
    tokens = piece * tp
    window = tokens * ctx
    most = window // 2 + 192
    split = PLANE if (KVH // tp) % PLANE == 0 else 1
    slots = tp * split
    kv_local = KVH // slots
    assert kv_local == 1 and tokens % 192 == 0
    unit = tokens * split
    lanes = PLANE // split
    plane = unit * lanes
    reach = (most - 1) // plane
    tail = -(-(most - 1 - reach * plane) // 192) * 192
    core = own_ctx % split
    lane = own_ctx // split % lanes
    level = own_ctx // PLANE
    f32 = jnp.float32
    bf16 = jnp.bfloat16

    members = [
        [t * ctx + n * split + c for t in range(tp) for c in range(split)]
        for n in range(ctx // split)
    ]

    def share(laid):
        return lax.all_to_all(
            laid, ("tp", "ctx"), 0, 0, axis_index_groups=members, tiled=True
        )

    permute = functools.partial(lax.ppermute, axis_name="ctx")

    def across(values, distance):
        return permute(values, perm=[(i, i ^ (distance * split)) for i in range(ctx)])

    def up(values):
        return permute(values, perm=[(i, i + PLANE) for i in range(ctx - PLANE)])

    def down(values):
        return permute(values, perm=[(i + PLANE, i) for i in range(ctx - PLANE)])

    def swap(values, distance):
        return permute(values, perm=[(i, i ^ distance) for i in range(ctx)])

    far = (reach + 1) * PLANE - (lanes - 1) * split
    far_pairs = [
        (i, i + far) for i in range(ctx - far) if i // split % lanes == lanes - 1
    ]

    streams = (gate_input, key_input, value_input, hyena_grad)
    heads = jnp.concatenate([s[:HALO] for s in streams], axis=0)
    tails = jnp.concatenate([s[tokens - HALO :] for s in streams], axis=0)
    before = permute(tails, perm=[(i, i + 1) for i in range(ctx - 1)])
    after = permute(heads, perm=[(i + 1, i) for i in range(ctx - 1)])

    kv = share(pack([key_heads, value_heads], slots, True))
    cuts = 2
    qgs = [share(pack([query_heads, out_grad], slots, False, cut, cuts)) for cut in range(cuts)]
    own_kv = kv.reshape(tp, split, 2, piece, kv_local * HD)
    own_kv = own_kv.transpose(2, 1, 0, 3, 4).reshape(2, unit, kv_local * HD)

    filters = (short_filter, long_filter)
    columns = [own_kv]
    hyena_outs = ()
    for hop in range(reach):
        coming = up(columns[-1])
        if hop < 2:
            before, columns[-1] = lax.optimization_barrier((before, columns[-1]))
            hyena_outs = hyena(streams, before, after, *filters, hop, 2, hyena_outs)
            coming, first_out = lax.optimization_barrier((coming, hyena_outs[0]))
            hyena_outs = (first_out,) + tuple(hyena_outs[1:])
        columns.append(coming)
    tail_kv = permute(own_kv[:, unit - tail :], perm=far_pairs)
    pieces = [tail_kv]
    places = [jnp.int32(0)]
    for back in range(reach + 1):
        for distance in range(lanes):
            held = columns[back]
            pieces.append(held if distance == 0 else across(held, distance))
            places.append(tail + (reach - back) * plane + (lane ^ distance) * unit)
    origin = (level - reach) * plane - tail
    info = jnp.stack([origin, core] + places).astype(jnp.int32)

    ends = jnp.cumsum(record_lengths)
    size = min(384, unit)
    steps = unit // size
    inside = split // steps if split > 1 else 1
    order = np.arange(unit, dtype=np.int32).reshape(steps, inside, tp, -1)
    order = order.transpose(0, 2, 1, 3).reshape(steps, size)
    start = own_ctx // split * unit
    pos = start + order
    low = jnp.max(jnp.where(ends <= pos[..., None], ends, 0), axis=-1)
    bounds = jnp.stack([pos[:, 0], low[:, 0], low[:, -1]], axis=1).astype(jnp.int32)
    group = QH // KVH // cuts
    pos_rows = jnp.tile(pos, (1, group)).reshape(steps, 1, -1)
    low_rows = jnp.tile(low, (1, group)).reshape(steps, 1, -1)

    shape = (1, unit, -1) if split == 1 else (tp, split * piece, -1)
    results = ()
    terms = []
    for cut in range(cuts):
        outs, sums = attention(
            qgs[cut].reshape(shape), pieces, info, bounds, pos_rows, low_rows, split, most
        )
        terms.append(sums)
        outs = [outs[0]] + [swap(outs[distance], distance) for distance in range(1, split)]
        results = settle(info, outs, cut, cuts, results)
    attn_out, grad_query = results

    def term_sum(index):
        return sum(part[index].astype(f32) for part in terms)

    def plane_sum(back):
        at = 1 + back * lanes
        total = term_sum(at)
        for distance in range(1, lanes):
            total = total + across(term_sum(at + distance).astype(bf16), distance).astype(f32)
        return total

    tail_term = permute(term_sum(0).astype(bf16), perm=[(j, i) for i, j in far_pairs])
    running = plane_sum(reach).astype(bf16)
    for back in range(reach - 1, -1, -1):
        running = plane_sum(back) + down(running).astype(f32)
        if back:
            running = running.astype(bf16)
    owned = jnp.concatenate(
        [running[:, : unit - tail], running[:, unit - tail :] + tail_term.astype(f32)], axis=1
    ).astype(bf16)

    parts = []
    for distance in range(split):
        held = lax.dynamic_slice_in_dim(owned, (core ^ distance) * tokens, tokens, 1)
        parts.append(swap(held, distance) if distance else held)
    bit = 1
    while bit < split:
        parts = [
            jnp.where(core & bit != 0, parts[index ^ bit], parts[index]) for index in range(split)
        ]
        bit = 2 * bit
    grads = jnp.concatenate(parts, axis=2)
    return (attn_out, grad_query, grads[0], grads[1]) + tuple(hyena_outs)


def solution(mesh):
    rows = P(("ctx", "tp"), None)
    both = P("ctx", "tp")
    return jax.shard_map(
        body,
        mesh=mesh,
        in_specs=(P(), rows, rows, rows, rows, both, both, both, both)
        + (P(None, None, "tp"), P(None, "tp")),
        out_specs=(both,) * 8,
        check_vma=False,
    )
```

```python
import functools

import jax
import jax.numpy as jnp
import numpy as np
from jax import lax
from jax.experimental import pallas as pl
from jax.experimental.pallas import tpu as pltpu
from jax.sharding import PartitionSpec as P

HD = 128
QH = 64
KVH = 8
GROUP = 16
TAPS = 7
SHORT = 3
HALO = 8
PLANE = 4
KB = 256
NEG = -1e30
SCALE = HD ** (-0.5)
TO_EXP2 = SCALE * 1.4426950408889634
VMEM = 48 * 1024 * 1024


def hyena_kernel(
    part,
    gate_ref,
    key_ref,
    value_ref,
    grad_ref,
    before_ref,
    after_ref,
    short_ref,
    long_ref,
    *refs,
):
    out_ref, dgate_ref, dkey_ref, dvalue_ref, taps = refs[-5:]
    tokens, width = gate_ref.shape
    own = pl.program_id(0)

    @pl.when(own == 0)
    def _():
        shape = (long_ref.shape[1], taps.shape[1])
        group = lax.broadcasted_iota(jnp.int32, shape, 0)
        channel = part * taps.shape[1] + lax.broadcasted_iota(jnp.int32, shape, 1)
        taps[...] = jnp.dot(
            long_ref[...],
            (group == channel // GROUP).astype(jnp.float32),
            precision=lax.Precision.HIGHEST,
            preferred_element_type=jnp.float32,
        )

    rows = tokens + 2 * HALO

    def chunk(index, carry):
        lanes = pl.ds(pl.multiple_of(index * HD, HD), HD)
        before = before_ref[:, lanes].astype(jnp.float32)
        after = after_ref[:, lanes].astype(jnp.float32)

        def padded(ref, which):
            part = slice(which * HALO, (which + 1) * HALO)
            return jnp.concatenate(
                [before[part], ref[:, lanes].astype(jnp.float32), after[part]], axis=0
            )

        def earlier(values, amount):
            return pltpu.roll(values, amount, 0) if amount else values

        def later(values, amount):
            return pltpu.roll(values, rows - amount, 0) if amount else values

        long = taps[:, pl.ds(pl.multiple_of(own * width + index * HD, HD), HD)]

        def short(which, tap):
            return short_ref[which, tap : tap + 1, lanes]

        def featurize(values, which):
            result = short(which, 0) * values
            for tap in range(1, SHORT):
                result = result + short(which, tap) * earlier(values, tap)
            return result

        def unfeaturize(grads, which):
            result = short(which, 0) * grads
            for tap in range(1, SHORT):
                result = result + short(which, tap) * later(grads, tap)
            return result[HALO : HALO + tokens].astype(jnp.bfloat16)

        key_f = featurize(padded(key_ref, 1), 1)
        value_f = featurize(padded(value_ref, 2), 2)
        mixed = key_f * value_f
        conv = long[0:1] * mixed
        for tap in range(1, TAPS):
            conv = conv + long[tap : tap + 1] * earlier(mixed, tap)
        gate_f = featurize(padded(gate_ref, 0), 0)
        out_ref[:, lanes] = (gate_f * conv)[HALO : HALO + tokens].astype(jnp.bfloat16)
        grad = padded(grad_ref, 3)
        dgate_ref[:, lanes] = unfeaturize(grad * conv, 0)
        dconv = grad * gate_f
        dmixed = long[0:1] * dconv
        for tap in range(1, TAPS):
            dmixed = dmixed + long[tap : tap + 1] * later(dconv, tap)
        dkey_ref[:, lanes] = unfeaturize(dmixed * value_f, 1)
        dvalue_ref[:, lanes] = unfeaturize(dmixed * key_f, 2)
        return carry

    lax.fori_loop(0, width // HD, chunk, 0)


def hyena(streams, before, after, short_filter, long_filter, part, parts, filled=()):
    tokens, channels = streams[0].shape
    own = channels // parts
    width = min(512, own)
    steps = own // width
    block = pl.BlockSpec((tokens, width), lambda i: (0, part * steps + i))
    edge = pl.BlockSpec((4 * HALO, width), lambda i: (0, part * steps + i))
    return pl.pallas_call(
        functools.partial(hyena_kernel, part),
        grid=(steps,),
        in_specs=[block] * 4
        + [edge, edge]
        + [
            pl.BlockSpec((3, SHORT, width), lambda i: (0, 0, part * steps + i)),
            pl.BlockSpec(long_filter.shape, lambda i: (0, 0)),
        ]
        + [pl.BlockSpec(memory_space=pl.ANY)] * len(filled),
        out_specs=[block] * 4,
        out_shape=[jax.ShapeDtypeStruct((tokens, channels), jnp.bfloat16)] * 4,
        scratch_shapes=[pltpu.VMEM((TAPS, own), jnp.float32)],
        input_output_aliases={8 + i: i for i in range(len(filled))},
        compiler_params=pltpu.CompilerParams(vmem_limit_bytes=VMEM),
        cost_estimate=pl.CostEstimate(
            flops=14000 * tokens * own, bytes_accessed=16 * tokens * own, transcendentals=0
        ),
        name="hyena",
    )(*streams, before, after, short_filter, long_filter, *filled)


def copy_all(copies, sems):
    started = [
        pltpu.make_async_copy(source, target, sems.at[index])
        for index, (source, target) in enumerate(copies)
    ]
    for copy in started:
        copy.start()
    for copy in started:
        copy.wait()


def own_slot(split):
    return lax.axis_index("tp") * split + lax.axis_index("ctx") % split


def pack_kv_kernel(k_ref, v_ref, out_ref, sems):
    width = out_ref.shape[3]
    copies = []
    for slot in range(out_ref.shape[0]):
        part = slice(slot * width, (slot + 1) * width)
        copies.append((k_ref.at[:, part], out_ref.at[slot, 0]))
        copies.append((v_ref.at[:, part], out_ref.at[slot, 1]))
    copy_all(copies, sems)


def pack_kv(keys, values, slots):
    rows, columns = keys.shape
    anywhere = pl.BlockSpec(memory_space=pl.ANY)
    return pl.pallas_call(
        pack_kv_kernel,
        in_specs=[anywhere] * 2,
        out_specs=anywhere,
        out_shape=jax.ShapeDtypeStruct((slots, 2, rows, columns // slots), keys.dtype),
        scratch_shapes=[pltpu.SemaphoreType.DMA((2 * slots,))],
        name="pack_kv",
    )(keys, values)


def pack_rows_kernel(split, q_ref, g_ref, *refs):
    outs, sems = refs[:-1], refs[-1]
    width = outs[0].shape[1] // 2
    slot = own_slot(split)
    copies = []
    for distance, out in enumerate(outs):
        start = pl.multiple_of((slot ^ distance) * width, HD)
        copies.append((q_ref.at[:, pl.ds(start, width)], out.at[:, :width]))
        copies.append((g_ref.at[:, pl.ds(start, width)], out.at[:, width:]))
    copy_all(copies, sems)


def pack_rows(queries, grads, slots, split):
    rows, columns = queries.shape
    anywhere = pl.BlockSpec(memory_space=pl.ANY)
    shape = jax.ShapeDtypeStruct((rows, 2 * columns // slots), queries.dtype)
    return pl.pallas_call(
        functools.partial(pack_rows_kernel, split),
        in_specs=[anywhere] * 2,
        out_specs=[anywhere] * slots,
        out_shape=[shape] * slots,
        scratch_shapes=[pltpu.SemaphoreType.DMA((2 * slots,))],
        name="pack_rows",
    )(queries, grads)


def attention_kernel(pieces, split, groups, reach, tail, *refs):
    (info_ref, lengths_ref), refs = refs[:2], refs[2:]
    qg_refs, refs = refs[: split * groups], refs[split * groups :]
    piece_refs, refs = refs[:pieces], refs[pieces:]
    out_refs, refs = refs[:split], refs[split:]
    term_refs, refs = refs[:pieces], refs[pieces:]
    kv, k_t, v_t, dk_sum, dv_sum, scores, weights, dscores = refs[:8]
    q_rows, q_t, g_rows, g_t, peak8, total8, out_t, dq_t = refs[8:]
    step = pl.program_id(0)
    blocks = k_t.shape[0]
    run = qg_refs[0].shape[0]
    columns = qg_refs[0].shape[1] // 2
    heads = columns // HD
    size = groups * run
    rows = size * heads
    f32 = jnp.float32
    bf16 = jnp.bfloat16
    chunks = [slice(start, min(start + 256, rows)) for start in range(0, rows, 256)]
    ctx = lax.axis_index("ctx")
    own = lax.axis_index("tp") if groups > 1 else 0
    origin = info_ref[0]

    def record_start(position):
        ends = 0
        start = position * 0
        for record in range(lengths_ref.shape[0]):
            ends = ends + lengths_ref[record]
            start = jnp.where(position >= ends, ends, start)
        return start

    def rows_of(b):
        return pl.ds(pl.multiple_of(b * KB, KB), KB)

    def piece_rows(index):
        count = piece_refs[index].shape[1]
        return pl.ds(pl.multiple_of(info_ref[1 + index], 64), count)

    @pl.when(step == 0)
    def _():
        filled = sum(ref.shape[1] for ref in piece_refs)
        if filled < kv.shape[0]:
            kv[filled:] = jnp.zeros((kv.shape[0] - filled, 2 * HD), bf16)
        for index in range(pieces):
            kv[piece_rows(index), :HD] = piece_refs[index][0]
            kv[piece_rows(index), HD:] = piece_refs[index][1]
        dk_sum[...] = jnp.zeros(dk_sum.shape, f32)
        dv_sum[...] = jnp.zeros(dv_sum.shape, f32)

        def prepare(b, carry):
            k_t[b] = kv[rows_of(b), :HD].T
            v_t[b] = kv[rows_of(b), HD:].T
            return carry

        lax.fori_loop(0, blocks, prepare, 0)

    for distance in range(split):

        @pl.when(step == distance)
        def _():
            for a in range(groups):
                ref = qg_refs[a * split + distance]
                for h in range(heads):
                    part = slice(h * size + a * run, h * size + (a + 1) * run)
                    q_rows[part] = ref[:, h * HD : (h + 1) * HD]
                    g_rows[part] = ref[:, columns + h * HD : columns + (h + 1) * HD]

    q_t[...] = q_rows[...].T
    g_t[...] = g_rows[...].T
    peak8[...] = jnp.full((8, rows), NEG, f32)
    total8[...] = jnp.zeros((8, rows), f32)
    out_t[...] = jnp.zeros((HD, rows), f32)
    dq_t[...] = jnp.zeros((HD, rows), f32)

    q_first = (ctx ^ step) * size
    low_first = record_start(q_first)
    low_last = record_start(q_first + (size - 1))
    token = lax.broadcasted_iota(jnp.int32, (1, rows), 1) % size
    if groups > 1:
        token = ((token // run) ^ own) * run + token % run
    pos = q_first + token
    low = record_start(pos)
    first = (low_first - origin) // KB
    last = (q_first + (size - 1) - origin) // KB + 1

    def fold(values, combine):
        result = values[0:8]
        for start in range(8, values.shape[0], 8):
            result = combine(result, values[start : start + 8])
        return result

    def score_pass(b, carry):
        base = origin + b * KB
        whole = (base + (KB - 1) <= q_first) & (base >= low_last)

        @pl.when(whole)
        def _():
            for part in chunks:
                s = jnp.dot(kv[rows_of(b), :HD], q_t[:, part], preferred_element_type=f32)
                scores[b - first, :, part] = s
                peak8[:, part] = jnp.maximum(peak8[:, part], fold(s, jnp.maximum))

        @pl.when(jnp.logical_not(whole))
        def _():
            for part in chunks:
                s = jnp.dot(kv[rows_of(b), :HD], q_t[:, part], preferred_element_type=f32)
                key_pos = base + lax.broadcasted_iota(jnp.int32, s.shape, 0)
                allowed = (key_pos <= pos[:, part]) & (key_pos >= low[:, part])
                s = jnp.where(allowed, s, NEG)
                scores[b - first, :, part] = s
                peak8[:, part] = jnp.maximum(peak8[:, part], fold(s, jnp.maximum))

        return carry

    lax.fori_loop(first, last, score_pass, 0)
    peak = jnp.max(peak8[...], axis=0, keepdims=True) * TO_EXP2

    def weight_pass(b, carry):
        for part in chunks:
            w = jnp.exp2(scores[b - first, :, part] * TO_EXP2 - peak[:, part])
            total8[:, part] += fold(w, jnp.add)
            w_b = w.astype(bf16)
            weights[b - first, :, part] = w_b
            out_t[:, part] += jnp.dot(v_t[b], w_b, preferred_element_type=f32)
        return carry

    lax.fori_loop(first, last, weight_pass, 0)
    inverse = 1.0 / jnp.sum(total8[...], axis=0, keepdims=True)
    out_b = (out_t[...] * inverse).astype(bf16)
    g_wide = g_t[...].astype(f32)
    delta = jnp.sum(g_wide * out_b.astype(f32), axis=0, keepdims=True) * inverse
    g_scaled = (g_wide * inverse).astype(bf16)
    g_t[...] = g_scaled
    g_rows[...] = g_scaled.T

    def give(wide, first):
        for distance in range(split):

            @pl.when(step == distance)
            def _():
                for a in range(groups):
                    to = pl.ds(pl.multiple_of((own ^ a) * run, 16), run)
                    for h in range(heads):
                        start = h * size + a * run
                        out_refs[distance][to, first + h * HD : first + (h + 1) * HD] = wide[
                            start : start + run
                        ]

    give(out_b.T, 0)

    def grad_pass(b, carry):
        for part in chunks:
            dp = jnp.dot(kv[rows_of(b), HD:], g_t[:, part], preferred_element_type=f32)
            w = weights[b - first, :, part].astype(f32)
            dscores[:, part] = (w * (dp - delta[:, part])).astype(bf16)
        dv_sum[rows_of(b)] += jnp.dot(weights[b - first], g_rows[...], preferred_element_type=f32)
        dk_sum[rows_of(b)] += jnp.dot(dscores[...], q_rows[...], preferred_element_type=f32)
        dq_t[...] += jnp.dot(k_t[b], dscores[...], preferred_element_type=f32)
        return carry

    lax.fori_loop(first, last, grad_pass, 0)
    give((dq_t[...] * SCALE).astype(bf16).T, heads * HD)

    @pl.when(step == split - 1)
    def _():
        for index in range(pieces):
            term_refs[index][0] = (dk_sum[piece_rows(index)] * SCALE).astype(bf16)
            term_refs[index][1] = dv_sum[piece_rows(index)].astype(bf16)


def attention(qg_pieces, kv_pieces, info, lengths, split, most, reach, tail):
    run, columns = qg_pieces[0].shape
    groups = len(qg_pieces) // split
    size = groups * run
    heads = columns // (2 * HD)
    rows = size * heads
    pieces = len(kv_pieces)
    keys = -(-sum(part.shape[1] for part in kv_pieces) // KB) * KB
    blocks = keys // KB
    live = min(blocks, (most + size - 3) // KB + 2)
    bf16 = jnp.bfloat16
    f32 = jnp.float32

    def still(shape):
        return pl.BlockSpec(shape, lambda i, *_: (0,) * len(shape))

    kv_specs = [still(part.shape) for part in kv_pieces]
    given = (size, columns)
    pairs = size * split * heads * keys
    results = pl.pallas_call(
        functools.partial(attention_kernel, pieces, split, groups, reach, tail),
        grid_spec=pltpu.PrefetchScalarGridSpec(
            num_scalar_prefetch=2,
            grid=(split,),
            in_specs=[still((run, columns))] * len(qg_pieces) + kv_specs,
            out_specs=[still(given)] * split + kv_specs,
            scratch_shapes=[
                pltpu.VMEM((keys, 2 * HD), bf16),
                pltpu.VMEM((blocks, HD, KB), bf16),
                pltpu.VMEM((blocks, HD, KB), bf16),
                pltpu.VMEM((keys, HD), f32),
                pltpu.VMEM((keys, HD), f32),
                pltpu.VMEM((live, KB, rows), f32),
                pltpu.VMEM((live, KB, rows), bf16),
                pltpu.VMEM((KB, rows), bf16),
                pltpu.VMEM((rows, HD), bf16),
                pltpu.VMEM((HD, rows), bf16),
                pltpu.VMEM((rows, HD), bf16),
                pltpu.VMEM((HD, rows), bf16),
                pltpu.VMEM((8, rows), f32),
                pltpu.VMEM((8, rows), f32),
                pltpu.VMEM((HD, rows), f32),
                pltpu.VMEM((HD, rows), f32),
            ],
        ),
        out_shape=[jax.ShapeDtypeStruct(given, bf16)] * split
        + [jax.ShapeDtypeStruct(part.shape, bf16) for part in kv_pieces],
        compiler_params=pltpu.CompilerParams(vmem_limit_bytes=VMEM),
        cost_estimate=pl.CostEstimate(
            flops=48 * HD * pairs, bytes_accessed=32 * rows * HD * split, transcendentals=pairs
        ),
        name="attention",
    )(info, lengths, *qg_pieces, *kv_pieces)
    return results[:split], results[split:]


def settle_kernel(split, *refs):
    piece_refs, (out_ref, dq_ref, sems) = refs[:split], refs[split:]
    width = piece_refs[0].shape[1] // 2
    core = lax.axis_index("ctx") % split
    copies = []
    for distance in range(split):
        to = pl.ds(pl.multiple_of((core ^ distance) * width, HD), width)
        copies.append((piece_refs[distance].at[:, :width], out_ref.at[:, to]))
        copies.append((piece_refs[distance].at[:, width:], dq_ref.at[:, to]))
    copy_all(copies, sems)


def settle(parts):
    split = len(parts)
    rows, width = parts[0].shape
    anywhere = pl.BlockSpec(memory_space=pl.ANY)
    shape = jax.ShapeDtypeStruct((rows, width * split // 2), parts[0].dtype)
    return pl.pallas_call(
        functools.partial(settle_kernel, split),
        in_specs=[anywhere] * split,
        out_specs=[anywhere] * 2,
        out_shape=[shape] * 2,
        scratch_shapes=[pltpu.SemaphoreType.DMA((2 * split,))],
        name="settle",
    )(*parts)


def body(
    record_lengths,
    query_heads,
    key_heads,
    value_heads,
    out_grad,
    gate_input,
    key_input,
    value_input,
    hyena_grad,
    short_filter,
    long_filter,
):
    ctx = lax.axis_size("ctx")
    tp = lax.axis_size("tp")
    own_ctx = lax.axis_index("ctx")
    piece = query_heads.shape[0]
    tokens = piece * tp
    window = tokens * ctx
    most = window // 2 + 192
    split = PLANE if (KVH // tp) % PLANE == 0 else 1
    slots = tp * split
    kv_local = KVH // slots
    assert kv_local == 1 and tokens % 192 == 0
    unit = tokens * split
    lanes = PLANE // split
    plane = unit * lanes
    reach = (most - 1) // plane
    tail = -(-(most - 1 - reach * plane) // 192) * 192
    core = own_ctx % split
    lane = own_ctx // split % lanes
    level = own_ctx // PLANE
    f32 = jnp.float32
    bf16 = jnp.bfloat16

    members = [
        [t * ctx + n * split + c for t in range(tp) for c in range(split)]
        for n in range(ctx // split)
    ]

    def share(laid):
        return lax.all_to_all(
            laid, ("tp", "ctx"), 0, 0, axis_index_groups=members, tiled=True
        )

    permute = functools.partial(lax.ppermute, axis_name="ctx")

    def across(values, distance):
        return permute(values, perm=[(i, i ^ (distance * split)) for i in range(ctx)])

    def up(values):
        return permute(values, perm=[(i, i + PLANE) for i in range(ctx - PLANE)])

    def down(values):
        return permute(values, perm=[(i + PLANE, i) for i in range(ctx - PLANE)])

    def swap(values, distance):
        return permute(values, perm=[(i, i ^ distance) for i in range(ctx)])

    far = (reach + 1) * PLANE - (lanes - 1) * split
    far_pairs = [
        (i, i + far) for i in range(ctx - far) if i // split % lanes == lanes - 1
    ]

    streams = (gate_input, key_input, value_input, hyena_grad)
    heads = jnp.concatenate([s[:HALO] for s in streams], axis=0)
    tails = jnp.concatenate([s[tokens - HALO :] for s in streams], axis=0)
    before = permute(tails, perm=[(i, i + 1) for i in range(ctx - 1)])
    after = permute(heads, perm=[(i + 1, i) for i in range(ctx - 1)])

    kv = share(pack_kv(key_heads, value_heads, slots))
    if piece % 32:
        cut = [part.reshape(piece, slots, -1) for part in (query_heads, out_grad)]
        laid = jnp.concatenate(cut, axis=2).transpose(1, 0, 2)
        qg = share(laid).reshape(tp, split, piece, -1).transpose(1, 0, 2, 3)
        qg = list(qg.reshape(split, tokens, -1))
    else:
        qg = list(pack_rows(query_heads, out_grad, slots, split))

    def exchange(which):
        for distance in which:
            far_t, far_c = distance // split, distance % split
            perm = [
                (i * tp + t, (i ^ far_c) * tp + (t ^ far_t))
                for t in range(tp)
                for i in range(ctx)
            ]
            qg[distance] = lax.ppermute(qg[distance], ("ctx", "tp"), perm)

    near, rest = [], []
    if piece % 32 == 0:
        single = [1 << bit for bit in range(1, slots.bit_length() - 1)]
        near = [n + c for n in single for c in (0, 1)]
        rest = [d for d in range(1, slots) if d not in near]
        before, after, *held = lax.optimization_barrier(
            (before, after) + tuple(qg[d] for d in near)
        )
        for distance, value in zip(near, held):
            qg[distance] = value
        exchange(near)
    own_kv = kv.reshape(tp, split, 2, piece, kv_local * HD)
    own_kv = own_kv.transpose(2, 1, 0, 3, 4).reshape(2, unit, kv_local * HD)

    filters = (short_filter, long_filter)
    columns = [own_kv]
    hyena_outs = ()
    for hop in range(reach):
        coming = up(columns[-1])
        if hop < 2:
            before, columns[-1] = lax.optimization_barrier((before, columns[-1]))
            hyena_outs = hyena(streams, before, after, *filters, hop, 2, hyena_outs)
            if hop:
                near, rest = [], []
            coming, first_out, *held = lax.optimization_barrier(
                (coming, hyena_outs[0]) + tuple(qg[d] for d in near + rest)
            )
            for distance, value in zip(near + rest, held):
                qg[distance] = value
            exchange(rest)
            hyena_outs = (first_out,) + tuple(hyena_outs[1:])
        columns.append(coming)
    tail_kv = permute(own_kv[:, unit - tail :], perm=far_pairs)
    pieces = [tail_kv]
    places = [jnp.int32(0)]
    for back in range(reach + 1):
        for distance in range(lanes):
            held = columns[back]
            pieces.append(held if distance == 0 else across(held, distance))
            places.append(tail + (reach - back) * plane + (lane ^ distance) * unit)
    origin = (level - reach) * plane - tail
    info = jnp.stack([origin] + places).astype(jnp.int32)

    outs, terms = attention(
        qg, pieces, info, record_lengths, split, most, reach, tail
    )
    outs = [outs[0]] + [swap(outs[distance], distance) for distance in range(1, split)]
    attn_out, grad_query = settle(outs)

    def plane_sum(back):
        at = 1 + back * lanes
        total = terms[at].astype(f32)
        for distance in range(1, lanes):
            total = total + across(terms[at + distance], distance).astype(f32)
        return total

    tail_term = permute(terms[0], perm=[(j, i) for i, j in far_pairs])
    running = plane_sum(reach).astype(bf16)
    for back in range(reach - 1, -1, -1):
        running = plane_sum(back) + down(running).astype(f32)
        if back:
            running = running.astype(bf16)
    running, attn_out = lax.optimization_barrier((running, attn_out))
    owned = jnp.concatenate(
        [running[:, : unit - tail], running[:, unit - tail :] + tail_term.astype(f32)], axis=1
    ).astype(bf16)

    parts = []
    for distance in range(split):
        held = lax.dynamic_slice_in_dim(owned, (core ^ distance) * tokens, tokens, 1)
        parts.append(swap(held, distance) if distance else held)
    bit = 1
    while bit < split:
        parts = [
            jnp.where(core & bit != 0, parts[index ^ bit], parts[index]) for index in range(split)
        ]
        bit = 2 * bit
    grads = jnp.concatenate(parts, axis=2)
    return (attn_out, grad_query, grads[0], grads[1]) + tuple(hyena_outs)


def solution(mesh):
    rows = P(("ctx", "tp"), None)
    both = P("ctx", "tp")
    return jax.shard_map(
        body,
        mesh=mesh,
        in_specs=(P(), rows, rows, rows, rows, both, both, both, both)
        + (P(None, None, "tp"), P(None, "tp")),
        out_specs=(both,) * 8,
        check_vma=False,
    )
```

```python
import functools

import jax
import jax.numpy as jnp
import numpy as np
from jax import lax
from jax.experimental import pallas as pl
from jax.experimental.pallas import tpu as pltpu
from jax.sharding import PartitionSpec as P

HD = 128
QH = 64
KVH = 8
GROUP = 16
TAPS = 7
SHORT = 3
HALO = 8
PLANE = 4
KB = 256
NEG = -1e30
SCALE = HD ** (-0.5)
TO_EXP2 = SCALE * 1.4426950408889634
VMEM = 48 * 1024 * 1024


def hyena_kernel(
    part,
    gate_ref,
    key_ref,
    value_ref,
    grad_ref,
    before_ref,
    after_ref,
    short_ref,
    long_ref,
    *refs,
):
    out_ref, dgate_ref, dkey_ref, dvalue_ref, taps = refs[-5:]
    tokens, width = gate_ref.shape
    own = pl.program_id(0)

    @pl.when(own == 0)
    def _():
        shape = (long_ref.shape[1], taps.shape[1])
        group = lax.broadcasted_iota(jnp.int32, shape, 0)
        channel = part * taps.shape[1] + lax.broadcasted_iota(jnp.int32, shape, 1)
        taps[...] = jnp.dot(
            long_ref[...],
            (group == channel // GROUP).astype(jnp.float32),
            precision=lax.Precision.HIGHEST,
            preferred_element_type=jnp.float32,
        )

    rows = tokens + 2 * HALO

    def chunk(index, carry):
        lanes = pl.ds(pl.multiple_of(index * HD, HD), HD)
        before = before_ref[:, lanes].astype(jnp.float32)
        after = after_ref[:, lanes].astype(jnp.float32)

        def padded(ref, which):
            part = slice(which * HALO, (which + 1) * HALO)
            return jnp.concatenate(
                [before[part], ref[:, lanes].astype(jnp.float32), after[part]], axis=0
            )

        def earlier(values, amount):
            return pltpu.roll(values, amount, 0) if amount else values

        def later(values, amount):
            return pltpu.roll(values, rows - amount, 0) if amount else values

        long = taps[:, pl.ds(pl.multiple_of(own * width + index * HD, HD), HD)]

        def short(which, tap):
            return short_ref[which, tap : tap + 1, lanes]

        def featurize(values, which):
            result = short(which, 0) * values
            for tap in range(1, SHORT):
                result = result + short(which, tap) * earlier(values, tap)
            return result

        def unfeaturize(grads, which):
            result = short(which, 0) * grads
            for tap in range(1, SHORT):
                result = result + short(which, tap) * later(grads, tap)
            return result[HALO : HALO + tokens].astype(jnp.bfloat16)

        key_f = featurize(padded(key_ref, 1), 1)
        value_f = featurize(padded(value_ref, 2), 2)
        mixed = key_f * value_f
        conv = long[0:1] * mixed
        for tap in range(1, TAPS):
            conv = conv + long[tap : tap + 1] * earlier(mixed, tap)
        gate_f = featurize(padded(gate_ref, 0), 0)
        out_ref[:, lanes] = (gate_f * conv)[HALO : HALO + tokens].astype(jnp.bfloat16)
        grad = padded(grad_ref, 3)
        dgate_ref[:, lanes] = unfeaturize(grad * conv, 0)
        dconv = grad * gate_f
        dmixed = long[0:1] * dconv
        for tap in range(1, TAPS):
            dmixed = dmixed + long[tap : tap + 1] * later(dconv, tap)
        dkey_ref[:, lanes] = unfeaturize(dmixed * value_f, 1)
        dvalue_ref[:, lanes] = unfeaturize(dmixed * key_f, 2)
        return carry

    lax.fori_loop(0, width // HD, chunk, 0)


def hyena(streams, before, after, short_filter, long_filter, part, parts, filled=()):
    tokens, channels = streams[0].shape
    own = channels // parts
    width = min(512, own)
    steps = own // width
    block = pl.BlockSpec((tokens, width), lambda i: (0, part * steps + i))
    edge = pl.BlockSpec((4 * HALO, width), lambda i: (0, part * steps + i))
    return pl.pallas_call(
        functools.partial(hyena_kernel, part),
        grid=(steps,),
        in_specs=[block] * 4
        + [edge, edge]
        + [
            pl.BlockSpec((3, SHORT, width), lambda i: (0, 0, part * steps + i)),
            pl.BlockSpec(long_filter.shape, lambda i: (0, 0)),
        ]
        + [pl.BlockSpec(memory_space=pl.ANY)] * len(filled),
        out_specs=[block] * 4,
        out_shape=[jax.ShapeDtypeStruct((tokens, channels), jnp.bfloat16)] * 4,
        scratch_shapes=[pltpu.VMEM((TAPS, own), jnp.float32)],
        input_output_aliases={8 + i: i for i in range(len(filled))},
        compiler_params=pltpu.CompilerParams(vmem_limit_bytes=VMEM),
        cost_estimate=pl.CostEstimate(
            flops=14000 * tokens * own, bytes_accessed=16 * tokens * own, transcendentals=0
        ),
        name="hyena",
    )(*streams, before, after, short_filter, long_filter, *filled)


def own_slot(split):
    return lax.axis_index("tp") * split + lax.axis_index("ctx") % split


def pack_edges_kernel(k_ref, v_ref, *refs):
    streams = (len(refs) - 3) // 2
    first_refs, last_refs = refs[:streams], refs[streams : 2 * streams]
    kv_ref, heads_ref, tails_ref = refs[2 * streams :]
    width = kv_ref.shape[3]
    for slot in range(kv_ref.shape[0]):
        part = slice(slot * width, (slot + 1) * width)
        kv_ref[slot, 0] = k_ref[:, part]
        kv_ref[slot, 1] = v_ref[:, part]
    f32 = jnp.float32
    for refs, target, start in ((first_refs, heads_ref, 0), (last_refs, tails_ref, HALO)):
        for at in range(0, streams, 2):
            pair = [ref[...].astype(f32)[start : start + HALO] for ref in refs[at : at + 2]]
            rows = slice(at * HALO, (at + 2) * HALO)
            target[rows] = jnp.concatenate(pair, axis=0).astype(target.dtype)


def pack_edges(keys, values, streams, slots):
    rows, columns = keys.shape
    tokens, channels = streams[0].shape
    edge = 2 * HALO
    count = len(streams)
    whole = pl.BlockSpec((rows, columns), lambda i: (0, 0))
    first = pl.BlockSpec((edge, channels), lambda i: (0, 0))
    last = pl.BlockSpec((edge, channels), lambda i: (tokens // edge - 1, 0))
    halo = (count * HALO, channels)
    laid = (slots, 2, rows, columns // slots)
    return pl.pallas_call(
        pack_edges_kernel,
        grid=(1,),
        in_specs=[whole] * 2 + [first] * count + [last] * count,
        out_specs=[
            pl.BlockSpec(laid, lambda i: (0, 0, 0, 0)),
            pl.BlockSpec(halo, lambda i: (0, 0)),
            pl.BlockSpec(halo, lambda i: (0, 0)),
        ],
        out_shape=[jax.ShapeDtypeStruct(shape, keys.dtype) for shape in (laid, halo, halo)],
        name="pack_edges",
    )(keys, values, *streams, *streams)


def pack_rows_kernel(split, q_ref, g_ref, *outs):
    width = outs[0].shape[1] // 2
    slot = own_slot(split)
    for distance, out in enumerate(outs):
        part = pl.ds(pl.multiple_of((slot ^ distance) * width, HD), width)
        out[:, :width] = q_ref[:, part]
        out[:, width:] = g_ref[:, part]


def pack_rows(queries, grads, slots, split):
    rows, columns = queries.shape
    shape = jax.ShapeDtypeStruct((rows, 2 * columns // slots), queries.dtype)
    return pl.pallas_call(
        functools.partial(pack_rows_kernel, split),
        out_shape=[shape] * slots,
        compiler_params=pltpu.CompilerParams(vmem_limit_bytes=VMEM),
        name="pack_rows",
    )(queries, grads)


def attention_kernel(pieces, distances, groups, prior, *refs):
    (info_ref, lengths_ref), refs = refs[:2], refs[2:]
    steps = len(distances)
    qg_refs, refs = refs[: steps * groups], refs[steps * groups :]
    piece_refs, refs = refs[:pieces], refs[pieces:]
    prior_refs, refs = refs[: prior * pieces], refs[prior * pieces :]
    out_refs, refs = refs[:steps], refs[steps:]
    term_refs, refs = refs[:pieces], refs[pieces:]
    kv, k_t, v_t, dk_sum, dv_sum, scores, weights, dscores = refs[:8]
    q_rows, g_rows, peak8, total8, out_t, dq_t = refs[8:]
    step = pl.program_id(0)
    blocks = k_t.shape[0]
    run = qg_refs[0].shape[0]
    columns = qg_refs[0].shape[1] // 2
    heads = columns // HD
    size = groups * run
    rows = size * heads
    f32 = jnp.float32
    bf16 = jnp.bfloat16
    chunks = [slice(start, min(start + 256, rows)) for start in range(0, rows, 256)]
    ctx = lax.axis_index("ctx")
    own = lax.axis_index("tp") if groups > 1 else 0
    origin = info_ref[0]

    def record_start(position):
        ends = 0
        start = position * 0
        for record in range(lengths_ref.shape[0]):
            ends = ends + lengths_ref[record]
            start = jnp.where(position >= ends, ends, start)
        return start

    def rows_of(b):
        return pl.ds(pl.multiple_of(b * KB, KB), KB)

    def piece_rows(index):
        count = piece_refs[index].shape[1]
        return pl.ds(pl.multiple_of(info_ref[1 + index], 64), count)

    @pl.when(step == 0)
    def _():
        filled = sum(ref.shape[1] for ref in piece_refs)
        if filled < kv.shape[0]:
            kv[filled:] = jnp.zeros((kv.shape[0] - filled, 2 * HD), bf16)
        for index in range(pieces):
            kv[piece_rows(index), :HD] = piece_refs[index][0]
            kv[piece_rows(index), HD:] = piece_refs[index][1]
        dk_sum[...] = jnp.zeros(dk_sum.shape, f32)
        dv_sum[...] = jnp.zeros(dv_sum.shape, f32)

        def prepare(b, carry):
            k_t[b] = kv[rows_of(b), :HD].T
            v_t[b] = kv[rows_of(b), HD:].T
            return carry

        lax.fori_loop(0, blocks, prepare, 0)

    for which in range(steps):

        @pl.when(step == which)
        def _():
            for a in range(groups):
                ref = qg_refs[which * groups + a]
                for h in range(heads):
                    part = slice(h * size + a * run, h * size + (a + 1) * run)
                    q_rows[part] = ref[:, h * HD : (h + 1) * HD]
                    g_rows[part] = ref[:, columns + h * HD : columns + (h + 1) * HD]

    peak8[...] = jnp.full((8, rows), NEG, f32)
    total8[...] = jnp.zeros((8, rows), f32)
    out_t[...] = jnp.zeros((HD, rows), f32)
    dq_t[...] = jnp.zeros((HD, rows), f32)

    distance = distances[0]
    for which in range(1, steps):
        distance = jnp.where(step == which, distances[which], distance)
    q_first = (ctx ^ distance) * size
    low_first = record_start(q_first)
    low_last = record_start(q_first + (size - 1))
    token = lax.broadcasted_iota(jnp.int32, (1, rows), 1) % size
    if groups > 1:
        token = ((token // run) ^ own) * run + token % run
    pos = q_first + token
    low = record_start(pos)
    first = (low_first - origin) // KB
    last = (q_first + (size - 1) - origin) // KB + 1

    def by_rows(left, right):
        return lax.dot_general(
            left, right, (((1,), (1,)), ((), ())), preferred_element_type=f32
        )

    def fold(values, combine):
        result = values[0:8]
        for start in range(8, values.shape[0], 8):
            result = combine(result, values[start : start + 8])
        return result

    def score_pass(b, carry):
        base = origin + b * KB
        whole = (base + (KB - 1) <= q_first) & (base >= low_last)

        @pl.when(whole)
        def _():
            for part in chunks:
                s = by_rows(kv[rows_of(b), :HD], q_rows[part])
                scores[b - first, :, part] = s
                peak8[:, part] = jnp.maximum(peak8[:, part], fold(s, jnp.maximum))

        @pl.when(jnp.logical_not(whole))
        def _():
            for part in chunks:
                s = by_rows(kv[rows_of(b), :HD], q_rows[part])
                key_pos = base + lax.broadcasted_iota(jnp.int32, s.shape, 0)
                allowed = (key_pos <= pos[:, part]) & (key_pos >= low[:, part])
                s = jnp.where(allowed, s, NEG)
                scores[b - first, :, part] = s
                peak8[:, part] = jnp.maximum(peak8[:, part], fold(s, jnp.maximum))

        return carry

    lax.fori_loop(first, last, score_pass, 0)
    peak = jnp.max(peak8[...], axis=0, keepdims=True) * TO_EXP2

    def weight_pass(b, carry):
        for part in chunks:
            w = jnp.exp2(scores[b - first, :, part] * TO_EXP2 - peak[:, part])
            total8[:, part] += fold(w, jnp.add)
            w_b = w.astype(bf16)
            weights[b - first, :, part] = w_b
            out_t[:, part] += jnp.dot(v_t[b], w_b, preferred_element_type=f32)
        return carry

    lax.fori_loop(first, last, weight_pass, 0)
    inverse = 1.0 / jnp.sum(total8[...], axis=0, keepdims=True)
    out_b = (out_t[...] * inverse).astype(bf16)
    out_rows = out_b.T
    g_wide = g_rows[...].astype(f32)
    products = g_wide * out_rows.astype(f32)
    high = products.astype(bf16)
    rest = (products - high.astype(f32)).astype(bf16)
    ones = jnp.ones((8, HD), bf16)
    delta = (by_rows(ones, high) + by_rows(ones, rest))[0:1] * inverse
    g_rows[...] = (g_wide * jnp.broadcast_to(inverse, (8, rows)).T[:, 0:1]).astype(bf16)

    def give(wide, first):
        for which in range(steps):

            @pl.when(step == which)
            def _():
                for a in range(groups):
                    to = pl.ds(pl.multiple_of((own ^ a) * run, 16), run)
                    for h in range(heads):
                        start = h * size + a * run
                        out_refs[which][to, first + h * HD : first + (h + 1) * HD] = wide[
                            start : start + run
                        ]

    give(out_rows, 0)

    def grad_pass(b, carry):
        for part in chunks:
            dp = by_rows(kv[rows_of(b), HD:], g_rows[part])
            w = weights[b - first, :, part].astype(f32)
            dscores[:, part] = (w * (dp - delta[:, part])).astype(bf16)
        dv_sum[rows_of(b)] += jnp.dot(weights[b - first], g_rows[...], preferred_element_type=f32)
        dk_sum[rows_of(b)] += jnp.dot(dscores[...], q_rows[...], preferred_element_type=f32)
        dq_t[...] += jnp.dot(k_t[b], dscores[...], preferred_element_type=f32)
        return carry

    lax.fori_loop(first, last, grad_pass, 0)
    give((dq_t[...] * SCALE).astype(bf16).T, heads * HD)

    @pl.when(step == steps - 1)
    def _():
        for index in range(pieces):
            dk = dk_sum[piece_rows(index)] * SCALE
            dv = dv_sum[piece_rows(index)]
            if prior:
                dk = dk + prior_refs[index][0].astype(f32)
                dv = dv + prior_refs[index][1].astype(f32)
            term_refs[index][0] = dk.astype(bf16)
            term_refs[index][1] = dv.astype(bf16)


def attention(qg_pieces, kv_pieces, info, lengths, distances, most, prior=()):
    run, columns = qg_pieces[0].shape
    steps = len(distances)
    groups = len(qg_pieces) // steps
    size = groups * run
    heads = columns // (2 * HD)
    rows = size * heads
    pieces = len(kv_pieces)
    keys = -(-sum(part.shape[1] for part in kv_pieces) // KB) * KB
    blocks = keys // KB
    live = min(blocks, (most + size - 3) // KB + 2)
    bf16 = jnp.bfloat16
    f32 = jnp.float32

    def still(shape):
        return pl.BlockSpec(shape, lambda i, *_: (0,) * len(shape))

    kv_specs = [still(part.shape) for part in kv_pieces]
    given = (size, columns)
    pairs = size * steps * heads * keys
    results = pl.pallas_call(
        functools.partial(attention_kernel, pieces, distances, groups, 1 if prior else 0),
        grid_spec=pltpu.PrefetchScalarGridSpec(
            num_scalar_prefetch=2,
            grid=(steps,),
            in_specs=[still((run, columns))] * len(qg_pieces)
            + kv_specs
            + (kv_specs if prior else []),
            out_specs=[still(given)] * steps + kv_specs,
            scratch_shapes=[
                pltpu.VMEM((keys, 2 * HD), bf16),
                pltpu.VMEM((blocks, HD, KB), bf16),
                pltpu.VMEM((blocks, HD, KB), bf16),
                pltpu.VMEM((keys, HD), f32),
                pltpu.VMEM((keys, HD), f32),
                pltpu.VMEM((live, KB, rows), f32),
                pltpu.VMEM((live, KB, rows), bf16),
                pltpu.VMEM((KB, rows), bf16),
                pltpu.VMEM((rows, HD), bf16),
                pltpu.VMEM((rows, HD), bf16),
                pltpu.VMEM((8, rows), f32),
                pltpu.VMEM((8, rows), f32),
                pltpu.VMEM((HD, rows), f32),
                pltpu.VMEM((HD, rows), f32),
            ],
        ),
        out_shape=[jax.ShapeDtypeStruct(given, bf16)] * steps
        + [jax.ShapeDtypeStruct(part.shape, bf16) for part in kv_pieces],
        compiler_params=pltpu.CompilerParams(vmem_limit_bytes=VMEM),
        cost_estimate=pl.CostEstimate(
            flops=48 * HD * pairs, bytes_accessed=32 * rows * HD * steps, transcendentals=pairs
        ),
        name="attention",
    )(info, lengths, *qg_pieces, *kv_pieces, *prior)
    return results[:steps], results[steps:]


def settle_kernel(split, *refs):
    piece_refs, (out_ref, dq_ref) = refs[:split], refs[split:]
    width = piece_refs[0].shape[1] // 2
    core = lax.axis_index("ctx") % split
    for distance in range(split):
        to = pl.ds(pl.multiple_of((core ^ distance) * width, HD), width)
        out_ref[:, to] = piece_refs[distance][:, :width]
        dq_ref[:, to] = piece_refs[distance][:, width:]


def settle(parts):
    split = len(parts)
    rows, width = parts[0].shape
    shape = jax.ShapeDtypeStruct((rows, width * split // 2), parts[0].dtype)
    return pl.pallas_call(
        functools.partial(settle_kernel, split),
        out_shape=[shape] * 2,
        compiler_params=pltpu.CompilerParams(vmem_limit_bytes=VMEM),
        name="settle",
    )(*parts)


def body(
    record_lengths,
    query_heads,
    key_heads,
    value_heads,
    out_grad,
    gate_input,
    key_input,
    value_input,
    hyena_grad,
    short_filter,
    long_filter,
):
    ctx = lax.axis_size("ctx")
    tp = lax.axis_size("tp")
    own_ctx = lax.axis_index("ctx")
    piece = query_heads.shape[0]
    tokens = piece * tp
    window = tokens * ctx
    most = window // 2 + 192
    split = PLANE if (KVH // tp) % PLANE == 0 else 1
    slots = tp * split
    kv_local = KVH // slots
    assert kv_local == 1 and tokens % 192 == 0
    unit = tokens * split
    lanes = PLANE // split
    plane = unit * lanes
    reach = (most - 1) // plane
    tail = -(-(most - 1 - reach * plane) // 192) * 192
    core = own_ctx % split
    lane = own_ctx // split % lanes
    level = own_ctx // PLANE
    f32 = jnp.float32
    bf16 = jnp.bfloat16

    members = [
        [t * ctx + n * split + c for t in range(tp) for c in range(split)]
        for n in range(ctx // split)
    ]

    def share(laid):
        return lax.all_to_all(
            laid, ("tp", "ctx"), 0, 0, axis_index_groups=members, tiled=True
        )

    permute = functools.partial(lax.ppermute, axis_name="ctx")

    def across(values, distance):
        return permute(values, perm=[(i, i ^ (distance * split)) for i in range(ctx)])

    def up(values):
        return permute(values, perm=[(i, i + PLANE) for i in range(ctx - PLANE)])

    def down(values):
        return permute(values, perm=[(i + PLANE, i) for i in range(ctx - PLANE)])

    def swap(values, distance):
        return permute(values, perm=[(i, i ^ distance) for i in range(ctx)])

    far = (reach + 1) * PLANE - (lanes - 1) * split
    far_pairs = [
        (i, i + far) for i in range(ctx - far) if i // split % lanes == lanes - 1
    ]

    streams = (gate_input, key_input, value_input, hyena_grad)
    laid_kv, heads, tails = pack_edges(key_heads, value_heads, streams, slots)
    before = permute(tails, perm=[(i, i + 1) for i in range(ctx - 1)])
    after = permute(heads, perm=[(i + 1, i) for i in range(ctx - 1)])

    kv = share(laid_kv)
    if piece % 32:
        cut = [part.reshape(piece, slots, -1) for part in (query_heads, out_grad)]
        laid = jnp.concatenate(cut, axis=2).transpose(1, 0, 2)
        qg = share(laid).reshape(tp, split, piece, -1).transpose(1, 0, 2, 3)
        qg = list(qg.reshape(split, tokens, -1))
    else:
        laid_kv, query_heads = lax.optimization_barrier((laid_kv, query_heads))
        qg = list(pack_rows(query_heads, out_grad, slots, split))

    def exchange(which):
        for distance in which:
            far_t, far_c = distance // split, distance % split
            perm = [
                (i * tp + t, (i ^ far_c) * tp + (t ^ far_t))
                for t in range(tp)
                for i in range(ctx)
            ]
            qg[distance] = lax.ppermute(qg[distance], ("ctx", "tp"), perm)

    calls = [(split - 1, 0), (split // 2, split // 2 - 1)] if split > 1 else [(0,)]

    def rows_for(call):
        return [a * split + c for c in calls[call] for a in range(tp)]

    if piece % 32 == 0:
        first = [d for d in rows_for(0) if d]
        before, after, *held = lax.optimization_barrier(
            (before, after) + tuple(qg[d] for d in first)
        )
        for distance, value in zip(first, held):
            qg[distance] = value
        exchange(first)
    own_kv = kv.reshape(tp, split, 2, piece, kv_local * HD)
    own_kv = own_kv.transpose(2, 1, 0, 3, 4).reshape(2, unit, kv_local * HD)

    filters = (short_filter, long_filter)
    columns = [own_kv]
    hyena_outs = ()
    for hop in range(reach):
        coming = up(columns[-1])
        if hop < 2:
            before, columns[-1] = lax.optimization_barrier((before, columns[-1]))
            hyena_outs = hyena(streams, before, after, *filters, hop, 2, hyena_outs)
            coming, first_out = lax.optimization_barrier((coming, hyena_outs[0]))
            hyena_outs = (first_out,) + tuple(hyena_outs[1:])
        columns.append(coming)
    tail_kv = permute(own_kv[:, unit - tail :], perm=far_pairs)
    pieces = [tail_kv]
    places = [jnp.int32(0)]
    for back in range(reach + 1):
        for distance in range(lanes):
            held = columns[back]
            pieces.append(held if distance == 0 else across(held, distance))
            places.append(tail + (reach - back) * plane + (lane ^ distance) * unit)
    origin = (level - reach) * plane - tail
    info = jnp.stack([origin] + places).astype(jnp.int32)

    owners = [None] * split
    terms = ()
    arrived = None
    for call, distances in enumerate(calls):
        if call:
            exchange(rows_for(call))
        held = [qg[d] for d in rows_for(call)] if piece % 32 == 0 else qg
        outs, terms = attention(held, pieces, info, record_lengths, distances, most, terms)
        if arrived is not None:
            arrived, first_term = lax.optimization_barrier((arrived, terms[1 + reach * lanes]))
            terms = list(terms)
            terms[1 + reach * lanes] = first_term
            owners[calls[0][0]] = arrived
        for distance, value in zip(distances, outs):
            owners[distance] = swap(value, distance) if distance else value
        if call == 0 and split > 1:
            arrived = owners[distances[0]]
    attn_out, grad_query = settle(owners)

    def plane_sum(back):
        at = 1 + back * lanes
        total = terms[at].astype(f32)
        for distance in range(1, lanes):
            total = total + across(terms[at + distance], distance).astype(f32)
        return total

    tail_term = permute(terms[0], perm=[(j, i) for i, j in far_pairs])
    running = plane_sum(reach).astype(bf16)
    for back in range(reach - 1, -1, -1):
        running = plane_sum(back) + down(running).astype(f32)
        if back:
            running = running.astype(bf16)
    running, attn_out = lax.optimization_barrier((running, attn_out))
    owned = jnp.concatenate(
        [running[:, : unit - tail], running[:, unit - tail :] + tail_term.astype(f32)], axis=1
    ).astype(bf16)

    parts = []
    for distance in range(split):
        held = lax.dynamic_slice_in_dim(owned, (core ^ distance) * tokens, tokens, 1)
        parts.append(swap(held, distance) if distance else held)
    bit = 1
    while bit < split:
        parts = [
            jnp.where(core & bit != 0, parts[index ^ bit], parts[index]) for index in range(split)
        ]
        bit = 2 * bit
    grads = jnp.concatenate(parts, axis=2)
    return (attn_out, grad_query, grads[0], grads[1]) + tuple(hyena_outs)


def solution(mesh):
    rows = P(("ctx", "tp"), None)
    both = P("ctx", "tp")
    return jax.shard_map(
        body,
        mesh=mesh,
        in_specs=(P(), rows, rows, rows, rows, both, both, both, both)
        + (P(None, None, "tp"), P(None, "tp")),
        out_specs=(both,) * 8,
        check_vma=False,
    )
```

```python
import functools

import jax
import jax.numpy as jnp
import numpy as np
from jax import lax
from jax.experimental import pallas as pl
from jax.experimental.pallas import tpu as pltpu
from jax.sharding import PartitionSpec as P

HD = 128
QH = 64
KVH = 8
GROUP = 16
TAPS = 7
SHORT = 3
HALO = 8
PLANE = 4
KB = 256
NEG = -1e30
SCALE = HD ** (-0.5)
TO_EXP2 = SCALE * 1.4426950408889634
CHUNK = 512
VMEM = 48 * 1024 * 1024
VMEM_ATTENTION = 58 * 1024 * 1024


def hyena_kernel(
    part,
    gate_ref,
    key_ref,
    value_ref,
    grad_ref,
    before_ref,
    after_ref,
    short_ref,
    long_ref,
    *refs,
):
    out_ref, dgate_ref, dkey_ref, dvalue_ref, taps = refs[-5:]
    tokens, width = gate_ref.shape
    own = pl.program_id(0)

    @pl.when(own == 0)
    def _():
        shape = (long_ref.shape[1], taps.shape[1])
        group = lax.broadcasted_iota(jnp.int32, shape, 0)
        channel = part * taps.shape[1] + lax.broadcasted_iota(jnp.int32, shape, 1)
        taps[...] = jnp.dot(
            long_ref[...],
            (group == channel // GROUP).astype(jnp.float32),
            precision=lax.Precision.HIGHEST,
            preferred_element_type=jnp.float32,
        )

    rows = tokens + 2 * HALO

    def chunk(index, carry):
        lanes = pl.ds(pl.multiple_of(index * HD, HD), HD)
        before = before_ref[:, lanes].astype(jnp.float32)
        after = after_ref[:, lanes].astype(jnp.float32)

        def padded(ref, which):
            part = slice(which * HALO, (which + 1) * HALO)
            return jnp.concatenate(
                [before[part], ref[:, lanes].astype(jnp.float32), after[part]], axis=0
            )

        def earlier(values, amount):
            return pltpu.roll(values, amount, 0) if amount else values

        def later(values, amount):
            return pltpu.roll(values, rows - amount, 0) if amount else values

        long = taps[:, pl.ds(pl.multiple_of(own * width + index * HD, HD), HD)]

        def short(which, tap):
            return short_ref[which, tap : tap + 1, lanes]

        def featurize(values, which):
            result = short(which, 0) * values
            for tap in range(1, SHORT):
                result = result + short(which, tap) * earlier(values, tap)
            return result

        def unfeaturize(grads, which):
            result = short(which, 0) * grads
            for tap in range(1, SHORT):
                result = result + short(which, tap) * later(grads, tap)
            return result[HALO : HALO + tokens].astype(jnp.bfloat16)

        key_f = featurize(padded(key_ref, 1), 1)
        value_f = featurize(padded(value_ref, 2), 2)
        mixed = key_f * value_f
        conv = long[0:1] * mixed
        for tap in range(1, TAPS):
            conv = conv + long[tap : tap + 1] * earlier(mixed, tap)
        gate_f = featurize(padded(gate_ref, 0), 0)
        out_ref[:, lanes] = (gate_f * conv)[HALO : HALO + tokens].astype(jnp.bfloat16)
        grad = padded(grad_ref, 3)
        dgate_ref[:, lanes] = unfeaturize(grad * conv, 0)
        dconv = grad * gate_f
        dmixed = long[0:1] * dconv
        for tap in range(1, TAPS):
            dmixed = dmixed + long[tap : tap + 1] * later(dconv, tap)
        dkey_ref[:, lanes] = unfeaturize(dmixed * value_f, 1)
        dvalue_ref[:, lanes] = unfeaturize(dmixed * key_f, 2)
        return carry

    lax.fori_loop(0, width // HD, chunk, 0)


def hyena(streams, before, after, short_filter, long_filter, part, parts, filled=()):
    tokens, channels = streams[0].shape
    own = channels // parts
    width = min(512, own)
    steps = own // width
    block = pl.BlockSpec((tokens, width), lambda i: (0, part * steps + i))
    edge = pl.BlockSpec((4 * HALO, width), lambda i: (0, part * steps + i))
    return pl.pallas_call(
        functools.partial(hyena_kernel, part),
        grid=(steps,),
        in_specs=[block] * 4
        + [edge, edge]
        + [
            pl.BlockSpec((3, SHORT, width), lambda i: (0, 0, part * steps + i)),
            pl.BlockSpec(long_filter.shape, lambda i: (0, 0)),
        ]
        + [pl.BlockSpec(memory_space=pl.ANY)] * len(filled),
        out_specs=[block] * 4,
        out_shape=[jax.ShapeDtypeStruct((tokens, channels), jnp.bfloat16)] * 4,
        scratch_shapes=[pltpu.VMEM((TAPS, own), jnp.float32)],
        input_output_aliases={8 + i: i for i in range(len(filled))},
        compiler_params=pltpu.CompilerParams(vmem_limit_bytes=VMEM),
        cost_estimate=pl.CostEstimate(
            flops=14000 * tokens * own, bytes_accessed=16 * tokens * own, transcendentals=0
        ),
        name="hyena",
    )(*streams, before, after, short_filter, long_filter, *filled)


def own_slot(split):
    return lax.axis_index("tp") * split + lax.axis_index("ctx") % split


def pack_edges_kernel(k_ref, v_ref, *refs):
    streams = (len(refs) - 3) // 2
    first_refs, last_refs = refs[:streams], refs[streams : 2 * streams]
    kv_ref, heads_ref, tails_ref = refs[2 * streams :]
    width = kv_ref.shape[3]
    for slot in range(kv_ref.shape[0]):
        part = slice(slot * width, (slot + 1) * width)
        kv_ref[slot, 0] = k_ref[:, part]
        kv_ref[slot, 1] = v_ref[:, part]
    f32 = jnp.float32
    for refs, target, start in ((first_refs, heads_ref, 0), (last_refs, tails_ref, HALO)):
        for at in range(0, streams, 2):
            pair = [ref[...].astype(f32)[start : start + HALO] for ref in refs[at : at + 2]]
            rows = slice(at * HALO, (at + 2) * HALO)
            target[rows] = jnp.concatenate(pair, axis=0).astype(target.dtype)


def pack_edges(keys, values, streams, slots):
    rows, columns = keys.shape
    tokens, channels = streams[0].shape
    edge = 2 * HALO
    count = len(streams)
    whole = pl.BlockSpec((rows, columns), lambda i: (0, 0))
    first = pl.BlockSpec((edge, channels), lambda i: (0, 0))
    last = pl.BlockSpec((edge, channels), lambda i: (tokens // edge - 1, 0))
    halo = (count * HALO, channels)
    laid = (slots, 2, rows, columns // slots)
    return pl.pallas_call(
        pack_edges_kernel,
        grid=(1,),
        in_specs=[whole] * 2 + [first] * count + [last] * count,
        out_specs=[
            pl.BlockSpec(laid, lambda i: (0, 0, 0, 0)),
            pl.BlockSpec(halo, lambda i: (0, 0)),
            pl.BlockSpec(halo, lambda i: (0, 0)),
        ],
        out_shape=[jax.ShapeDtypeStruct(shape, keys.dtype) for shape in (laid, halo, halo)],
        name="pack_edges",
    )(keys, values, *streams, *streams)


def pack_rows_kernel(split, q_ref, g_ref, *refs):
    outs, sems = refs[:-1], refs[-1]
    width = outs[0].shape[1] // 2
    slot = own_slot(split)
    copies = []
    for distance, out in enumerate(outs):
        part = pl.ds(pl.multiple_of((slot ^ distance) * width, HD), width)
        for ref, first in ((q_ref, 0), (g_ref, width)):
            copies.append(
                pltpu.make_async_copy(
                    ref.at[:, part], out.at[:, first : first + width], sems.at[len(copies)]
                )
            )
    for copy in copies:
        copy.start()
    for copy in copies:
        copy.wait()


def pack_rows(queries, grads, slots, split):
    rows, columns = queries.shape
    shape = jax.ShapeDtypeStruct((rows, 2 * columns // slots), queries.dtype)
    return pl.pallas_call(
        functools.partial(pack_rows_kernel, split),
        in_specs=[pl.BlockSpec(memory_space=pltpu.VMEM)] * 2,
        out_specs=[pl.BlockSpec(memory_space=pltpu.HBM)] * slots,
        out_shape=[shape] * slots,
        scratch_shapes=[pltpu.SemaphoreType.DMA((2 * slots,))],
        compiler_params=pltpu.CompilerParams(vmem_limit_bytes=VMEM),
        name="pack_rows",
    )(queries, grads)


def attention_kernel(pieces, distances, groups, begun, ended, *refs):
    (info_ref, lengths_ref), refs = refs[:2], refs[2:]
    steps = len(distances)
    qg_refs, refs = refs[: steps * groups], refs[steps * groups :]
    piece_refs, refs = refs[:pieces], refs[pieces:]
    begun_refs, refs = refs[: 2 * begun], refs[2 * begun :]
    out_refs, refs = refs[:steps], refs[steps:]
    count = pieces if ended else 2
    term_refs, refs = refs[:count], refs[count:]
    kv, dk_t, dv_t, scores, weights, dscores = refs[:6]
    q_rows, g_rows, q_t, g_t, peak, total, delta, out_sum, dq_sum, last_key, first_key = refs[6:]
    step = pl.program_id(0)
    blocks = dk_t.shape[0]
    run = qg_refs[0].shape[0]
    columns = qg_refs[0].shape[1] // 2
    heads = columns // HD
    size = groups * run
    rows = size * heads
    f32 = jnp.float32
    bf16 = jnp.bfloat16
    chunks = [slice(start, min(start + CHUNK, rows)) for start in range(0, rows, CHUNK)]
    ctx = lax.axis_index("ctx")
    own = lax.axis_index("tp") if groups > 1 else 0
    origin = info_ref[0]

    def record_start(position):
        ends = 0
        start = position * 0
        for record in range(lengths_ref.shape[0]):
            ends = ends + lengths_ref[record]
            start = jnp.where(position >= ends, ends, start)
        return start

    def rows_of(b):
        return pl.ds(pl.multiple_of(b * KB, KB), KB)

    def piece_rows(index):
        count = piece_refs[index].shape[1]
        return pl.ds(pl.multiple_of(info_ref[1 + index], 64), count)

    @pl.when(step == 0)
    def _():
        filled = sum(ref.shape[1] for ref in piece_refs)
        if filled < kv.shape[0]:
            kv[filled:] = jnp.zeros((kv.shape[0] - filled, 2 * HD), bf16)
        for index in range(pieces):
            kv[piece_rows(index), :HD] = piece_refs[index][0]
            kv[piece_rows(index), HD:] = piece_refs[index][1]
        for which, ref in enumerate((dk_t, dv_t)):
            ref[...] = begun_refs[which][...] if begun else jnp.zeros(ref.shape, f32)

    for which in range(steps):

        @pl.when(step == which)
        def _():
            for a in range(groups):
                ref = qg_refs[which * groups + a]
                for h in range(heads):
                    part = slice(h * size + a * run, h * size + (a + 1) * run)
                    q_rows[part] = ref[:, h * HD : (h + 1) * HD]
                    g_rows[part] = ref[:, columns + h * HD : columns + (h + 1) * HD]

    peak[...] = jnp.full(peak.shape, NEG, f32)
    total[...] = jnp.zeros(total.shape, f32)
    out_sum[...] = jnp.zeros(out_sum.shape, f32)
    dq_sum[...] = jnp.zeros(dq_sum.shape, f32)

    distance = distances[0]
    for which in range(1, steps):
        distance = jnp.where(step == which, distances[which], distance)
    q_first = (ctx ^ distance) * size
    low_first = record_start(q_first)
    low_last = record_start(q_first + (size - 1))
    token = lax.broadcasted_iota(jnp.int32, (size, HD), 0)
    pos = q_first + own * run + token
    for a in range(1, groups):
        pos = jnp.where(token >= a * run, q_first + (own ^ a) * run + (token - a * run), pos)
    last_key[...] = pos
    first_key[...] = record_start(pos)
    first = (low_first - origin) // KB
    last = (q_first + (size - 1) - origin) // KB + 1

    def by_rows(left, right):
        return lax.dot_general(
            left, right, (((1,), (1,)), ((), ())), preferred_element_type=f32
        )

    def score_pass(b, carry):
        base = origin + b * KB
        whole = (base + (KB - 1) <= q_first) & (base >= low_last)

        @pl.when(whole)
        def _():
            for part in chunks:
                s = by_rows(q_rows[part], kv[rows_of(b), :HD])
                scores[b - first, part] = s
                peak[part] = jnp.maximum(peak[part], jnp.maximum(s[:, :HD], s[:, HD:]))

        @pl.when(jnp.logical_not(whole))
        def _():
            key_pos = base + lax.broadcasted_iota(jnp.int32, (size, HD), 1)
            for h in range(heads):
                part = slice(h * size, (h + 1) * size)
                s = by_rows(q_rows[part], kv[rows_of(b), :HD])
                for lane in (0, HD):
                    key = key_pos + lane
                    allowed = (key <= last_key[...]) & (key >= first_key[...])
                    side = jnp.where(allowed, s[:, lane : lane + HD], NEG)
                    scores[b - first, part, lane : lane + HD] = side
                    peak[part] = jnp.maximum(peak[part], side)

        return carry

    lax.fori_loop(first, last, score_pass, 0)
    for part in chunks:
        highest = jnp.max(peak[part], axis=1, keepdims=True) * TO_EXP2
        peak[part] = jnp.broadcast_to(highest, peak[part].shape)

    def weight_pass(b, carry):
        for part in chunks:
            left = jnp.exp2(scores[b - first, part, :HD] * TO_EXP2 - peak[part])
            right = jnp.exp2(scores[b - first, part, HD:] * TO_EXP2 - peak[part])
            total[part] += left + right
            w = jnp.concatenate([left, right], axis=1).astype(bf16)
            weights[b - first, part] = w
            out_sum[part] += jnp.dot(w, kv[rows_of(b), HD:], preferred_element_type=f32)
        return carry

    lax.fori_loop(first, last, weight_pass, 0)

    def give(values, first_column):
        for which in range(steps):

            @pl.when(step == which)
            def _():
                for a in range(groups):
                    to = pl.ds(pl.multiple_of((own ^ a) * run, 16), run)
                    for h in range(heads):
                        start = h * size + a * run
                        column = first_column + h * HD
                        out_refs[which][to, column : column + HD] = values[start : start + run, :HD]

    for part in chunks:
        inverse = 1.0 / jnp.sum(total[part], axis=1, keepdims=True)
        out = (out_sum[part] * inverse).astype(bf16)
        dscores[part, :HD] = out
        g_wide = g_rows[part].astype(f32)
        inner = jnp.sum(g_wide * out.astype(f32), axis=1, keepdims=True) * inverse
        delta[part] = jnp.broadcast_to(inner, delta[part].shape)
        g_rows[part] = (g_wide * inverse).astype(bf16)
    give(dscores, 0)
    q_t[...] = q_rows[...].T
    g_t[...] = g_rows[...].T

    def grad_pass(b, carry):
        for part in chunks:
            dp = by_rows(g_rows[part], kv[rows_of(b), HD:])
            w = weights[b - first, part].astype(f32)
            left = w[:, :HD] * (dp[:, :HD] - delta[part])
            right = w[:, HD:] * (dp[:, HD:] - delta[part])
            ds = jnp.concatenate([left, right], axis=1).astype(bf16)
            dscores[part] = ds
            dq_sum[part] += jnp.dot(ds, kv[rows_of(b), :HD], preferred_element_type=f32)
        dv_t[b] += jnp.dot(g_t[...], weights[b - first], preferred_element_type=f32)
        dk_t[b] += jnp.dot(q_t[...], dscores[...], preferred_element_type=f32)
        return carry

    lax.fori_loop(first, last, grad_pass, 0)
    for part in chunks:
        dscores[part, :HD] = (dq_sum[part] * SCALE).astype(bf16)
    give(dscores, heads * HD)

    @pl.when(step == steps - 1)
    def _():
        if not ended:
            term_refs[0][...] = dk_t[...]
            term_refs[1][...] = dv_t[...]
            return

        def turn(b, carry):
            kv[rows_of(b), :HD] = (dk_t[b] * SCALE).T.astype(bf16)
            kv[rows_of(b), HD:] = dv_t[b].T.astype(bf16)
            return carry

        lax.fori_loop(0, blocks, turn, 0)
        for index in range(pieces):
            term_refs[index][0] = kv[piece_rows(index), :HD]
            term_refs[index][1] = kv[piece_rows(index), HD:]


def attention(qg_pieces, kv_pieces, info, lengths, distances, most, begun, ended):
    run, columns = qg_pieces[0].shape
    steps = len(distances)
    groups = len(qg_pieces) // steps
    size = groups * run
    heads = columns // (2 * HD)
    rows = size * heads
    pieces = len(kv_pieces)
    keys = -(-sum(part.shape[1] for part in kv_pieces) // KB) * KB
    blocks = keys // KB
    live = min(blocks, (most + size - 3) // KB + 2)
    bf16 = jnp.bfloat16
    f32 = jnp.float32

    def still(shape):
        return pl.BlockSpec(
            shape, lambda i, *_: (0,) * len(shape), pipeline_mode=pl.Buffered(1)
        )

    def kept(shape):
        return pl.BlockSpec(shape, lambda i, *_: (0,) * len(shape))

    shapes = [part.shape for part in kv_pieces]
    sums = [(blocks, HD, KB)] * 2
    given = (size, columns)
    pairs = size * steps * heads * keys
    results = pl.pallas_call(
        functools.partial(attention_kernel, pieces, distances, groups, len(begun) // 2, ended),
        grid_spec=pltpu.PrefetchScalarGridSpec(
            num_scalar_prefetch=2,
            grid=(steps,),
            in_specs=[still((run, columns))] * len(qg_pieces)
            + [still(shape) for shape in shapes]
            + [still(shape) for shape in (sums if begun else [])],
            out_specs=[kept(given)] * steps
            + [kept(shape) for shape in (shapes if ended else sums)],
            scratch_shapes=[
                pltpu.VMEM((keys, 2 * HD), bf16),
                pltpu.VMEM((blocks, HD, KB), f32),
                pltpu.VMEM((blocks, HD, KB), f32),
                pltpu.VMEM((live, rows, KB), f32),
                pltpu.VMEM((live, rows, KB), bf16),
                pltpu.VMEM((rows, KB), bf16),
                pltpu.VMEM((rows, HD), bf16),
                pltpu.VMEM((rows, HD), bf16),
                pltpu.VMEM((HD, rows), bf16),
                pltpu.VMEM((HD, rows), bf16),
                pltpu.VMEM((rows, HD), f32),
                pltpu.VMEM((rows, HD), f32),
                pltpu.VMEM((rows, HD), f32),
                pltpu.VMEM((rows, HD), f32),
                pltpu.VMEM((rows, HD), f32),
                pltpu.VMEM((size, HD), jnp.int32),
                pltpu.VMEM((size, HD), jnp.int32),
            ],
        ),
        out_shape=[jax.ShapeDtypeStruct(given, bf16)] * steps
        + (
            [jax.ShapeDtypeStruct(shape, bf16) for shape in shapes]
            if ended
            else [jax.ShapeDtypeStruct(shape, f32) for shape in sums]
        ),
        compiler_params=pltpu.CompilerParams(vmem_limit_bytes=VMEM_ATTENTION),
        cost_estimate=pl.CostEstimate(
            flops=48 * HD * pairs, bytes_accessed=32 * rows * HD * steps, transcendentals=pairs
        ),
        name="attention",
    )(info, lengths, *qg_pieces, *kv_pieces, *begun)
    return results[:steps], list(results[steps:])


def settle_kernel(split, *refs):
    piece_refs, (out_ref, dq_ref) = refs[:split], refs[split:]
    width = piece_refs[0].shape[1] // 2
    core = lax.axis_index("ctx") % split
    for distance in range(split):
        to = pl.ds(pl.multiple_of((core ^ distance) * width, HD), width)
        out_ref[:, to] = piece_refs[distance][:, :width]
        dq_ref[:, to] = piece_refs[distance][:, width:]


def settle(parts):
    split = len(parts)
    rows, width = parts[0].shape
    shape = jax.ShapeDtypeStruct((rows, width * split // 2), parts[0].dtype)
    return pl.pallas_call(
        functools.partial(settle_kernel, split),
        out_shape=[shape] * 2,
        compiler_params=pltpu.CompilerParams(vmem_limit_bytes=VMEM),
        name="settle",
    )(*parts)


def body(
    record_lengths,
    query_heads,
    key_heads,
    value_heads,
    out_grad,
    gate_input,
    key_input,
    value_input,
    hyena_grad,
    short_filter,
    long_filter,
):
    ctx = lax.axis_size("ctx")
    tp = lax.axis_size("tp")
    own_ctx = lax.axis_index("ctx")
    piece = query_heads.shape[0]
    tokens = piece * tp
    window = tokens * ctx
    most = window // 2 + 192
    split = PLANE if (KVH // tp) % PLANE == 0 else 1
    slots = tp * split
    kv_local = KVH // slots
    assert kv_local == 1 and tokens % 192 == 0
    unit = tokens * split
    lanes = PLANE // split
    plane = unit * lanes
    reach = (most - 1) // plane
    tail = -(-(most - 1 - reach * plane) // 192) * 192
    core = own_ctx % split
    lane = own_ctx // split % lanes
    level = own_ctx // PLANE
    f32 = jnp.float32
    bf16 = jnp.bfloat16

    members = [
        [t * ctx + n * split + c for t in range(tp) for c in range(split)]
        for n in range(ctx // split)
    ]

    def share(laid):
        return lax.all_to_all(
            laid, ("tp", "ctx"), 0, 0, axis_index_groups=members, tiled=True
        )

    permute = functools.partial(lax.ppermute, axis_name="ctx")

    def across(values, distance):
        return permute(values, perm=[(i, i ^ (distance * split)) for i in range(ctx)])

    def up(values):
        return permute(values, perm=[(i, i + PLANE) for i in range(ctx - PLANE)])

    def down(values):
        return permute(values, perm=[(i + PLANE, i) for i in range(ctx - PLANE)])

    def swap(values, distance):
        return permute(values, perm=[(i, i ^ distance) for i in range(ctx)])

    far = (reach + 1) * PLANE - (lanes - 1) * split
    far_pairs = [
        (i, i + far) for i in range(ctx - far) if i // split % lanes == lanes - 1
    ]

    streams = (gate_input, key_input, value_input, hyena_grad)
    laid_kv, heads, tails = pack_edges(key_heads, value_heads, streams, slots)
    before = permute(tails, perm=[(i, i + 1) for i in range(ctx - 1)])
    after = permute(heads, perm=[(i + 1, i) for i in range(ctx - 1)])

    kv = share(laid_kv)
    if piece % 32:
        cut = [part.reshape(piece, slots, -1) for part in (query_heads, out_grad)]
        laid = jnp.concatenate(cut, axis=2).transpose(1, 0, 2)
        qg = share(laid).reshape(tp, split, piece, -1).transpose(1, 0, 2, 3)
        qg = list(qg.reshape(split, tokens, -1))
    else:
        laid_kv, query_heads = lax.optimization_barrier((laid_kv, query_heads))
        qg = list(pack_rows(query_heads, out_grad, slots, split))

    def exchange(which):
        for distance in which:
            far_t, far_c = distance // split, distance % split
            perm = [
                (i * tp + t, (i ^ far_c) * tp + (t ^ far_t))
                for t in range(tp)
                for i in range(ctx)
            ]
            qg[distance] = lax.ppermute(qg[distance], ("ctx", "tp"), perm)

    calls = [(split - 1, 0), (split // 2, split // 2 - 1)] if split > 1 else [(0,)]

    def rows_for(call):
        return [a * split + c for c in calls[call] for a in range(tp)]

    if piece % 32 == 0:
        first = [d for d in rows_for(0) if d]
    own_kv = kv.reshape(tp, split, 2, piece, kv_local * HD)
    own_kv = own_kv.transpose(2, 1, 0, 3, 4).reshape(2, unit, kv_local * HD)

    filters = (short_filter, long_filter)
    columns = [own_kv]
    if piece % 32 == 0:
        own_kv, *held = lax.optimization_barrier((own_kv,) + tuple(qg[d] for d in first))
        columns = [own_kv]
        for distance, value in zip(first, held):
            qg[distance] = value
        exchange(first)
    for hop in range(reach):
        coming = up(columns[-1])
        if hop == reach - 1:
            before, columns[-1] = lax.optimization_barrier((before, columns[-1]))
            hyena_outs = hyena(streams, before, after, *filters, 0, 2)
            coming, first_out = lax.optimization_barrier((coming, hyena_outs[0]))
            hyena_outs = [first_out] + list(hyena_outs[1:])
        columns.append(coming)
    tail_kv = permute(own_kv[:, unit - tail :], perm=far_pairs)
    pieces = [tail_kv]
    places = [jnp.int32(0)]
    for back in range(reach + 1):
        for distance in range(lanes):
            held = columns[back]
            pieces.append(held if distance == 0 else across(held, distance))
            places.append(tail + (reach - back) * plane + (lane ^ distance) * unit)
    origin = (level - reach) * plane - tail
    info = jnp.stack([origin] + places).astype(jnp.int32)

    owners = [None] * split
    terms = ()
    arrived = None
    for call, distances in enumerate(calls):
        if call:
            exchange(rows_for(call))
        held = [qg[d] for d in rows_for(call)] if piece % 32 == 0 else qg
        outs, terms = attention(held, pieces, info, record_lengths, distances, most, terms, call == len(calls) - 1)
        if arrived is not None:
            arrived, first_term = lax.optimization_barrier((arrived, terms[1 + reach * lanes]))
            terms[1 + reach * lanes] = first_term
            owners[calls[0][0]] = arrived
        for distance, value in zip(distances, outs):
            owners[distance] = swap(value, distance) if distance else value
        if call == 0 and split > 1:
            arrived = owners[distances[0]]
    attn_out, grad_query = settle(owners)

    def plane_sum(back):
        at = 1 + back * lanes
        total = terms[at].astype(f32)
        for distance in range(1, lanes):
            total = total + across(terms[at + distance], distance).astype(f32)
        return total

    tail_term = permute(terms[0], perm=[(j, i) for i, j in far_pairs])
    running = plane_sum(reach).astype(bf16)
    for back in range(reach - 1, -1, -1):
        coming = down(running)
        if back == reach - 1:
            before, running = lax.optimization_barrier((before, running))
            hyena_outs = hyena(streams, before, after, *filters, 1, 2, hyena_outs)
            coming, first_out = lax.optimization_barrier((coming, hyena_outs[0]))
            hyena_outs = [first_out] + list(hyena_outs[1:])
        running = plane_sum(back) + coming.astype(f32)
        if back:
            running = running.astype(bf16)
    running, attn_out = lax.optimization_barrier((running, attn_out))
    owned = jnp.concatenate(
        [running[:, : unit - tail], running[:, unit - tail :] + tail_term.astype(f32)], axis=1
    ).astype(bf16)

    parts = []
    for distance in range(split):
        held = lax.dynamic_slice_in_dim(owned, (core ^ distance) * tokens, tokens, 1)
        parts.append(swap(held, distance) if distance else held)
    bit = 1
    while bit < split:
        parts = [
            jnp.where(core & bit != 0, parts[index ^ bit], parts[index]) for index in range(split)
        ]
        bit = 2 * bit
    grads = jnp.concatenate(parts, axis=2)
    return (attn_out, grad_query, grads[0], grads[1]) + tuple(hyena_outs)


def solution(mesh):
    rows = P(("ctx", "tp"), None)
    both = P("ctx", "tp")
    return jax.shard_map(
        body,
        mesh=mesh,
        in_specs=(P(), rows, rows, rows, rows, both, both, both, both)
        + (P(None, None, "tp"), P(None, "tp")),
        out_specs=(both,) * 8,
        check_vma=False,
    )
```

```python
import functools

import jax
import jax.numpy as jnp
import numpy as np
from jax import lax
from jax.experimental import pallas as pl
from jax.experimental.pallas import tpu as pltpu
from jax.sharding import PartitionSpec as P

HD = 128
QH = 64
KVH = 8
GROUP = 16
TAPS = 7
SHORT = 3
HALO = 8
PLANE = 4
KB = 256
NEG = -1e30
SCALE = HD ** (-0.5)
TO_EXP2 = SCALE * 1.4426950408889634
CHUNK = 256
VMEM = 48 * 1024 * 1024
VMEM_ATTENTION = 58 * 1024 * 1024
VMEM_PACK = 62 * 1024 * 1024


def hyena_kernel(
    part,
    gate_ref,
    key_ref,
    value_ref,
    grad_ref,
    inner_ref,
    outer_ref,
    short_ref,
    long_ref,
    *refs,
):
    out_ref, dgate_ref, dkey_ref, dvalue_ref, taps = refs[-5:]
    tokens, width = gate_ref.shape
    own = pl.program_id(0)
    odd = lax.axis_index("ctx") % 2

    @pl.when(own == 0)
    def _():
        shape = (long_ref.shape[1], taps.shape[1])
        group = lax.broadcasted_iota(jnp.int32, shape, 0)
        channel = part * taps.shape[1] + lax.broadcasted_iota(jnp.int32, shape, 1)
        taps[...] = jnp.dot(
            long_ref[...],
            (group == channel // GROUP).astype(jnp.float32),
            precision=lax.Precision.HIGHEST,
            preferred_element_type=jnp.float32,
        )

    rows = tokens + 2 * HALO

    def chunk(index, carry):
        lanes = pl.ds(pl.multiple_of(index * HD, HD), HD)
        inner = inner_ref[:, lanes].astype(jnp.float32)
        outer = outer_ref[:, lanes].astype(jnp.float32)
        before = jnp.where(odd == 1, inner, outer)
        after = jnp.where(odd == 1, outer, inner)

        def padded(ref, which):
            part = slice(which * HALO, (which + 1) * HALO)
            return jnp.concatenate(
                [before[part], ref[:, lanes].astype(jnp.float32), after[part]], axis=0
            )

        def earlier(values, amount):
            return pltpu.roll(values, amount, 0) if amount else values

        def later(values, amount):
            return pltpu.roll(values, rows - amount, 0) if amount else values

        long = taps[:, pl.ds(pl.multiple_of(own * width + index * HD, HD), HD)]

        def short(which, tap):
            return short_ref[which, tap : tap + 1, lanes]

        def featurize(values, which):
            result = short(which, 0) * values
            for tap in range(1, SHORT):
                result = result + short(which, tap) * earlier(values, tap)
            return result

        def unfeaturize(grads, which):
            result = short(which, 0) * grads
            for tap in range(1, SHORT):
                result = result + short(which, tap) * later(grads, tap)
            return result[HALO : HALO + tokens].astype(jnp.bfloat16)

        key_f = featurize(padded(key_ref, 1), 1)
        value_f = featurize(padded(value_ref, 2), 2)
        mixed = key_f * value_f
        conv = long[0:1] * mixed
        for tap in range(1, TAPS):
            conv = conv + long[tap : tap + 1] * earlier(mixed, tap)
        gate_f = featurize(padded(gate_ref, 0), 0)
        out_ref[:, lanes] = (gate_f * conv)[HALO : HALO + tokens].astype(jnp.bfloat16)
        grad = padded(grad_ref, 3)
        dgate_ref[:, lanes] = unfeaturize(grad * conv, 0)
        dconv = grad * gate_f
        dmixed = long[0:1] * dconv
        for tap in range(1, TAPS):
            dmixed = dmixed + long[tap : tap + 1] * later(dconv, tap)
        dkey_ref[:, lanes] = unfeaturize(dmixed * value_f, 1)
        dvalue_ref[:, lanes] = unfeaturize(dmixed * key_f, 2)
        return carry

    lax.fori_loop(0, width // HD, chunk, 0)


def hyena(streams, inner, outer, short_filter, long_filter, part, parts, filled=()):
    tokens, channels = streams[0].shape
    own = channels // parts
    width = min(512, own)
    steps = own // width
    block = pl.BlockSpec((tokens, width), lambda i: (0, part * steps + i))
    edge = pl.BlockSpec((4 * HALO, width), lambda i: (0, part * steps + i))
    return pl.pallas_call(
        functools.partial(hyena_kernel, part),
        grid=(steps,),
        in_specs=[block] * 4
        + [edge, edge]
        + [
            pl.BlockSpec((3, SHORT, width), lambda i: (0, 0, part * steps + i)),
            pl.BlockSpec(long_filter.shape, lambda i: (0, 0)),
        ]
        + [pl.BlockSpec(memory_space=pl.ANY)] * len(filled),
        out_specs=[block] * 4,
        out_shape=[jax.ShapeDtypeStruct((tokens, channels), jnp.bfloat16)] * 4,
        scratch_shapes=[pltpu.VMEM((TAPS, own), jnp.float32)],
        input_output_aliases={8 + i: i for i in range(len(filled))},
        compiler_params=pltpu.CompilerParams(vmem_limit_bytes=VMEM),
        cost_estimate=pl.CostEstimate(
            flops=14000 * tokens * own, bytes_accessed=16 * tokens * own, transcendentals=0
        ),
        name="hyena",
    )(*streams, inner, outer, short_filter, long_filter, *filled)


def own_slot(split):
    return lax.axis_index("tp") * split + lax.axis_index("ctx") % split


def pack_edges_kernel(k_ref, v_ref, *refs):
    streams = (len(refs) - 3) // 2
    first_refs, last_refs = refs[:streams], refs[streams : 2 * streams]
    kv_ref, inner_ref, outer_ref = refs[2 * streams :]
    width = kv_ref.shape[3]
    for slot in range(kv_ref.shape[0]):
        part = slice(slot * width, (slot + 1) * width)
        kv_ref[slot, 0] = k_ref[:, part]
        kv_ref[slot, 1] = v_ref[:, part]
    f32 = jnp.float32
    odd = lax.axis_index("ctx") % 2

    def edge(refs, start, at):
        pair = [ref[...].astype(f32)[start : start + HALO] for ref in refs[at : at + 2]]
        return jnp.concatenate(pair, axis=0)

    for at in range(0, streams, 2):
        rows = slice(at * HALO, (at + 2) * HALO)
        head, tail = edge(first_refs, 0, at), edge(last_refs, HALO, at)
        inner_ref[rows] = jnp.where(odd == 1, head, tail).astype(inner_ref.dtype)
        outer_ref[rows] = jnp.where(odd == 1, tail, head).astype(outer_ref.dtype)


def pack_edges(keys, values, streams, slots):
    rows, columns = keys.shape
    tokens, channels = streams[0].shape
    edge = 2 * HALO
    count = len(streams)
    whole = pl.BlockSpec((rows, columns), lambda i: (0, 0))
    first = pl.BlockSpec((edge, channels), lambda i: (0, 0))
    last = pl.BlockSpec((edge, channels), lambda i: (tokens // edge - 1, 0))
    halo = (count * HALO, channels)
    laid = (slots, 2, rows, columns // slots)
    return pl.pallas_call(
        pack_edges_kernel,
        grid=(1,),
        in_specs=[whole] * 2 + [first] * count + [last] * count,
        out_specs=[
            pl.BlockSpec(laid, lambda i: (0, 0, 0, 0)),
            pl.BlockSpec(halo, lambda i: (0, 0)),
            pl.BlockSpec(halo, lambda i: (0, 0)),
        ],
        out_shape=[jax.ShapeDtypeStruct(shape, keys.dtype) for shape in (laid, halo, halo)],
        name="pack_edges",
    )(keys, values, *streams, *streams)


def pack_rows_kernel(split, q_ref, g_ref, *refs):
    outs, sems = refs[:-1], refs[-1]
    width = outs[0].shape[1] // 2
    slot = own_slot(split)
    copies = []
    for distance, out in enumerate(outs):
        part = pl.ds(pl.multiple_of((slot ^ distance) * width, HD), width)
        for ref, first in ((q_ref, 0), (g_ref, width)):
            copies.append(
                pltpu.make_async_copy(
                    ref.at[:, part], out.at[:, first : first + width], sems.at[len(copies)]
                )
            )
    for copy in copies:
        copy.start()
    for copy in copies:
        copy.wait()


def pack_rows(queries, grads, slots, split):
    rows, columns = queries.shape
    shape = jax.ShapeDtypeStruct((rows, 2 * columns // slots), queries.dtype)
    return pl.pallas_call(
        functools.partial(pack_rows_kernel, split),
        in_specs=[pl.BlockSpec(memory_space=pltpu.VMEM)] * 2,
        out_specs=[pl.BlockSpec(memory_space=pltpu.HBM)] * slots,
        out_shape=[shape] * slots,
        scratch_shapes=[pltpu.SemaphoreType.DMA((2 * slots,))],
        compiler_params=pltpu.CompilerParams(vmem_limit_bytes=VMEM_PACK),
        name="pack_rows",
    )(queries, grads)


def attention_kernel(pieces, distances, groups, begun, ended, *refs):
    (info_ref, lengths_ref), refs = refs[:2], refs[2:]
    steps = len(distances)
    qg_refs, refs = refs[: steps * groups], refs[steps * groups :]
    piece_refs, refs = refs[:pieces], refs[pieces:]
    begun_refs, refs = refs[: 2 * begun], refs[2 * begun :]
    out_refs, refs = refs[:steps], refs[steps:]
    count = pieces if ended else 2
    term_refs, refs = refs[:count], refs[count:]
    kv, k_t, v_t, dk_sum, dv_sum, scores, weights, dscores = refs[:8]
    q_rows, q_t, g_rows, g_t, peak8, total8, out_t, dq_t = refs[8:]
    step = pl.program_id(0)
    blocks = k_t.shape[0]
    run = qg_refs[0].shape[0]
    columns = qg_refs[0].shape[1] // 2
    heads = columns // HD
    size = groups * run
    rows = size * heads
    f32 = jnp.float32
    bf16 = jnp.bfloat16
    chunks = [slice(start, min(start + CHUNK, rows)) for start in range(0, rows, CHUNK)]
    ctx = lax.axis_index("ctx")
    own = lax.axis_index("tp") if groups > 1 else 0
    origin = info_ref[0]

    def record_start(position):
        ends = 0
        start = position * 0
        for record in range(lengths_ref.shape[0]):
            ends = ends + lengths_ref[record]
            start = jnp.where(position >= ends, ends, start)
        return start

    def rows_of(b):
        return pl.ds(pl.multiple_of(b * KB, KB), KB)

    def piece_rows(index):
        count = piece_refs[index].shape[1]
        return pl.ds(pl.multiple_of(info_ref[1 + index], 64), count)

    @pl.when(step == 0)
    def _():
        filled = sum(ref.shape[1] for ref in piece_refs)
        if filled < kv.shape[0]:
            kv[filled:] = jnp.zeros((kv.shape[0] - filled, 2 * HD), bf16)
        for index in range(pieces):
            kv[piece_rows(index), :HD] = piece_refs[index][0]
            kv[piece_rows(index), HD:] = piece_refs[index][1]
        for which, ref in enumerate((dk_sum, dv_sum)):
            ref[...] = begun_refs[which][...] if begun else jnp.zeros(ref.shape, f32)

        def prepare(b, carry):
            k_t[b] = kv[rows_of(b), :HD].T
            v_t[b] = kv[rows_of(b), HD:].T
            return carry

        lax.fori_loop(0, blocks, prepare, 0)

    for which in range(steps):

        @pl.when(step == which)
        def _():
            for a in range(groups):
                ref = qg_refs[which * groups + a]
                for h in range(heads):
                    part = slice(h * size + a * run, h * size + (a + 1) * run)
                    q_rows[part] = ref[:, h * HD : (h + 1) * HD]
                    g_rows[part] = ref[:, columns + h * HD : columns + (h + 1) * HD]

    q_t[...] = q_rows[...].T
    g_t[...] = g_rows[...].T
    peak8[...] = jnp.full((8, rows), NEG, f32)
    total8[...] = jnp.zeros((8, rows), f32)
    out_t[...] = jnp.zeros((HD, rows), f32)
    dq_t[...] = jnp.zeros((HD, rows), f32)

    distance = distances[0]
    for which in range(1, steps):
        distance = jnp.where(step == which, distances[which], distance)
    q_first = (ctx ^ distance) * size
    low_first = record_start(q_first)
    low_last = record_start(q_first + (size - 1))
    token = lax.broadcasted_iota(jnp.int32, (1, rows), 1) % size
    if groups > 1:
        token = ((token // run) ^ own) * run + token % run
    pos = q_first + token
    low = record_start(pos)
    first = (low_first - origin) // KB
    last = (q_first + (size - 1) - origin) // KB + 1

    def fold(values, combine):
        result = values[0:8]
        for start in range(8, values.shape[0], 8):
            result = combine(result, values[start : start + 8])
        return result

    def score_pass(b, carry):
        base = origin + b * KB
        whole = (base + (KB - 1) <= q_first) & (base >= low_last)

        @pl.when(whole)
        def _():
            for part in chunks:
                s = jnp.dot(kv[rows_of(b), :HD], q_t[:, part], preferred_element_type=f32)
                scores[b - first, :, part] = s
                peak8[:, part] = jnp.maximum(peak8[:, part], fold(s, jnp.maximum))

        @pl.when(jnp.logical_not(whole))
        def _():
            for part in chunks:
                s = jnp.dot(kv[rows_of(b), :HD], q_t[:, part], preferred_element_type=f32)
                key_pos = base + lax.broadcasted_iota(jnp.int32, s.shape, 0)
                allowed = (key_pos <= pos[:, part]) & (key_pos >= low[:, part])
                s = jnp.where(allowed, s, NEG)
                scores[b - first, :, part] = s
                peak8[:, part] = jnp.maximum(peak8[:, part], fold(s, jnp.maximum))

        return carry

    lax.fori_loop(first, last, score_pass, 0)
    peak = jnp.max(peak8[...], axis=0, keepdims=True) * TO_EXP2

    def weight_pass(b, carry):
        for part in chunks:
            w = jnp.exp2(scores[b - first, :, part] * TO_EXP2 - peak[:, part])
            total8[:, part] += fold(w, jnp.add)
            w_b = w.astype(bf16)
            weights[b - first, :, part] = w_b
            out_t[:, part] += jnp.dot(v_t[b], w_b, preferred_element_type=f32)
        return carry

    lax.fori_loop(first, last, weight_pass, 0)
    inverse = 1.0 / jnp.sum(total8[...], axis=0, keepdims=True)
    out_b = (out_t[...] * inverse).astype(bf16)
    g_wide = g_t[...].astype(f32)
    delta = jnp.sum(g_wide * out_b.astype(f32), axis=0, keepdims=True) * inverse
    g_scaled = (g_wide * inverse).astype(bf16)
    g_t[...] = g_scaled
    g_rows[...] = g_scaled.T

    def give(wide, first_column):
        for which in range(steps):

            @pl.when(step == which)
            def _():
                for a in range(groups):
                    to = pl.ds(pl.multiple_of((own ^ a) * run, 16), run)
                    for h in range(heads):
                        start = h * size + a * run
                        column = first_column + h * HD
                        out_refs[which][to, column : column + HD] = wide[start : start + run]

    give(out_b.T, 0)

    def grad_pass(b, carry):
        for part in chunks:
            dp = jnp.dot(kv[rows_of(b), HD:], g_t[:, part], preferred_element_type=f32)
            w = weights[b - first, :, part].astype(f32)
            dscores[:, part] = (w * (dp - delta[:, part])).astype(bf16)
        dv_sum[rows_of(b)] += jnp.dot(weights[b - first], g_rows[...], preferred_element_type=f32)
        dk_sum[rows_of(b)] += jnp.dot(dscores[...], q_rows[...], preferred_element_type=f32)
        dq_t[...] += jnp.dot(k_t[b], dscores[...], preferred_element_type=f32)
        return carry

    lax.fori_loop(first, last, grad_pass, 0)
    give((dq_t[...] * SCALE).astype(bf16).T, heads * HD)

    @pl.when(step == steps - 1)
    def _():
        if not ended:
            term_refs[0][...] = dk_sum[...]
            term_refs[1][...] = dv_sum[...]
            return
        for index in range(pieces):
            term_refs[index][0] = (dk_sum[piece_rows(index)] * SCALE).astype(bf16)
            term_refs[index][1] = dv_sum[piece_rows(index)].astype(bf16)


def attention(qg_pieces, kv_pieces, info, lengths, distances, most, begun, ended):
    run, columns = qg_pieces[0].shape
    steps = len(distances)
    groups = len(qg_pieces) // steps
    size = groups * run
    heads = columns // (2 * HD)
    rows = size * heads
    pieces = len(kv_pieces)
    keys = -(-sum(part.shape[1] for part in kv_pieces) // KB) * KB
    blocks = keys // KB
    live = min(blocks, (most + size - 3) // KB + 2)
    bf16 = jnp.bfloat16
    f32 = jnp.float32

    def still(shape):
        return pl.BlockSpec(
            shape, lambda i, *_: (0,) * len(shape), pipeline_mode=pl.Buffered(1)
        )

    def kept(shape):
        return pl.BlockSpec(shape, lambda i, *_: (0,) * len(shape))

    shapes = [part.shape for part in kv_pieces]
    sums = [(keys, HD)] * 2
    given = (size, columns)
    pairs = size * steps * heads * keys
    results = pl.pallas_call(
        functools.partial(attention_kernel, pieces, distances, groups, len(begun) // 2, ended),
        grid_spec=pltpu.PrefetchScalarGridSpec(
            num_scalar_prefetch=2,
            grid=(steps,),
            in_specs=[still((run, columns))] * len(qg_pieces)
            + [still(shape) for shape in shapes]
            + [still(shape) for shape in (sums if begun else [])],
            out_specs=[kept(given)] * steps
            + [kept(shape) for shape in (shapes if ended else sums)],
            scratch_shapes=[
                pltpu.VMEM((keys, 2 * HD), bf16),
                pltpu.VMEM((blocks, HD, KB), bf16),
                pltpu.VMEM((blocks, HD, KB), bf16),
                pltpu.VMEM((keys, HD), f32),
                pltpu.VMEM((keys, HD), f32),
                pltpu.VMEM((live, KB, rows), f32),
                pltpu.VMEM((live, KB, rows), bf16),
                pltpu.VMEM((KB, rows), bf16),
                pltpu.VMEM((rows, HD), bf16),
                pltpu.VMEM((HD, rows), bf16),
                pltpu.VMEM((rows, HD), bf16),
                pltpu.VMEM((HD, rows), bf16),
                pltpu.VMEM((8, rows), f32),
                pltpu.VMEM((8, rows), f32),
                pltpu.VMEM((HD, rows), f32),
                pltpu.VMEM((HD, rows), f32),
            ],
        ),
        out_shape=[jax.ShapeDtypeStruct(given, bf16)] * steps
        + (
            [jax.ShapeDtypeStruct(shape, bf16) for shape in shapes]
            if ended
            else [jax.ShapeDtypeStruct(shape, f32) for shape in sums]
        ),
        compiler_params=pltpu.CompilerParams(vmem_limit_bytes=VMEM_ATTENTION),
        cost_estimate=pl.CostEstimate(
            flops=48 * HD * pairs, bytes_accessed=32 * rows * HD * steps, transcendentals=pairs
        ),
        name="attention",
    )(info, lengths, *qg_pieces, *kv_pieces, *begun)
    return results[:steps], list(results[steps:])


def settle_kernel(split, *refs):
    piece_refs, (out_ref, dq_ref) = refs[:split], refs[split:]
    width = piece_refs[0].shape[1] // 2
    core = lax.axis_index("ctx") % split
    for distance in range(split):
        to = pl.ds(pl.multiple_of((core ^ distance) * width, HD), width)
        out_ref[:, to] = piece_refs[distance][:, :width]
        dq_ref[:, to] = piece_refs[distance][:, width:]


def settle(parts):
    split = len(parts)
    rows, width = parts[0].shape
    shape = jax.ShapeDtypeStruct((rows, width * split // 2), parts[0].dtype)
    return pl.pallas_call(
        functools.partial(settle_kernel, split),
        out_shape=[shape] * 2,
        compiler_params=pltpu.CompilerParams(vmem_limit_bytes=VMEM),
        name="settle",
    )(*parts)


def body(
    record_lengths,
    query_heads,
    key_heads,
    value_heads,
    out_grad,
    gate_input,
    key_input,
    value_input,
    hyena_grad,
    short_filter,
    long_filter,
):
    ctx = lax.axis_size("ctx")
    tp = lax.axis_size("tp")
    own_ctx = lax.axis_index("ctx")
    piece = query_heads.shape[0]
    tokens = piece * tp
    window = tokens * ctx
    most = window // 2 + 192
    split = PLANE if (KVH // tp) % PLANE == 0 else 1
    slots = tp * split
    kv_local = KVH // slots
    assert kv_local == 1 and tokens % 192 == 0
    unit = tokens * split
    lanes = PLANE // split
    plane = unit * lanes
    reach = (most - 1) // plane
    tail = -(-(most - 1 - reach * plane) // 192) * 192
    core = own_ctx % split
    lane = own_ctx // split % lanes
    level = own_ctx // PLANE
    f32 = jnp.float32
    bf16 = jnp.bfloat16

    members = [
        [t * ctx + n * split + c for t in range(tp) for c in range(split)]
        for n in range(ctx // split)
    ]

    def share(laid):
        return lax.all_to_all(
            laid, ("tp", "ctx"), 0, 0, axis_index_groups=members, tiled=True
        )

    permute = functools.partial(lax.ppermute, axis_name="ctx")

    def across(values, distance):
        return permute(values, perm=[(i, i ^ (distance * split)) for i in range(ctx)])

    def up(values):
        return permute(values, perm=[(i, i + PLANE) for i in range(ctx - PLANE)])

    def down(values):
        return permute(values, perm=[(i + PLANE, i) for i in range(ctx - PLANE)])

    def swap(values, distance):
        return permute(values, perm=[(i, i ^ distance) for i in range(ctx)])

    far = (reach + 1) * PLANE - (lanes - 1) * split
    far_pairs = [
        (i, i + far) for i in range(ctx - far) if i // split % lanes == lanes - 1
    ]

    streams = (gate_input, key_input, value_input, hyena_grad)
    laid_kv, inner, outer = pack_edges(key_heads, value_heads, streams, slots)
    inner = permute(inner, perm=[(i, i ^ 1) for i in range(ctx)])
    outer = permute(
        outer, perm=[(i, (i + 1 if i % 2 else i - 1)) for i in range(1, ctx - 1)]
    )

    kv = share(laid_kv)
    if piece % 32:
        cut = [part.reshape(piece, slots, -1) for part in (query_heads, out_grad)]
        laid = jnp.concatenate(cut, axis=2).transpose(1, 0, 2)
        qg = share(laid).reshape(tp, split, piece, -1).transpose(1, 0, 2, 3)
        qg = list(qg.reshape(split, tokens, -1))
    else:
        laid_kv, query_heads = lax.optimization_barrier((laid_kv, query_heads))
        qg = list(pack_rows(query_heads, out_grad, slots, split))

    def exchange(which):
        for distance in which:
            far_t, far_c = distance // split, distance % split
            perm = [
                (i * tp + t, (i ^ far_c) * tp + (t ^ far_t))
                for t in range(tp)
                for i in range(ctx)
            ]
            qg[distance] = lax.ppermute(qg[distance], ("ctx", "tp"), perm)

    calls = [(split - 1, 0), (split // 2, split // 2 - 1)] if split > 1 else [(0,)]

    def rows_for(call):
        return [a * split + c for c in calls[call] for a in range(tp)]

    if piece % 32 == 0:
        first = [d for d in rows_for(0) if d]
    kv, inner, outer, qg[0] = lax.optimization_barrier((kv, inner, outer, qg[0]))
    own_kv = kv.reshape(tp, split, 2, piece, kv_local * HD)
    own_kv = own_kv.transpose(2, 1, 0, 3, 4).reshape(2, unit, kv_local * HD)

    filters = (short_filter, long_filter)
    columns = [own_kv]
    if piece % 32 == 0:
        own_kv, *held = lax.optimization_barrier((own_kv,) + tuple(qg[d] for d in first))
        columns = [own_kv]
        for distance, value in zip(first, held):
            qg[distance] = value
        exchange(first)
    for hop in range(reach):
        coming = up(columns[-1])
        if hop == reach - 1:
            inner, columns[-1] = lax.optimization_barrier((inner, columns[-1]))
            hyena_outs = hyena(streams, inner, outer, *filters, 0, 2)
            coming, first_out = lax.optimization_barrier((coming, hyena_outs[0]))
            hyena_outs = [first_out] + list(hyena_outs[1:])
        columns.append(coming)
    tail_kv = own_kv[:, unit - tail :]
    tail_kv, columns[1] = lax.optimization_barrier((tail_kv, columns[1]))
    tail_kv = permute(tail_kv, perm=far_pairs)
    pieces = [tail_kv]
    places = [jnp.int32(0)]
    for back in range(reach + 1):
        for distance in range(lanes):
            held = columns[back]
            pieces.append(held if distance == 0 else across(held, distance))
            places.append(tail + (reach - back) * plane + (lane ^ distance) * unit)
    origin = (level - reach) * plane - tail
    info = jnp.stack([origin] + places).astype(jnp.int32)

    owners = [None] * split
    terms = ()
    arrived = None
    for call, distances in enumerate(calls):
        if call:
            exchange(rows_for(call))
        held = [qg[d] for d in rows_for(call)] if piece % 32 == 0 else qg
        outs, terms = attention(held, pieces, info, record_lengths, distances, most, terms, call == len(calls) - 1)
        if arrived is not None:
            at = 1 + reach * lanes
            arrived, terms[at] = lax.optimization_barrier((arrived, terms[at]))
            owners[calls[0][0]] = arrived
        for distance, value in zip(distances, outs):
            owners[distance] = swap(value, distance) if distance else value
        if call == 0 and split > 1:
            arrived = owners[distances[0]]
    attn_out, grad_query = settle(owners)

    def plane_sum(back):
        at = 1 + back * lanes
        total = terms[at].astype(f32)
        for distance in range(1, lanes):
            total = total + across(terms[at + distance], distance).astype(f32)
        return total

    tail_term = permute(terms[0], perm=[(j, i) for i, j in far_pairs])
    running = plane_sum(reach).astype(bf16)
    for back in range(reach - 1, -1, -1):
        coming = down(running)
        if back == reach - 1:
            inner, running = lax.optimization_barrier((inner, running))
            hyena_outs = hyena(streams, inner, outer, *filters, 1, 2, hyena_outs)
            coming, first_out = lax.optimization_barrier((coming, hyena_outs[0]))
            hyena_outs = [first_out] + list(hyena_outs[1:])
        running = plane_sum(back) + coming.astype(f32)
        if back:
            running = running.astype(bf16)
    running, attn_out = lax.optimization_barrier((running, attn_out))
    owned = jnp.concatenate(
        [running[:, : unit - tail], running[:, unit - tail :] + tail_term.astype(f32)], axis=1
    ).astype(bf16)

    parts = []
    for distance in range(split):
        held = lax.dynamic_slice_in_dim(owned, (core ^ distance) * tokens, tokens, 1)
        parts.append(swap(held, distance) if distance else held)
    bit = 1
    while bit < split:
        parts = [
            jnp.where(core & bit != 0, parts[index ^ bit], parts[index]) for index in range(split)
        ]
        bit = 2 * bit
    grads = jnp.concatenate(parts, axis=2)
    return (attn_out, grad_query, grads[0], grads[1]) + tuple(hyena_outs)


def solution(mesh):
    rows = P(("ctx", "tp"), None)
    both = P("ctx", "tp")
    return jax.shard_map(
        body,
        mesh=mesh,
        in_specs=(P(), rows, rows, rows, rows, both, both, both, both)
        + (P(None, None, "tp"), P(None, "tp")),
        out_specs=(both,) * 8,
        check_vma=False,
    )
```

```python
import functools

import jax
import jax.numpy as jnp
import numpy as np
from jax import lax
from jax.experimental import pallas as pl
from jax.experimental.pallas import tpu as pltpu
from jax.sharding import PartitionSpec as P

HD = 128
QH = 64
KVH = 8
GROUP = 16
TAPS = 7
SHORT = 3
HALO = 8
PLANE = 4
KB = 256
NEG = -1e30
SCALE = HD ** (-0.5)
TO_EXP2 = SCALE * 1.4426950408889634
VMEM = 48 * 1024 * 1024
VMEM_PACK = 62 * 1024 * 1024


def hyena_kernel(
    first,
    gate_ref,
    key_ref,
    value_ref,
    grad_ref,
    inner_ref,
    outer_ref,
    short_ref,
    long_ref,
    *refs,
):
    out_ref, dgate_ref, dkey_ref, dvalue_ref, taps = refs[-5:]
    tokens, width = gate_ref.shape
    own = pl.program_id(0)
    odd = lax.axis_index("ctx") % 2

    @pl.when(own == 0)
    def _():
        shape = (long_ref.shape[1], taps.shape[1])
        group = lax.broadcasted_iota(jnp.int32, shape, 0)
        channel = first + lax.broadcasted_iota(jnp.int32, shape, 1)
        taps[...] = jnp.dot(
            long_ref[...],
            (group == channel // GROUP).astype(jnp.float32),
            precision=lax.Precision.HIGHEST,
            preferred_element_type=jnp.float32,
        )

    rows = tokens + 2 * HALO

    def chunk(index, carry):
        lanes = pl.ds(pl.multiple_of(index * HD, HD), HD)
        inner = inner_ref[:, lanes].astype(jnp.float32)
        outer = outer_ref[:, lanes].astype(jnp.float32)
        before = jnp.where(odd == 1, inner, outer)
        after = jnp.where(odd == 1, outer, inner)

        def padded(ref, which):
            part = slice(which * HALO, (which + 1) * HALO)
            return jnp.concatenate(
                [before[part], ref[:, lanes].astype(jnp.float32), after[part]], axis=0
            )

        def earlier(values, amount):
            return pltpu.roll(values, amount, 0) if amount else values

        def later(values, amount):
            return pltpu.roll(values, rows - amount, 0) if amount else values

        long = taps[:, pl.ds(pl.multiple_of(own * width + index * HD, HD), HD)]

        def short(which, tap):
            return short_ref[which, tap : tap + 1, lanes]

        def featurize(values, which):
            result = short(which, 0) * values
            for tap in range(1, SHORT):
                result = result + short(which, tap) * earlier(values, tap)
            return result

        def unfeaturize(grads, which):
            result = short(which, 0) * grads
            for tap in range(1, SHORT):
                result = result + short(which, tap) * later(grads, tap)
            return result[HALO : HALO + tokens].astype(jnp.bfloat16)

        key_f = featurize(padded(key_ref, 1), 1)
        value_f = featurize(padded(value_ref, 2), 2)
        mixed = key_f * value_f
        conv = long[0:1] * mixed
        for tap in range(1, TAPS):
            conv = conv + long[tap : tap + 1] * earlier(mixed, tap)
        gate_f = featurize(padded(gate_ref, 0), 0)
        out_ref[:, lanes] = (gate_f * conv)[HALO : HALO + tokens].astype(jnp.bfloat16)
        grad = padded(grad_ref, 3)
        dgate_ref[:, lanes] = unfeaturize(grad * conv, 0)
        dconv = grad * gate_f
        dmixed = long[0:1] * dconv
        for tap in range(1, TAPS):
            dmixed = dmixed + long[tap : tap + 1] * later(dconv, tap)
        dkey_ref[:, lanes] = unfeaturize(dmixed * value_f, 1)
        dvalue_ref[:, lanes] = unfeaturize(dmixed * key_f, 2)
        return carry

    lax.fori_loop(0, width // HD, chunk, 0)


def hyena(streams, inner, outer, short_filter, long_filter, first, steps, filled=()):
    tokens, channels = streams[0].shape
    width = channels // 8
    own = steps * width
    block = pl.BlockSpec((tokens, width), lambda i: (0, first + i))
    edge = pl.BlockSpec((4 * HALO, width), lambda i: (0, first + i))
    return pl.pallas_call(
        functools.partial(hyena_kernel, first * width),
        grid=(steps,),
        in_specs=[block] * 4
        + [edge, edge]
        + [
            pl.BlockSpec((3, SHORT, width), lambda i: (0, 0, first + i)),
            pl.BlockSpec(long_filter.shape, lambda i: (0, 0)),
        ]
        + [pl.BlockSpec(memory_space=pl.ANY)] * len(filled),
        out_specs=[block] * 4,
        out_shape=[jax.ShapeDtypeStruct((tokens, channels), jnp.bfloat16)] * 4,
        scratch_shapes=[pltpu.VMEM((TAPS, own), jnp.float32)],
        input_output_aliases={8 + i: i for i in range(len(filled))},
        compiler_params=pltpu.CompilerParams(vmem_limit_bytes=VMEM),
        cost_estimate=pl.CostEstimate(
            flops=(14000 if filled else 28000) * tokens * own, bytes_accessed=16 * tokens * own, transcendentals=0
        ),
        name="hyena",
    )(*streams, inner, outer, short_filter, long_filter, *filled)


def own_slot(split):
    return lax.axis_index("tp") * split + lax.axis_index("ctx") % split


def pack_edges_kernel(k_ref, v_ref, *refs):
    streams = (len(refs) - 3) // 2
    first_refs, last_refs = refs[:streams], refs[streams : 2 * streams]
    kv_ref, inner_ref, outer_ref = refs[2 * streams :]
    width = kv_ref.shape[3]
    for slot in range(kv_ref.shape[0]):
        part = slice(slot * width, (slot + 1) * width)
        kv_ref[slot, 0] = k_ref[:, part]
        kv_ref[slot, 1] = v_ref[:, part]
    f32 = jnp.float32
    odd = lax.axis_index("ctx") % 2

    def edge(refs, start, at):
        pair = [ref[...].astype(f32)[start : start + HALO] for ref in refs[at : at + 2]]
        return jnp.concatenate(pair, axis=0)

    for at in range(0, streams, 2):
        rows = slice(at * HALO, (at + 2) * HALO)
        head, tail = edge(first_refs, 0, at), edge(last_refs, HALO, at)
        inner_ref[rows] = jnp.where(odd == 1, head, tail).astype(inner_ref.dtype)
        outer_ref[rows] = jnp.where(odd == 1, tail, head).astype(outer_ref.dtype)


def pack_edges(keys, values, streams, slots):
    rows, columns = keys.shape
    tokens, channels = streams[0].shape
    edge = 2 * HALO
    count = len(streams)
    whole = pl.BlockSpec((rows, columns), lambda i: (0, 0))
    first = pl.BlockSpec((edge, channels), lambda i: (0, 0))
    last = pl.BlockSpec((edge, channels), lambda i: (tokens // edge - 1, 0))
    halo = (count * HALO, channels)
    laid = (slots, 2, rows, columns // slots)
    return pl.pallas_call(
        pack_edges_kernel,
        grid=(1,),
        in_specs=[whole] * 2 + [first] * count + [last] * count,
        out_specs=[
            pl.BlockSpec(laid, lambda i: (0, 0, 0, 0)),
            pl.BlockSpec(halo, lambda i: (0, 0)),
            pl.BlockSpec(halo, lambda i: (0, 0)),
        ],
        out_shape=[jax.ShapeDtypeStruct(shape, keys.dtype) for shape in (laid, halo, halo)],
        name="pack_edges",
    )(keys, values, *streams, *streams)


def pack_rows_kernel(split, q_ref, g_ref, *refs):
    outs, sems = refs[:-1], refs[-1]
    width = outs[0].shape[1] // 2
    slot = own_slot(split)
    copies = []
    for distance, out in enumerate(outs):
        part = pl.ds(pl.multiple_of((slot ^ distance) * width, HD), width)
        for ref, first in ((q_ref, 0), (g_ref, width)):
            copies.append(
                pltpu.make_async_copy(
                    ref.at[:, part], out.at[:, first : first + width], sems.at[len(copies)]
                )
            )
    for copy in copies:
        copy.start()
    for copy in copies:
        copy.wait()


def pack_rows(queries, grads, slots, split):
    rows, columns = queries.shape
    shape = jax.ShapeDtypeStruct((rows, 2 * columns // slots), queries.dtype)
    return pl.pallas_call(
        functools.partial(pack_rows_kernel, split),
        in_specs=[pl.BlockSpec(memory_space=pltpu.VMEM)] * 2,
        out_specs=[pl.BlockSpec(memory_space=pltpu.HBM)] * slots,
        out_shape=[shape] * slots,
        scratch_shapes=[pltpu.SemaphoreType.DMA((2 * slots,))],
        compiler_params=pltpu.CompilerParams(vmem_limit_bytes=VMEM_PACK),
        name="pack_rows",
    )(queries, grads)


def attention_kernel(pieces, distances, groups, prior, *refs):
    (info_ref, lengths_ref), refs = refs[:2], refs[2:]
    steps = len(distances)
    qg_refs, refs = refs[: steps * groups], refs[steps * groups :]
    piece_refs, refs = refs[:pieces], refs[pieces:]
    prior_refs, refs = refs[: prior * pieces], refs[prior * pieces :]
    out_refs, refs = refs[:steps], refs[steps:]
    term_refs, refs = refs[:pieces], refs[pieces:]
    kv, k_t, v_t, dk_sum, dv_sum, scores, weights, dscores = refs[:8]
    q_rows, g_rows, peak8, total8, out_t, dq_t = refs[8:]
    step = pl.program_id(0)
    blocks = k_t.shape[0]
    run = qg_refs[0].shape[0]
    columns = qg_refs[0].shape[1] // 2
    heads = columns // HD
    size = groups * run
    rows = size * heads
    f32 = jnp.float32
    bf16 = jnp.bfloat16
    chunks = [slice(start, min(start + 256, rows)) for start in range(0, rows, 256)]
    ctx = lax.axis_index("ctx")
    own = lax.axis_index("tp") if groups > 1 else 0
    origin = info_ref[0]

    def record_start(position):
        ends = 0
        start = position * 0
        for record in range(lengths_ref.shape[0]):
            ends = ends + lengths_ref[record]
            start = jnp.where(position >= ends, ends, start)
        return start

    def rows_of(b):
        return pl.ds(pl.multiple_of(b * KB, KB), KB)

    def piece_rows(index):
        count = piece_refs[index].shape[1]
        return pl.ds(pl.multiple_of(info_ref[1 + index], 64), count)

    @pl.when(step == 0)
    def _():
        filled = sum(ref.shape[1] for ref in piece_refs)
        if filled < kv.shape[0]:
            kv[filled:] = jnp.zeros((kv.shape[0] - filled, 2 * HD), bf16)
        for index in range(pieces):
            kv[piece_rows(index), :HD] = piece_refs[index][0]
            kv[piece_rows(index), HD:] = piece_refs[index][1]
        dk_sum[...] = jnp.zeros(dk_sum.shape, f32)
        dv_sum[...] = jnp.zeros(dv_sum.shape, f32)

        def prepare(b, carry):
            k_t[b] = kv[rows_of(b), :HD].T
            v_t[b] = kv[rows_of(b), HD:].T
            return carry

        lax.fori_loop(0, blocks, prepare, 0)

    for which in range(steps):

        @pl.when(step == which)
        def _():
            for a in range(groups):
                ref = qg_refs[which * groups + a]
                for h in range(heads):
                    part = slice(h * size + a * run, h * size + (a + 1) * run)
                    q_rows[part] = ref[:, h * HD : (h + 1) * HD]
                    g_rows[part] = ref[:, columns + h * HD : columns + (h + 1) * HD]

    peak8[...] = jnp.full((8, rows), NEG, f32)
    total8[...] = jnp.zeros((8, rows), f32)
    out_t[...] = jnp.zeros((HD, rows), f32)
    dq_t[...] = jnp.zeros((HD, rows), f32)

    distance = distances[0]
    for which in range(1, steps):
        distance = jnp.where(step == which, distances[which], distance)
    q_first = (ctx ^ distance) * size
    low_first = record_start(q_first)
    low_last = record_start(q_first + (size - 1))
    token = lax.broadcasted_iota(jnp.int32, (1, rows), 1) % size
    if groups > 1:
        token = ((token // run) ^ own) * run + token % run
    pos = q_first + token
    low = record_start(pos)
    first = (low_first - origin) // KB
    last = (q_first + (size - 1) - origin) // KB + 1

    def by_rows(left, right):
        return lax.dot_general(
            left, right, (((1,), (1,)), ((), ())), preferred_element_type=f32
        )

    def fold(values, combine):
        result = values[0:8]
        for start in range(8, values.shape[0], 8):
            result = combine(result, values[start : start + 8])
        return result

    def score_pass(b, carry):
        base = origin + b * KB
        whole = (base + (KB - 1) <= q_first) & (base >= low_last)

        @pl.when(whole)
        def _():
            for part in chunks:
                s = by_rows(kv[rows_of(b), :HD], q_rows[part])
                scores[b - first, :, part] = s
                peak8[:, part] = jnp.maximum(peak8[:, part], fold(s, jnp.maximum))

        @pl.when(jnp.logical_not(whole))
        def _():
            for part in chunks:
                s = by_rows(kv[rows_of(b), :HD], q_rows[part])
                key_pos = base + lax.broadcasted_iota(jnp.int32, s.shape, 0)
                allowed = (key_pos <= pos[:, part]) & (key_pos >= low[:, part])
                s = jnp.where(allowed, s, NEG)
                scores[b - first, :, part] = s
                peak8[:, part] = jnp.maximum(peak8[:, part], fold(s, jnp.maximum))

        return carry

    lax.fori_loop(first, last, score_pass, 0)
    peak = jnp.max(peak8[...], axis=0, keepdims=True) * TO_EXP2

    def weight_pass(b, carry):
        for part in chunks:
            w = jnp.exp2(scores[b - first, :, part] * TO_EXP2 - peak[:, part])
            total8[:, part] += fold(w, jnp.add)
            w_b = w.astype(bf16)
            weights[b - first, :, part] = w_b
            out_t[:, part] += jnp.dot(v_t[b], w_b, preferred_element_type=f32)
        return carry

    lax.fori_loop(first, last, weight_pass, 0)
    inverse = 1.0 / jnp.sum(total8[...], axis=0, keepdims=True)
    out_b = (out_t[...] * inverse).astype(bf16)
    out_rows = out_b.T
    g_wide = g_rows[...].astype(f32)
    products = g_wide * out_rows.astype(f32)
    high = products.astype(bf16)
    rest = (products - high.astype(f32)).astype(bf16)
    ones = jnp.ones((8, HD), bf16)
    delta = (by_rows(ones, high) + by_rows(ones, rest))[0:1] * inverse
    g_rows[...] = (g_wide * jnp.broadcast_to(inverse, (8, rows)).T[:, 0:1]).astype(bf16)

    def give(wide, first):
        for which in range(steps):

            @pl.when(step == which)
            def _():
                for a in range(groups):
                    to = pl.ds(pl.multiple_of((own ^ a) * run, 16), run)
                    for h in range(heads):
                        start = h * size + a * run
                        out_refs[which][to, first + h * HD : first + (h + 1) * HD] = wide[
                            start : start + run
                        ]

    give(out_rows, 0)

    def grad_pass(b, carry):
        for part in chunks:
            dp = by_rows(kv[rows_of(b), HD:], g_rows[part])
            w = weights[b - first, :, part].astype(f32)
            dscores[:, part] = (w * (dp - delta[:, part])).astype(bf16)
        dv_sum[rows_of(b)] += jnp.dot(weights[b - first], g_rows[...], preferred_element_type=f32)
        dk_sum[rows_of(b)] += jnp.dot(dscores[...], q_rows[...], preferred_element_type=f32)
        dq_t[...] += jnp.dot(k_t[b], dscores[...], preferred_element_type=f32)
        return carry

    lax.fori_loop(first, last, grad_pass, 0)
    give((dq_t[...] * SCALE).astype(bf16).T, heads * HD)

    @pl.when(step == steps - 1)
    def _():
        for index in range(pieces):
            dk = dk_sum[piece_rows(index)] * SCALE
            dv = dv_sum[piece_rows(index)]
            if prior:
                dk = dk + prior_refs[index][0].astype(f32)
                dv = dv + prior_refs[index][1].astype(f32)
            term_refs[index][0] = dk.astype(bf16)
            term_refs[index][1] = dv.astype(bf16)


def attention(qg_pieces, kv_pieces, info, lengths, distances, most, prior=()):
    run, columns = qg_pieces[0].shape
    steps = len(distances)
    groups = len(qg_pieces) // steps
    size = groups * run
    heads = columns // (2 * HD)
    rows = size * heads
    pieces = len(kv_pieces)
    keys = -(-sum(part.shape[1] for part in kv_pieces) // KB) * KB
    blocks = keys // KB
    live = min(blocks, (most + size - 3) // KB + 2)
    bf16 = jnp.bfloat16
    f32 = jnp.float32

    def still(shape):
        return pl.BlockSpec(shape, lambda i, *_: (0,) * len(shape))

    kv_specs = [still(part.shape) for part in kv_pieces]
    given = (size, columns)
    pairs = size * steps * heads * keys
    results = pl.pallas_call(
        functools.partial(attention_kernel, pieces, distances, groups, 1 if prior else 0),
        grid_spec=pltpu.PrefetchScalarGridSpec(
            num_scalar_prefetch=2,
            grid=(steps,),
            in_specs=[still((run, columns))] * len(qg_pieces)
            + kv_specs
            + (kv_specs if prior else []),
            out_specs=[still(given)] * steps + kv_specs,
            scratch_shapes=[
                pltpu.VMEM((keys, 2 * HD), bf16),
                pltpu.VMEM((blocks, HD, KB), bf16),
                pltpu.VMEM((blocks, HD, KB), bf16),
                pltpu.VMEM((keys, HD), f32),
                pltpu.VMEM((keys, HD), f32),
                pltpu.VMEM((live, KB, rows), f32),
                pltpu.VMEM((live, KB, rows), bf16),
                pltpu.VMEM((KB, rows), bf16),
                pltpu.VMEM((rows, HD), bf16),
                pltpu.VMEM((rows, HD), bf16),
                pltpu.VMEM((8, rows), f32),
                pltpu.VMEM((8, rows), f32),
                pltpu.VMEM((HD, rows), f32),
                pltpu.VMEM((HD, rows), f32),
            ],
        ),
        out_shape=[jax.ShapeDtypeStruct(given, bf16)] * steps
        + [jax.ShapeDtypeStruct(part.shape, bf16) for part in kv_pieces],
        compiler_params=pltpu.CompilerParams(vmem_limit_bytes=VMEM),
        cost_estimate=pl.CostEstimate(
            flops=48 * HD * pairs, bytes_accessed=32 * rows * HD * steps, transcendentals=pairs
        ),
        name="attention",
    )(info, lengths, *qg_pieces, *kv_pieces, *prior)
    return results[:steps], results[steps:]


def settle_kernel(split, *refs):
    piece_refs, (out_ref, dq_ref) = refs[:split], refs[split:]
    width = piece_refs[0].shape[1] // 2
    core = lax.axis_index("ctx") % split
    for distance in range(split):
        to = pl.ds(pl.multiple_of((core ^ distance) * width, HD), width)
        out_ref[:, to] = piece_refs[distance][:, :width]
        dq_ref[:, to] = piece_refs[distance][:, width:]


def settle(parts):
    split = len(parts)
    rows, width = parts[0].shape
    shape = jax.ShapeDtypeStruct((rows, width * split // 2), parts[0].dtype)
    return pl.pallas_call(
        functools.partial(settle_kernel, split),
        out_shape=[shape] * 2,
        compiler_params=pltpu.CompilerParams(vmem_limit_bytes=VMEM),
        name="settle",
    )(*parts)


def body(
    record_lengths,
    query_heads,
    key_heads,
    value_heads,
    out_grad,
    gate_input,
    key_input,
    value_input,
    hyena_grad,
    short_filter,
    long_filter,
):
    ctx = lax.axis_size("ctx")
    tp = lax.axis_size("tp")
    own_ctx = lax.axis_index("ctx")
    piece = query_heads.shape[0]
    tokens = piece * tp
    window = tokens * ctx
    most = window // 2 + 192
    split = PLANE if (KVH // tp) % PLANE == 0 else 1
    slots = tp * split
    kv_local = KVH // slots
    assert kv_local == 1 and tokens % 192 == 0
    unit = tokens * split
    lanes = PLANE // split
    plane = unit * lanes
    reach = (most - 1) // plane
    tail = -(-(most - 1 - reach * plane) // 192) * 192
    core = own_ctx % split
    lane = own_ctx // split % lanes
    level = own_ctx // PLANE
    f32 = jnp.float32
    bf16 = jnp.bfloat16

    members = [
        [t * ctx + n * split + c for t in range(tp) for c in range(split)]
        for n in range(ctx // split)
    ]

    def share(laid):
        return lax.all_to_all(
            laid, ("tp", "ctx"), 0, 0, axis_index_groups=members, tiled=True
        )

    permute = functools.partial(lax.ppermute, axis_name="ctx")

    def across(values, distance):
        return permute(values, perm=[(i, i ^ (distance * split)) for i in range(ctx)])

    def up(values):
        return permute(values, perm=[(i, i + PLANE) for i in range(ctx - PLANE)])

    def down(values):
        return permute(values, perm=[(i + PLANE, i) for i in range(ctx - PLANE)])

    def swap(values, distance):
        return permute(values, perm=[(i, i ^ distance) for i in range(ctx)])

    far = (reach + 1) * PLANE - (lanes - 1) * split
    far_pairs = [
        (i, i + far) for i in range(ctx - far) if i // split % lanes == lanes - 1
    ]

    streams = (gate_input, key_input, value_input, hyena_grad)
    laid_kv, inner, outer = pack_edges(key_heads, value_heads, streams, slots)
    inner = permute(inner, perm=[(i, i ^ 1) for i in range(ctx)])
    outer = permute(
        outer, perm=[(i, (i + 1 if i % 2 else i - 1)) for i in range(1, ctx - 1)]
    )

    kv = share(laid_kv)
    if piece % 32:
        cut = [part.reshape(piece, slots, -1) for part in (query_heads, out_grad)]
        laid = jnp.concatenate(cut, axis=2).transpose(1, 0, 2)
        qg = share(laid).reshape(tp, split, piece, -1).transpose(1, 0, 2, 3)
        qg = list(qg.reshape(split, tokens, -1))
    else:
        laid_kv, query_heads = lax.optimization_barrier((laid_kv, query_heads))
        qg = list(pack_rows(query_heads, out_grad, slots, split))

    def exchange(which):
        for distance in which:
            far_t, far_c = distance // split, distance % split
            perm = [
                (i * tp + t, (i ^ far_c) * tp + (t ^ far_t))
                for t in range(tp)
                for i in range(ctx)
            ]
            qg[distance] = lax.ppermute(qg[distance], ("ctx", "tp"), perm)

    calls = [(split - 1, 0), (split // 2, split // 2 - 1)] if split > 1 else [(0,)]

    def rows_for(call):
        return [a * split + c for c in calls[call] for a in range(tp)]

    if piece % 32 == 0:
        first = [d for d in rows_for(0) if d]
    kv, inner, outer, qg[0] = lax.optimization_barrier((kv, inner, outer, qg[0]))
    own_kv = kv.reshape(tp, split, 2, piece, kv_local * HD)
    own_kv = own_kv.transpose(2, 1, 0, 3, 4).reshape(2, unit, kv_local * HD)

    filters = (short_filter, long_filter)
    columns = [own_kv]
    if piece % 32 == 0:
        own_kv, *held = lax.optimization_barrier((own_kv,) + tuple(qg[d] for d in first))
        columns = [own_kv]
        for distance, value in zip(first, held):
            qg[distance] = value
        exchange(first)
    for hop in range(reach):
        coming = up(columns[-1])
        if hop == reach - 1:
            inner, columns[-1] = lax.optimization_barrier((inner, columns[-1]))
            hyena_outs = hyena(streams, inner, outer, *filters, 0, 2)
            coming, first_out = lax.optimization_barrier((coming, hyena_outs[0]))
            hyena_outs = [first_out] + list(hyena_outs[1:])
        columns.append(coming)
    tail_kv = own_kv[:, unit - tail :]
    tail_kv, columns[1] = lax.optimization_barrier((tail_kv, columns[1]))
    tail_kv = permute(tail_kv, perm=far_pairs)
    pieces = [tail_kv]
    places = [jnp.int32(0)]
    for back in range(reach + 1):
        for distance in range(lanes):
            held = columns[back]
            pieces.append(held if distance == 0 else across(held, distance))
            places.append(tail + (reach - back) * plane + (lane ^ distance) * unit)
    origin = (level - reach) * plane - tail
    info = jnp.stack([origin] + places).astype(jnp.int32)

    owners = [None] * split
    terms = ()
    arrived = None
    for call, distances in enumerate(calls):
        if call:
            exchange(rows_for(call))
        held = [qg[d] for d in rows_for(call)] if piece % 32 == 0 else qg
        outs, terms = attention(held, pieces, info, record_lengths, distances, most, terms)
        if arrived is not None:
            at = 1 + reach * lanes
            terms = list(terms)
            arrived, terms[at] = lax.optimization_barrier((arrived, terms[at]))
            owners[calls[0][0]] = arrived
        for distance, value in zip(distances, outs):
            owners[distance] = swap(value, distance) if distance else value
        if call == 0 and split > 1:
            arrived = owners[distances[0]]
    attn_out, grad_query = settle(owners)

    def plane_sum(back):
        at = 1 + back * lanes
        total = terms[at].astype(f32)
        for distance in range(1, lanes):
            total = total + across(terms[at + distance], distance).astype(f32)
        return total

    tail_term = permute(terms[0], perm=[(j, i) for i, j in far_pairs])
    running = plane_sum(reach).astype(bf16)
    for back in range(reach - 1, -1, -1):
        coming = down(running)
        if back >= reach - 2:
            inner, running = lax.optimization_barrier((inner, running))
            share_of = (2, 4) if back == reach - 1 else (6, 2)
            hyena_outs = hyena(streams, inner, outer, *filters, *share_of, hyena_outs)
            coming, first_out = lax.optimization_barrier((coming, hyena_outs[0]))
            hyena_outs = [first_out] + list(hyena_outs[1:])
        running = plane_sum(back) + coming.astype(f32)
        if back:
            running = running.astype(bf16)
    running, attn_out = lax.optimization_barrier((running, attn_out))
    owned = jnp.concatenate(
        [running[:, : unit - tail], running[:, unit - tail :] + tail_term.astype(f32)], axis=1
    ).astype(bf16)

    parts = []
    for distance in range(split):
        held = lax.dynamic_slice_in_dim(owned, (core ^ distance) * tokens, tokens, 1)
        parts.append(swap(held, distance) if distance else held)
    bit = 1
    while bit < split:
        parts = [
            jnp.where(core & bit != 0, parts[index ^ bit], parts[index]) for index in range(split)
        ]
        bit = 2 * bit
    grads = jnp.concatenate(parts, axis=2)
    return (attn_out, grad_query, grads[0], grads[1]) + tuple(hyena_outs)


def solution(mesh):
    rows = P(("ctx", "tp"), None)
    both = P("ctx", "tp")
    return jax.shard_map(
        body,
        mesh=mesh,
        in_specs=(P(), rows, rows, rows, rows, both, both, both, both)
        + (P(None, None, "tp"), P(None, "tp")),
        out_specs=(both,) * 8,
        check_vma=False,
    )
```

```python
import functools

import jax
import jax.numpy as jnp
import numpy as np
from jax import lax
from jax.experimental import pallas as pl
from jax.experimental.pallas import tpu as pltpu
from jax.sharding import PartitionSpec as P

HD = 128
QH = 64
KVH = 8
GROUP = 16
TAPS = 7
SHORT = 3
HALO = 8
PLANE = 4
KB = 256
NEG = -1e30
SCALE = HD ** (-0.5)
TO_EXP2 = SCALE * 1.4426950408889634
VMEM = 48 * 1024 * 1024
VMEM_PACK = 62 * 1024 * 1024


def hyena_kernel(
    first,
    gate_ref,
    key_ref,
    value_ref,
    grad_ref,
    inner_ref,
    outer_ref,
    short_ref,
    long_ref,
    *refs,
):
    out_ref, dgate_ref, dkey_ref, dvalue_ref, taps, shift = refs[-6:]
    tokens, width = gate_ref.shape
    own = pl.program_id(0)
    odd = lax.axis_index("ctx") % 2

    @pl.when(own == 0)
    def _():
        shape = (long_ref.shape[1], taps.shape[1])
        group = lax.broadcasted_iota(jnp.int32, shape, 0)
        channel = first + lax.broadcasted_iota(jnp.int32, shape, 1)
        taps[...] = jnp.dot(
            long_ref[...],
            (group == channel // GROUP).astype(jnp.float32),
            precision=lax.Precision.HIGHEST,
            preferred_element_type=jnp.float32,
        )

    rows = tokens + 2 * HALO

    def chunk(index, carry):
        lanes = pl.ds(pl.multiple_of(index * HD, HD), HD)
        inner = inner_ref[:, lanes].astype(jnp.float32)
        outer = outer_ref[:, lanes].astype(jnp.float32)
        before = jnp.where(odd == 1, inner, outer)
        after = jnp.where(odd == 1, outer, inner)

        long = taps[:, pl.ds(pl.multiple_of(own * width + index * HD, HD), HD)]

        def short(which, tap):
            return short_ref[which, tap : tap + 1, lanes]

        def hold(slot, values, first=0):
            shift[slot, first + HALO : first + HALO + values.shape[0]] = values

        def at(slot, first, count):
            return shift[slot, first + HALO : first + HALO + count]

        def padded(ref, which):
            part = slice(which * HALO, (which + 1) * HALO)
            return jnp.concatenate(
                [before[part], ref[:, lanes].astype(jnp.float32), after[part]], axis=0
            )

        def featurize(ref, which):
            values = padded(ref, which)
            hold(which, values)
            result = short(which, 0) * values
            for tap in range(1, SHORT):
                result = result + short(which, tap) * at(which, -tap, rows)
            return result

        def unfeaturize(grads, which):
            hold(which, grads, HALO)
            result = short(which, 0) * grads[:tokens]
            for tap in range(1, SHORT):
                result = result + short(which, tap) * at(which, HALO + tap, tokens)
            return result.astype(jnp.bfloat16)

        count = tokens + HALO
        key_f = featurize(key_ref, 1)
        value_f = featurize(value_ref, 2)
        mixed = key_f * value_f
        hold(3, mixed)
        conv = long[0:1] * mixed[HALO:]
        for tap in range(1, TAPS):
            conv = conv + long[tap : tap + 1] * at(3, HALO - tap, count)
        gate_f = featurize(gate_ref, 0)[HALO:]
        out_ref[:, lanes] = (gate_f * conv)[:tokens].astype(jnp.bfloat16)
        grad = padded(grad_ref, 3)[HALO:]
        dgate_ref[:, lanes] = unfeaturize(grad * conv, 0)
        dconv = grad * gate_f
        hold(4, dconv, HALO)
        dmixed = long[0:1] * dconv
        for tap in range(1, TAPS):
            dmixed = dmixed + long[tap : tap + 1] * at(4, HALO + tap, count)
        dkey_ref[:, lanes] = unfeaturize(dmixed * value_f[HALO:], 1)
        dvalue_ref[:, lanes] = unfeaturize(dmixed * key_f[HALO:], 2)
        return carry

    lax.fori_loop(0, width // HD, chunk, 0)


def hyena(streams, inner, outer, short_filter, long_filter, first, steps, filled=()):
    tokens, channels = streams[0].shape
    width = channels // 8
    own = steps * width
    block = pl.BlockSpec((tokens, width), lambda i: (0, first + i))
    edge = pl.BlockSpec((4 * HALO, width), lambda i: (0, first + i))
    return pl.pallas_call(
        functools.partial(hyena_kernel, first * width),
        grid=(steps,),
        in_specs=[block] * 4
        + [edge, edge]
        + [
            pl.BlockSpec((3, SHORT, width), lambda i: (0, 0, first + i)),
            pl.BlockSpec(long_filter.shape, lambda i: (0, 0)),
        ]
        + [pl.BlockSpec(memory_space=pl.ANY)] * len(filled),
        out_specs=[block] * 4,
        out_shape=[jax.ShapeDtypeStruct((tokens, channels), jnp.bfloat16)] * 4,
        scratch_shapes=[
            pltpu.VMEM((TAPS, own), jnp.float32),
            pltpu.VMEM((5, tokens + 4 * HALO, HD), jnp.float32),
        ],
        input_output_aliases={8 + i: i for i in range(len(filled))},
        compiler_params=pltpu.CompilerParams(vmem_limit_bytes=VMEM),
        cost_estimate=pl.CostEstimate(
            flops=14000 * tokens * own, bytes_accessed=16 * tokens * own, transcendentals=0
        ),
        name="hyena",
    )(*streams, inner, outer, short_filter, long_filter, *filled)


def own_slot(split):
    return lax.axis_index("tp") * split + lax.axis_index("ctx") % split


def pack_edges_kernel(k_ref, v_ref, *refs):
    streams = (len(refs) - 3) // 2
    first_refs, last_refs = refs[:streams], refs[streams : 2 * streams]
    kv_ref, inner_ref, outer_ref = refs[2 * streams :]
    width = kv_ref.shape[3]
    for slot in range(kv_ref.shape[0]):
        part = slice(slot * width, (slot + 1) * width)
        kv_ref[slot, 0] = k_ref[:, part]
        kv_ref[slot, 1] = v_ref[:, part]
    f32 = jnp.float32
    odd = lax.axis_index("ctx") % 2

    def edge(refs, start, at):
        pair = [ref[...].astype(f32)[start : start + HALO] for ref in refs[at : at + 2]]
        return jnp.concatenate(pair, axis=0)

    for at in range(0, streams, 2):
        rows = slice(at * HALO, (at + 2) * HALO)
        head, tail = edge(first_refs, 0, at), edge(last_refs, HALO, at)
        inner_ref[rows] = jnp.where(odd == 1, head, tail).astype(inner_ref.dtype)
        outer_ref[rows] = jnp.where(odd == 1, tail, head).astype(outer_ref.dtype)


def pack_edges(keys, values, streams, slots):
    rows, columns = keys.shape
    tokens, channels = streams[0].shape
    edge = 2 * HALO
    count = len(streams)
    whole = pl.BlockSpec((rows, columns), lambda i: (0, 0))
    first = pl.BlockSpec((edge, channels), lambda i: (0, 0))
    last = pl.BlockSpec((edge, channels), lambda i: (tokens // edge - 1, 0))
    halo = (count * HALO, channels)
    laid = (slots, 2, rows, columns // slots)
    return pl.pallas_call(
        pack_edges_kernel,
        grid=(1,),
        in_specs=[whole] * 2 + [first] * count + [last] * count,
        out_specs=[
            pl.BlockSpec(laid, lambda i: (0, 0, 0, 0)),
            pl.BlockSpec(halo, lambda i: (0, 0)),
            pl.BlockSpec(halo, lambda i: (0, 0)),
        ],
        out_shape=[jax.ShapeDtypeStruct(shape, keys.dtype) for shape in (laid, halo, halo)],
        name="pack_edges",
    )(keys, values, *streams, *streams)


def pack_rows_kernel(split, q_ref, g_ref, *refs):
    outs, sems = refs[:-1], refs[-1]
    width = outs[0].shape[1] // 2
    slot = own_slot(split)
    copies = []
    for distance, out in enumerate(outs):
        part = pl.ds(pl.multiple_of((slot ^ distance) * width, HD), width)
        for ref, first in ((q_ref, 0), (g_ref, width)):
            copies.append(
                pltpu.make_async_copy(
                    ref.at[:, part], out.at[:, first : first + width], sems.at[len(copies)]
                )
            )
    for copy in copies:
        copy.start()
    for copy in copies:
        copy.wait()


def pack_rows(queries, grads, slots, split):
    rows, columns = queries.shape
    shape = jax.ShapeDtypeStruct((rows, 2 * columns // slots), queries.dtype)
    return pl.pallas_call(
        functools.partial(pack_rows_kernel, split),
        in_specs=[pl.BlockSpec(memory_space=pltpu.VMEM)] * 2,
        out_specs=[pl.BlockSpec(memory_space=pltpu.HBM)] * slots,
        out_shape=[shape] * slots,
        scratch_shapes=[pltpu.SemaphoreType.DMA((2 * slots,))],
        compiler_params=pltpu.CompilerParams(vmem_limit_bytes=VMEM_PACK),
        name="pack_rows",
    )(queries, grads)


def attention_kernel(pieces, distances, groups, prior, *refs):
    (info_ref, lengths_ref), refs = refs[:2], refs[2:]
    steps = len(distances)
    qg_refs, refs = refs[: steps * groups], refs[steps * groups :]
    piece_refs, refs = refs[:pieces], refs[pieces:]
    prior_refs, refs = refs[: prior * pieces], refs[prior * pieces :]
    out_refs, refs = refs[:steps], refs[steps:]
    term_refs, refs = refs[:pieces], refs[pieces:]
    kv, k_t, v_t, dk_sum, dv_sum, scores, weights, dscores = refs[:8]
    q_rows, q_t, g_rows, g_t, peak8, total8, out_t, dq_t = refs[8:]
    step = pl.program_id(0)
    blocks = k_t.shape[0]
    run = qg_refs[0].shape[0]
    columns = qg_refs[0].shape[1] // 2
    heads = columns // HD
    size = groups * run
    rows = size * heads
    f32 = jnp.float32
    bf16 = jnp.bfloat16
    chunks = [slice(start, min(start + 256, rows)) for start in range(0, rows, 256)]
    ctx = lax.axis_index("ctx")
    own = lax.axis_index("tp") if groups > 1 else 0
    origin = info_ref[0]

    def record_start(position):
        ends = 0
        start = position * 0
        for record in range(lengths_ref.shape[0]):
            ends = ends + lengths_ref[record]
            start = jnp.where(position >= ends, ends, start)
        return start

    def rows_of(b):
        return pl.ds(pl.multiple_of(b * KB, KB), KB)

    def piece_rows(index):
        count = piece_refs[index].shape[1]
        return pl.ds(pl.multiple_of(info_ref[1 + index], 64), count)

    @pl.when(step == 0)
    def _():
        filled = sum(ref.shape[1] for ref in piece_refs)
        if filled < kv.shape[0]:
            kv[filled:] = jnp.zeros((kv.shape[0] - filled, 2 * HD), bf16)
        for index in range(pieces):
            kv[piece_rows(index), :HD] = piece_refs[index][0]
            kv[piece_rows(index), HD:] = piece_refs[index][1]
        dk_sum[...] = jnp.zeros(dk_sum.shape, f32)
        dv_sum[...] = jnp.zeros(dv_sum.shape, f32)

        def prepare(b, carry):
            k_t[b] = kv[rows_of(b), :HD].T
            v_t[b] = kv[rows_of(b), HD:].T
            return carry

        lax.fori_loop(0, blocks, prepare, 0)

    for which in range(steps):

        @pl.when(step == which)
        def _():
            for a in range(groups):
                ref = qg_refs[which * groups + a]
                for h in range(heads):
                    part = slice(h * size + a * run, h * size + (a + 1) * run)
                    q_rows[part] = ref[:, h * HD : (h + 1) * HD]
                    g_rows[part] = ref[:, columns + h * HD : columns + (h + 1) * HD]

    q_t[...] = q_rows[...].T
    g_t[...] = g_rows[...].T
    peak8[...] = jnp.full((8, rows), NEG, f32)
    total8[...] = jnp.zeros((8, rows), f32)
    out_t[...] = jnp.zeros((HD, rows), f32)
    dq_t[...] = jnp.zeros((HD, rows), f32)

    distance = distances[0]
    for which in range(1, steps):
        distance = jnp.where(step == which, distances[which], distance)
    q_first = (ctx ^ distance) * size
    low_first = record_start(q_first)
    low_last = record_start(q_first + (size - 1))
    token = lax.broadcasted_iota(jnp.int32, (1, rows), 1) % size
    if groups > 1:
        token = ((token // run) ^ own) * run + token % run
    pos = q_first + token
    low = record_start(pos)
    first = (low_first - origin) // KB
    last = (q_first + (size - 1) - origin) // KB + 1

    def fold(values, combine):
        result = values[0:8]
        for start in range(8, values.shape[0], 8):
            result = combine(result, values[start : start + 8])
        return result

    def score_pass(b, carry):
        base = origin + b * KB
        whole = (base + (KB - 1) <= q_first) & (base >= low_last)

        @pl.when(whole)
        def _():
            for part in chunks:
                s = jnp.dot(kv[rows_of(b), :HD], q_t[:, part], preferred_element_type=f32)
                scores[b - first, :, part] = s
                peak8[:, part] = jnp.maximum(peak8[:, part], fold(s, jnp.maximum))

        @pl.when(jnp.logical_not(whole))
        def _():
            for part in chunks:
                s = jnp.dot(kv[rows_of(b), :HD], q_t[:, part], preferred_element_type=f32)
                key_pos = base + lax.broadcasted_iota(jnp.int32, s.shape, 0)
                allowed = (key_pos <= pos[:, part]) & (key_pos >= low[:, part])
                s = jnp.where(allowed, s, NEG)
                scores[b - first, :, part] = s
                peak8[:, part] = jnp.maximum(peak8[:, part], fold(s, jnp.maximum))

        return carry

    lax.fori_loop(first, last, score_pass, 0)
    peak = jnp.max(peak8[...], axis=0, keepdims=True) * TO_EXP2

    def weight_pass(b, carry):
        for part in chunks:
            w = jnp.exp2(scores[b - first, :, part] * TO_EXP2 - peak[:, part])
            total8[:, part] += fold(w, jnp.add)
            w_b = w.astype(bf16)
            weights[b - first, :, part] = w_b
            out_t[:, part] += jnp.dot(v_t[b], w_b, preferred_element_type=f32)
        return carry

    lax.fori_loop(first, last, weight_pass, 0)
    inverse = 1.0 / jnp.sum(total8[...], axis=0, keepdims=True)
    out_b = (out_t[...] * inverse).astype(bf16)
    g_wide = g_t[...].astype(f32)
    delta = jnp.sum(g_wide * out_b.astype(f32), axis=0, keepdims=True) * inverse
    g_scaled = (g_wide * inverse).astype(bf16)
    g_t[...] = g_scaled
    g_rows[...] = g_scaled.T

    def give(wide, first):
        for which in range(steps):

            @pl.when(step == which)
            def _():
                for a in range(groups):
                    to = pl.ds(pl.multiple_of((own ^ a) * run, 16), run)
                    for h in range(heads):
                        start = h * size + a * run
                        out_refs[which][to, first + h * HD : first + (h + 1) * HD] = wide[
                            start : start + run
                        ]

    give(out_b.T, 0)

    def grad_pass(b, carry):
        for part in chunks:
            dp = jnp.dot(kv[rows_of(b), HD:], g_t[:, part], preferred_element_type=f32)
            w = weights[b - first, :, part].astype(f32)
            dscores[:, part] = (w * (dp - delta[:, part])).astype(bf16)
        dv_sum[rows_of(b)] += jnp.dot(weights[b - first], g_rows[...], preferred_element_type=f32)
        dk_sum[rows_of(b)] += jnp.dot(dscores[...], q_rows[...], preferred_element_type=f32)
        dq_t[...] += jnp.dot(k_t[b], dscores[...], preferred_element_type=f32)
        return carry

    lax.fori_loop(first, last, grad_pass, 0)
    give((dq_t[...] * SCALE).astype(bf16).T, heads * HD)

    @pl.when(step == steps - 1)
    def _():
        for index in range(pieces):
            dk = dk_sum[piece_rows(index)] * SCALE
            dv = dv_sum[piece_rows(index)]
            if prior:
                dk = dk + prior_refs[index][0].astype(f32)
                dv = dv + prior_refs[index][1].astype(f32)
            term_refs[index][0] = dk.astype(bf16)
            term_refs[index][1] = dv.astype(bf16)


def attention(qg_pieces, kv_pieces, info, lengths, distances, most, prior=()):
    run, columns = qg_pieces[0].shape
    steps = len(distances)
    groups = len(qg_pieces) // steps
    size = groups * run
    heads = columns // (2 * HD)
    rows = size * heads
    pieces = len(kv_pieces)
    keys = -(-sum(part.shape[1] for part in kv_pieces) // KB) * KB
    blocks = keys // KB
    live = min(blocks, (most + size - 3) // KB + 2)
    bf16 = jnp.bfloat16
    f32 = jnp.float32

    def still(shape):
        return pl.BlockSpec(shape, lambda i, *_: (0,) * len(shape))

    kv_specs = [still(part.shape) for part in kv_pieces]
    given = (size, columns)
    pairs = size * steps * heads * keys
    results = pl.pallas_call(
        functools.partial(attention_kernel, pieces, distances, groups, 1 if prior else 0),
        grid_spec=pltpu.PrefetchScalarGridSpec(
            num_scalar_prefetch=2,
            grid=(steps,),
            in_specs=[still((run, columns))] * len(qg_pieces)
            + kv_specs
            + (kv_specs if prior else []),
            out_specs=[still(given)] * steps + kv_specs,
            scratch_shapes=[
                pltpu.VMEM((keys, 2 * HD), bf16),
                pltpu.VMEM((blocks, HD, KB), bf16),
                pltpu.VMEM((blocks, HD, KB), bf16),
                pltpu.VMEM((keys, HD), f32),
                pltpu.VMEM((keys, HD), f32),
                pltpu.VMEM((live, KB, rows), f32),
                pltpu.VMEM((live, KB, rows), bf16),
                pltpu.VMEM((KB, rows), bf16),
                pltpu.VMEM((rows, HD), bf16),
                pltpu.VMEM((HD, rows), bf16),
                pltpu.VMEM((rows, HD), bf16),
                pltpu.VMEM((HD, rows), bf16),
                pltpu.VMEM((8, rows), f32),
                pltpu.VMEM((8, rows), f32),
                pltpu.VMEM((HD, rows), f32),
                pltpu.VMEM((HD, rows), f32),
            ],
        ),
        out_shape=[jax.ShapeDtypeStruct(given, bf16)] * steps
        + [jax.ShapeDtypeStruct(part.shape, bf16) for part in kv_pieces],
        compiler_params=pltpu.CompilerParams(vmem_limit_bytes=VMEM),
        cost_estimate=pl.CostEstimate(
            flops=48 * HD * pairs, bytes_accessed=32 * rows * HD * steps, transcendentals=pairs
        ),
        name="attention",
    )(info, lengths, *qg_pieces, *kv_pieces, *prior)
    return results[:steps], results[steps:]


def settle_kernel(split, *refs):
    piece_refs, (out_ref, dq_ref) = refs[:split], refs[split:]
    width = piece_refs[0].shape[1] // 2
    core = lax.axis_index("ctx") % split
    for distance in range(split):
        to = pl.ds(pl.multiple_of((core ^ distance) * width, HD), width)
        out_ref[:, to] = piece_refs[distance][:, :width]
        dq_ref[:, to] = piece_refs[distance][:, width:]


def settle(parts):
    split = len(parts)
    rows, width = parts[0].shape
    shape = jax.ShapeDtypeStruct((rows, width * split // 2), parts[0].dtype)
    return pl.pallas_call(
        functools.partial(settle_kernel, split),
        out_shape=[shape] * 2,
        compiler_params=pltpu.CompilerParams(vmem_limit_bytes=VMEM),
        name="settle",
    )(*parts)


def body(
    record_lengths,
    query_heads,
    key_heads,
    value_heads,
    out_grad,
    gate_input,
    key_input,
    value_input,
    hyena_grad,
    short_filter,
    long_filter,
):
    ctx = lax.axis_size("ctx")
    tp = lax.axis_size("tp")
    own_ctx = lax.axis_index("ctx")
    piece = query_heads.shape[0]
    tokens = piece * tp
    window = tokens * ctx
    most = window // 2 + 192
    split = PLANE if (KVH // tp) % PLANE == 0 else 1
    slots = tp * split
    kv_local = KVH // slots
    assert kv_local == 1 and tokens % 192 == 0
    unit = tokens * split
    lanes = PLANE // split
    plane = unit * lanes
    reach = (most - 1) // plane
    tail = -(-(most - 1 - reach * plane) // 192) * 192
    core = own_ctx % split
    lane = own_ctx // split % lanes
    level = own_ctx // PLANE
    f32 = jnp.float32
    bf16 = jnp.bfloat16

    members = [
        [t * ctx + n * split + c for t in range(tp) for c in range(split)]
        for n in range(ctx // split)
    ]

    def share(laid):
        return lax.all_to_all(
            laid, ("tp", "ctx"), 0, 0, axis_index_groups=members, tiled=True
        )

    permute = functools.partial(lax.ppermute, axis_name="ctx")

    def across(values, distance):
        return permute(values, perm=[(i, i ^ (distance * split)) for i in range(ctx)])

    def up(values):
        return permute(values, perm=[(i, i + PLANE) for i in range(ctx - PLANE)])

    def down(values):
        return permute(values, perm=[(i + PLANE, i) for i in range(ctx - PLANE)])

    def swap(values, distance):
        return permute(values, perm=[(i, i ^ distance) for i in range(ctx)])

    far = (reach + 1) * PLANE - (lanes - 1) * split
    far_pairs = [
        (i, i + far) for i in range(ctx - far) if i // split % lanes == lanes - 1
    ]

    streams = (gate_input, key_input, value_input, hyena_grad)
    laid_kv, inner, outer = pack_edges(key_heads, value_heads, streams, slots)
    inner = permute(inner, perm=[(i, i ^ 1) for i in range(ctx)])
    outer = permute(
        outer, perm=[(i, (i + 1 if i % 2 else i - 1)) for i in range(1, ctx - 1)]
    )

    kv = share(laid_kv)
    if piece % 32:
        cut = [part.reshape(piece, slots, -1) for part in (query_heads, out_grad)]
        laid = jnp.concatenate(cut, axis=2).transpose(1, 0, 2)
        qg = share(laid).reshape(tp, split, piece, -1).transpose(1, 0, 2, 3)
        qg = list(qg.reshape(split, tokens, -1))
    else:
        laid_kv, query_heads = lax.optimization_barrier((laid_kv, query_heads))
        qg = list(pack_rows(query_heads, out_grad, slots, split))

    def exchange(which):
        for distance in which:
            far_t, far_c = distance // split, distance % split
            perm = [
                (i * tp + t, (i ^ far_c) * tp + (t ^ far_t))
                for t in range(tp)
                for i in range(ctx)
            ]
            qg[distance] = lax.ppermute(qg[distance], ("ctx", "tp"), perm)

    calls = [(split - 1, 0), (split // 2, split // 2 - 1)] if split > 1 else [(0,)]

    def rows_for(call):
        return [a * split + c for c in calls[call] for a in range(tp)]

    if piece % 32 == 0:
        first = [d for d in rows_for(0) if d]
    kv, inner, outer, qg[0] = lax.optimization_barrier((kv, inner, outer, qg[0]))
    own_kv = kv.reshape(tp, split, 2, piece, kv_local * HD)
    own_kv = own_kv.transpose(2, 1, 0, 3, 4).reshape(2, unit, kv_local * HD)

    filters = (short_filter, long_filter)
    columns = [own_kv]
    if piece % 32 == 0:
        own_kv, *held = lax.optimization_barrier((own_kv,) + tuple(qg[d] for d in first))
        columns = [own_kv]
        for distance, value in zip(first, held):
            qg[distance] = value
        exchange(first)
    for hop in range(reach):
        coming = up(columns[-1])
        if hop == reach - 1:
            inner, columns[-1] = lax.optimization_barrier((inner, columns[-1]))
            hyena_outs = hyena(streams, inner, outer, *filters, 0, 4)
            coming, first_out = lax.optimization_barrier((coming, hyena_outs[0]))
            hyena_outs = [first_out] + list(hyena_outs[1:])
        columns.append(coming)
    tail_kv = own_kv[:, unit - tail :]
    tail_kv, columns[1] = lax.optimization_barrier((tail_kv, columns[1]))
    tail_kv = permute(tail_kv, perm=far_pairs)
    pieces = [tail_kv]
    places = [jnp.int32(0)]
    for back in range(reach + 1):
        for distance in range(lanes):
            held = columns[back]
            pieces.append(held if distance == 0 else across(held, distance))
            places.append(tail + (reach - back) * plane + (lane ^ distance) * unit)
    origin = (level - reach) * plane - tail
    info = jnp.stack([origin] + places).astype(jnp.int32)

    owners = [None] * split
    terms = ()
    arrived = None
    for call, distances in enumerate(calls):
        if call:
            exchange(rows_for(call))
        held = [qg[d] for d in rows_for(call)] if piece % 32 == 0 else qg
        outs, terms = attention(held, pieces, info, record_lengths, distances, most, terms)
        if arrived is not None:
            at = 1 + reach * lanes
            terms = list(terms)
            arrived, terms[at] = lax.optimization_barrier((arrived, terms[at]))
            owners[calls[0][0]] = arrived
        for distance, value in zip(distances, outs):
            owners[distance] = swap(value, distance) if distance else value
        if call == 0 and split > 1:
            arrived = owners[distances[0]]
    attn_out, grad_query = settle(owners)

    def plane_sum(back):
        at = 1 + back * lanes
        total = terms[at].astype(f32)
        for distance in range(1, lanes):
            total = total + across(terms[at + distance], distance).astype(f32)
        return total

    tail_term = permute(terms[0], perm=[(j, i) for i, j in far_pairs])
    running = plane_sum(reach).astype(bf16)
    for back in range(reach - 1, -1, -1):
        coming = down(running)
        if back == reach - 1:
            inner, running = lax.optimization_barrier((inner, running))
            hyena_outs = hyena(streams, inner, outer, *filters, 4, 4, hyena_outs)
            coming, first_out = lax.optimization_barrier((coming, hyena_outs[0]))
            hyena_outs = [first_out] + list(hyena_outs[1:])
        running = plane_sum(back) + coming.astype(f32)
        if back:
            running = running.astype(bf16)
    running, attn_out = lax.optimization_barrier((running, attn_out))
    owned = jnp.concatenate(
        [running[:, : unit - tail], running[:, unit - tail :] + tail_term.astype(f32)], axis=1
    ).astype(bf16)

    parts = []
    for distance in range(split):
        held = lax.dynamic_slice_in_dim(owned, (core ^ distance) * tokens, tokens, 1)
        parts.append(swap(held, distance) if distance else held)
    bit = 1
    while bit < split:
        parts = [
            jnp.where(core & bit != 0, parts[index ^ bit], parts[index]) for index in range(split)
        ]
        bit = 2 * bit
    grads = jnp.concatenate(parts, axis=2)
    return (attn_out, grad_query, grads[0], grads[1]) + tuple(hyena_outs)


def solution(mesh):
    rows = P(("ctx", "tp"), None)
    both = P("ctx", "tp")
    return jax.shard_map(
        body,
        mesh=mesh,
        in_specs=(P(), rows, rows, rows, rows, both, both, both, both)
        + (P(None, None, "tp"), P(None, "tp")),
        out_specs=(both,) * 8,
        check_vma=False,
    )
```

```python
import functools

import jax
import jax.numpy as jnp
import numpy as np
from jax import lax
from jax.experimental import pallas as pl
from jax.experimental.pallas import tpu as pltpu
from jax.sharding import PartitionSpec as P

HD = 128
QH = 64
KVH = 8
GROUP = 16
TAPS = 7
SHORT = 3
HALO = 8
PLANE = 4
KB = 256
NEG = -1e30
SCALE = HD ** (-0.5)
TO_EXP2 = SCALE * 1.4426950408889634
VMEM = 48 * 1024 * 1024
VMEM_PACK = 62 * 1024 * 1024


def hyena_kernel(
    first,
    gate_ref,
    key_ref,
    value_ref,
    grad_ref,
    inner_ref,
    outer_ref,
    short_ref,
    long_ref,
    *refs,
):
    out_ref, dgate_ref, dkey_ref, dvalue_ref, taps, shift = refs[-6:]
    tokens, width = gate_ref.shape
    own = pl.program_id(0)
    odd = lax.axis_index("ctx") % 2

    @pl.when(own == 0)
    def _():
        shape = (long_ref.shape[1], taps.shape[1])
        group = lax.broadcasted_iota(jnp.int32, shape, 0)
        channel = first + lax.broadcasted_iota(jnp.int32, shape, 1)
        taps[...] = jnp.dot(
            long_ref[...],
            (group == channel // GROUP).astype(jnp.float32),
            precision=lax.Precision.HIGHEST,
            preferred_element_type=jnp.float32,
        )

    rows = tokens + 2 * HALO

    def chunk(index, carry):
        lanes = pl.ds(pl.multiple_of(index * HD, HD), HD)
        inner = inner_ref[:, lanes].astype(jnp.float32)
        outer = outer_ref[:, lanes].astype(jnp.float32)
        before = jnp.where(odd == 1, inner, outer)
        after = jnp.where(odd == 1, outer, inner)

        long = taps[:, pl.ds(pl.multiple_of(own * width + index * HD, HD), HD)]

        def short(which, tap):
            return short_ref[which, tap : tap + 1, lanes]

        def hold(slot, values, first=0):
            shift[slot, first + HALO : first + HALO + values.shape[0]] = values

        def at(slot, first, count):
            return shift[slot, first + HALO : first + HALO + count]

        def padded(ref, which):
            part = slice(which * HALO, (which + 1) * HALO)
            return jnp.concatenate(
                [before[part], ref[:, lanes].astype(jnp.float32), after[part]], axis=0
            )

        def featurize(ref, which):
            values = padded(ref, which)
            hold(which, values)
            result = short(which, 0) * values
            for tap in range(1, SHORT):
                result = result + short(which, tap) * at(which, -tap, rows)
            return result

        def unfeaturize(grads, which):
            hold(which, grads, HALO)
            result = short(which, 0) * grads[:tokens]
            for tap in range(1, SHORT):
                result = result + short(which, tap) * at(which, HALO + tap, tokens)
            return result.astype(jnp.bfloat16)

        count = tokens + HALO
        key_f = featurize(key_ref, 1)
        value_f = featurize(value_ref, 2)
        mixed = key_f * value_f
        hold(3, mixed)
        conv = long[0:1] * mixed[HALO:]
        for tap in range(1, TAPS):
            conv = conv + long[tap : tap + 1] * at(3, HALO - tap, count)
        gate_f = featurize(gate_ref, 0)[HALO:]
        out_ref[:, lanes] = (gate_f * conv)[:tokens].astype(jnp.bfloat16)
        grad = padded(grad_ref, 3)[HALO:]
        dgate_ref[:, lanes] = unfeaturize(grad * conv, 0)
        dconv = grad * gate_f
        hold(4, dconv, HALO)
        dmixed = long[0:1] * dconv
        for tap in range(1, TAPS):
            dmixed = dmixed + long[tap : tap + 1] * at(4, HALO + tap, count)
        dkey_ref[:, lanes] = unfeaturize(dmixed * value_f[HALO:], 1)
        dvalue_ref[:, lanes] = unfeaturize(dmixed * key_f[HALO:], 2)
        return carry

    lax.fori_loop(0, width // HD, chunk, 0)


def hyena(streams, inner, outer, short_filter, long_filter, first, steps, filled=()):
    tokens, channels = streams[0].shape
    width = channels // 8
    own = steps * width
    block = pl.BlockSpec((tokens, width), lambda i: (0, first + i))
    edge = pl.BlockSpec((4 * HALO, width), lambda i: (0, first + i))
    return pl.pallas_call(
        functools.partial(hyena_kernel, first * width),
        grid=(steps,),
        in_specs=[block] * 4
        + [edge, edge]
        + [
            pl.BlockSpec((3, SHORT, width), lambda i: (0, 0, first + i)),
            pl.BlockSpec(long_filter.shape, lambda i: (0, 0)),
        ]
        + [pl.BlockSpec(memory_space=pl.ANY)] * len(filled),
        out_specs=[block] * 4,
        out_shape=[jax.ShapeDtypeStruct((tokens, channels), jnp.bfloat16)] * 4,
        scratch_shapes=[
            pltpu.VMEM((TAPS, own), jnp.float32),
            pltpu.VMEM((5, tokens + 4 * HALO, HD), jnp.float32),
        ],
        input_output_aliases={8 + i: i for i in range(len(filled))},
        compiler_params=pltpu.CompilerParams(vmem_limit_bytes=VMEM),
        cost_estimate=pl.CostEstimate(
            flops=(14000 if filled else 56000) * tokens * own, bytes_accessed=16 * tokens * own, transcendentals=0
        ),
        name="hyena",
    )(*streams, inner, outer, short_filter, long_filter, *filled)


def own_slot(split):
    return lax.axis_index("tp") * split + lax.axis_index("ctx") % split


def pack_edges_kernel(streams, split, k_ref, v_ref, *refs):
    first_refs, last_refs = refs[:streams], refs[streams : 2 * streams]
    kv_refs, (inner_ref, outer_ref) = refs[2 * streams : -2], refs[-2:]
    width = kv_refs[0].shape[2]
    own = own_slot(split) if split > 1 else 0
    for distance, ref in enumerate(kv_refs):
        part = pl.ds(pl.multiple_of((own ^ distance) * width, HD), width)
        ref[0] = k_ref[:, part]
        ref[1] = v_ref[:, part]
    f32 = jnp.float32
    odd = lax.axis_index("ctx") % 2

    def edge(refs, start, at):
        pair = [ref[...].astype(f32)[start : start + HALO] for ref in refs[at : at + 2]]
        return jnp.concatenate(pair, axis=0)

    for at in range(0, streams, 2):
        rows = slice(at * HALO, (at + 2) * HALO)
        head, tail = edge(first_refs, 0, at), edge(last_refs, HALO, at)
        inner_ref[rows] = jnp.where(odd == 1, head, tail).astype(inner_ref.dtype)
        outer_ref[rows] = jnp.where(odd == 1, tail, head).astype(outer_ref.dtype)


def pack_edges(keys, values, streams, slots, split):
    rows, columns = keys.shape
    tokens, channels = streams[0].shape
    edge = 2 * HALO
    count = len(streams)
    whole = pl.BlockSpec((rows, columns), lambda i: (0, 0))
    first = pl.BlockSpec((edge, channels), lambda i: (0, 0))
    last = pl.BlockSpec((edge, channels), lambda i: (tokens // edge - 1, 0))
    halo = (count * HALO, channels)
    laid = (2, rows, columns // slots)
    return pl.pallas_call(
        functools.partial(pack_edges_kernel, count, split),
        grid=(1,),
        in_specs=[whole] * 2 + [first] * count + [last] * count,
        out_specs=[pl.BlockSpec(laid, lambda i: (0, 0, 0))] * slots
        + [pl.BlockSpec(halo, lambda i: (0, 0))] * 2,
        out_shape=[jax.ShapeDtypeStruct(laid, keys.dtype)] * slots
        + [jax.ShapeDtypeStruct(halo, keys.dtype)] * 2,
        name="pack_edges",
    )(keys, values, *streams, *streams)


def join_kernel(split, *refs):
    parts, target = refs[:-1], refs[-1]
    piece = parts[0].shape[1]
    slot = own_slot(split)
    for distance, ref in enumerate(parts):
        held = slot ^ distance
        place = held % split * (len(parts) // split) + held // split
        target[:, pl.ds(pl.multiple_of(place * piece, 32), piece)] = ref[...]


def join(parts, split):
    pair, rows, width = parts[0].shape
    return pl.pallas_call(
        functools.partial(join_kernel, split),
        out_shape=jax.ShapeDtypeStruct((pair, rows * len(parts), width), parts[0].dtype),
        name="join",
    )(*parts)


def pack_rows_kernel(split, q_ref, g_ref, *refs):
    outs, sems = refs[:-1], refs[-1]
    width = outs[0].shape[1] // 2
    slot = own_slot(split)
    copies = []
    for distance, out in enumerate(outs):
        part = pl.ds(pl.multiple_of((slot ^ distance) * width, HD), width)
        for ref, first in ((q_ref, 0), (g_ref, width)):
            copies.append(
                pltpu.make_async_copy(
                    ref.at[:, part], out.at[:, first : first + width], sems.at[len(copies)]
                )
            )
    for copy in copies:
        copy.start()
    for copy in copies:
        copy.wait()


def pack_rows(queries, grads, slots, split):
    rows, columns = queries.shape
    shape = jax.ShapeDtypeStruct((rows, 2 * columns // slots), queries.dtype)
    return pl.pallas_call(
        functools.partial(pack_rows_kernel, split),
        in_specs=[pl.BlockSpec(memory_space=pltpu.VMEM)] * 2,
        out_specs=[pl.BlockSpec(memory_space=pltpu.HBM)] * slots,
        out_shape=[shape] * slots,
        scratch_shapes=[pltpu.SemaphoreType.DMA((2 * slots,))],
        compiler_params=pltpu.CompilerParams(vmem_limit_bytes=VMEM_PACK),
        name="pack_rows",
    )(queries, grads)


def attention_kernel(pieces, distances, groups, prior, *refs):
    (info_ref, lengths_ref), refs = refs[:2], refs[2:]
    steps = len(distances)
    qg_refs, refs = refs[: steps * groups], refs[steps * groups :]
    piece_refs, refs = refs[:pieces], refs[pieces:]
    prior_refs, refs = refs[: prior * pieces], refs[prior * pieces :]
    out_refs, refs = refs[:steps], refs[steps:]
    term_refs, refs = refs[:pieces], refs[pieces:]
    kv, k_t, v_t, dk_sum, dv_sum, scores, weights, dscores = refs[:8]
    q_rows, q_t, g_rows, g_t, peak8, total8, out_t, dq_t = refs[8:]
    step = pl.program_id(0)
    blocks = k_t.shape[0]
    run = qg_refs[0].shape[0]
    columns = qg_refs[0].shape[1] // 2
    heads = columns // HD
    size = groups * run
    rows = size * heads
    f32 = jnp.float32
    bf16 = jnp.bfloat16
    chunks = [slice(start, min(start + 256, rows)) for start in range(0, rows, 256)]
    ctx = lax.axis_index("ctx")
    own = lax.axis_index("tp") if groups > 1 else 0
    origin = info_ref[0]

    def record_start(position):
        ends = 0
        start = position * 0
        for record in range(lengths_ref.shape[0]):
            ends = ends + lengths_ref[record]
            start = jnp.where(position >= ends, ends, start)
        return start

    def rows_of(b):
        return pl.ds(pl.multiple_of(b * KB, KB), KB)

    def piece_rows(index):
        count = piece_refs[index].shape[1]
        return pl.ds(pl.multiple_of(info_ref[1 + index], 64), count)

    @pl.when(step == 0)
    def _():
        filled = sum(ref.shape[1] for ref in piece_refs)
        if filled < kv.shape[0]:
            kv[filled:] = jnp.zeros((kv.shape[0] - filled, 2 * HD), bf16)
        for index in range(pieces):
            kv[piece_rows(index), :HD] = piece_refs[index][0]
            kv[piece_rows(index), HD:] = piece_refs[index][1]
        dk_sum[...] = jnp.zeros(dk_sum.shape, f32)
        dv_sum[...] = jnp.zeros(dv_sum.shape, f32)

        def prepare(b, carry):
            k_t[b] = kv[rows_of(b), :HD].T
            v_t[b] = kv[rows_of(b), HD:].T
            return carry

        lax.fori_loop(0, blocks, prepare, 0)

    for which in range(steps):

        @pl.when(step == which)
        def _():
            for a in range(groups):
                ref = qg_refs[which * groups + a]
                for h in range(heads):
                    part = slice(h * size + a * run, h * size + (a + 1) * run)
                    q_rows[part] = ref[:, h * HD : (h + 1) * HD]
                    g_rows[part] = ref[:, columns + h * HD : columns + (h + 1) * HD]

    q_t[...] = q_rows[...].T
    g_t[...] = g_rows[...].T
    peak8[...] = jnp.full((8, rows), NEG, f32)
    total8[...] = jnp.zeros((8, rows), f32)
    out_t[...] = jnp.zeros((HD, rows), f32)
    dq_t[...] = jnp.zeros((HD, rows), f32)

    distance = distances[0]
    for which in range(1, steps):
        distance = jnp.where(step == which, distances[which], distance)
    q_first = (ctx ^ distance) * size
    low_first = record_start(q_first)
    low_last = record_start(q_first + (size - 1))
    token = lax.broadcasted_iota(jnp.int32, (1, rows), 1) % size
    if groups > 1:
        token = ((token // run) ^ own) * run + token % run
    pos = q_first + token
    low = record_start(pos)
    first = (low_first - origin) // KB
    last = (q_first + (size - 1) - origin) // KB + 1

    def fold(values, combine):
        result = values[0:8]
        for start in range(8, values.shape[0], 8):
            result = combine(result, values[start : start + 8])
        return result

    def score_pass(b, carry):
        base = origin + b * KB
        whole = (base + (KB - 1) <= q_first) & (base >= low_last)

        @pl.when(whole)
        def _():
            for part in chunks:
                s = jnp.dot(kv[rows_of(b), :HD], q_t[:, part], preferred_element_type=f32)
                scores[b - first, :, part] = s
                peak8[:, part] = jnp.maximum(peak8[:, part], fold(s, jnp.maximum))

        @pl.when(jnp.logical_not(whole))
        def _():
            for part in chunks:
                s = jnp.dot(kv[rows_of(b), :HD], q_t[:, part], preferred_element_type=f32)
                key_pos = base + lax.broadcasted_iota(jnp.int32, s.shape, 0)
                allowed = (key_pos <= pos[:, part]) & (key_pos >= low[:, part])
                s = jnp.where(allowed, s, NEG)
                scores[b - first, :, part] = s
                peak8[:, part] = jnp.maximum(peak8[:, part], fold(s, jnp.maximum))

        return carry

    lax.fori_loop(first, last, score_pass, 0)
    peak = jnp.max(peak8[...], axis=0, keepdims=True) * TO_EXP2

    def weight_pass(b, carry):
        for part in chunks:
            w = jnp.exp2(scores[b - first, :, part] * TO_EXP2 - peak[:, part])
            total8[:, part] += fold(w, jnp.add)
            w_b = w.astype(bf16)
            weights[b - first, :, part] = w_b
            out_t[:, part] += jnp.dot(v_t[b], w_b, preferred_element_type=f32)
        return carry

    lax.fori_loop(first, last, weight_pass, 0)
    inverse = 1.0 / jnp.sum(total8[...], axis=0, keepdims=True)
    out_b = (out_t[...] * inverse).astype(bf16)
    g_wide = g_t[...].astype(f32)
    delta = jnp.sum(g_wide * out_b.astype(f32), axis=0, keepdims=True) * inverse
    g_scaled = (g_wide * inverse).astype(bf16)
    g_t[...] = g_scaled
    g_rows[...] = g_scaled.T

    def give(wide, first):
        for which in range(steps):

            @pl.when(step == which)
            def _():
                for a in range(groups):
                    to = pl.ds(pl.multiple_of((own ^ a) * run, 16), run)
                    for h in range(heads):
                        start = h * size + a * run
                        out_refs[which][to, first + h * HD : first + (h + 1) * HD] = wide[
                            start : start + run
                        ]

    give(out_b.T, 0)

    def grad_pass(b, carry):
        for part in chunks:
            dp = jnp.dot(kv[rows_of(b), HD:], g_t[:, part], preferred_element_type=f32)
            w = weights[b - first, :, part].astype(f32)
            dscores[:, part] = (w * (dp - delta[:, part])).astype(bf16)
        dv_sum[rows_of(b)] += jnp.dot(weights[b - first], g_rows[...], preferred_element_type=f32)
        dk_sum[rows_of(b)] += jnp.dot(dscores[...], q_rows[...], preferred_element_type=f32)
        dq_t[...] += jnp.dot(k_t[b], dscores[...], preferred_element_type=f32)
        return carry

    lax.fori_loop(first, last, grad_pass, 0)
    give((dq_t[...] * SCALE).astype(bf16).T, heads * HD)

    @pl.when(step == steps - 1)
    def _():
        for index in range(pieces):
            dk = dk_sum[piece_rows(index)] * SCALE
            dv = dv_sum[piece_rows(index)]
            if prior:
                dk = dk + prior_refs[index][0].astype(f32)
                dv = dv + prior_refs[index][1].astype(f32)
            term_refs[index][0] = dk.astype(bf16)
            term_refs[index][1] = dv.astype(bf16)


def attention(qg_pieces, kv_pieces, info, lengths, distances, most, prior=()):
    run, columns = qg_pieces[0].shape
    steps = len(distances)
    groups = len(qg_pieces) // steps
    size = groups * run
    heads = columns // (2 * HD)
    rows = size * heads
    pieces = len(kv_pieces)
    keys = -(-sum(part.shape[1] for part in kv_pieces) // KB) * KB
    blocks = keys // KB
    live = min(blocks, (most + size - 3) // KB + 2)
    bf16 = jnp.bfloat16
    f32 = jnp.float32

    def still(shape):
        return pl.BlockSpec(shape, lambda i, *_: (0,) * len(shape))

    kv_specs = [still(part.shape) for part in kv_pieces]
    given = (size, columns)
    pairs = size * steps * heads * keys
    results = pl.pallas_call(
        functools.partial(attention_kernel, pieces, distances, groups, 1 if prior else 0),
        grid_spec=pltpu.PrefetchScalarGridSpec(
            num_scalar_prefetch=2,
            grid=(steps,),
            in_specs=[still((run, columns))] * len(qg_pieces)
            + kv_specs
            + (kv_specs if prior else []),
            out_specs=[still(given)] * steps + kv_specs,
            scratch_shapes=[
                pltpu.VMEM((keys, 2 * HD), bf16),
                pltpu.VMEM((blocks, HD, KB), bf16),
                pltpu.VMEM((blocks, HD, KB), bf16),
                pltpu.VMEM((keys, HD), f32),
                pltpu.VMEM((keys, HD), f32),
                pltpu.VMEM((live, KB, rows), f32),
                pltpu.VMEM((live, KB, rows), bf16),
                pltpu.VMEM((KB, rows), bf16),
                pltpu.VMEM((rows, HD), bf16),
                pltpu.VMEM((HD, rows), bf16),
                pltpu.VMEM((rows, HD), bf16),
                pltpu.VMEM((HD, rows), bf16),
                pltpu.VMEM((8, rows), f32),
                pltpu.VMEM((8, rows), f32),
                pltpu.VMEM((HD, rows), f32),
                pltpu.VMEM((HD, rows), f32),
            ],
        ),
        out_shape=[jax.ShapeDtypeStruct(given, bf16)] * steps
        + [jax.ShapeDtypeStruct(part.shape, bf16) for part in kv_pieces],
        compiler_params=pltpu.CompilerParams(vmem_limit_bytes=VMEM),
        cost_estimate=pl.CostEstimate(
            flops=48 * HD * pairs, bytes_accessed=32 * rows * HD * steps, transcendentals=pairs
        ),
        name="attention",
    )(info, lengths, *qg_pieces, *kv_pieces, *prior)
    return results[:steps], results[steps:]


def settle_kernel(split, *refs):
    piece_refs, (out_ref, dq_ref) = refs[:split], refs[split:]
    width = piece_refs[0].shape[1] // 2
    core = lax.axis_index("ctx") % split
    for distance in range(split):
        to = pl.ds(pl.multiple_of((core ^ distance) * width, HD), width)
        out_ref[:, to] = piece_refs[distance][:, :width]
        dq_ref[:, to] = piece_refs[distance][:, width:]


def settle(parts):
    split = len(parts)
    rows, width = parts[0].shape
    shape = jax.ShapeDtypeStruct((rows, width * split // 2), parts[0].dtype)
    return pl.pallas_call(
        functools.partial(settle_kernel, split),
        out_shape=[shape] * 2,
        compiler_params=pltpu.CompilerParams(vmem_limit_bytes=VMEM),
        name="settle",
    )(*parts)


def body(
    record_lengths,
    query_heads,
    key_heads,
    value_heads,
    out_grad,
    gate_input,
    key_input,
    value_input,
    hyena_grad,
    short_filter,
    long_filter,
):
    ctx = lax.axis_size("ctx")
    tp = lax.axis_size("tp")
    own_ctx = lax.axis_index("ctx")
    piece = query_heads.shape[0]
    tokens = piece * tp
    window = tokens * ctx
    most = window // 2 + 192
    split = PLANE if (KVH // tp) % PLANE == 0 else 1
    slots = tp * split
    kv_local = KVH // slots
    assert kv_local == 1 and tokens % 192 == 0
    unit = tokens * split
    lanes = PLANE // split
    plane = unit * lanes
    reach = (most - 1) // plane
    tail = -(-(most - 1 - reach * plane) // 192) * 192
    core = own_ctx % split
    lane = own_ctx // split % lanes
    level = own_ctx // PLANE
    f32 = jnp.float32
    bf16 = jnp.bfloat16

    members = [
        [t * ctx + n * split + c for t in range(tp) for c in range(split)]
        for n in range(ctx // split)
    ]

    def share(laid):
        return lax.all_to_all(
            laid, ("tp", "ctx"), 0, 0, axis_index_groups=members, tiled=True
        )

    permute = functools.partial(lax.ppermute, axis_name="ctx")

    def across(values, distance):
        return permute(values, perm=[(i, i ^ (distance * split)) for i in range(ctx)])

    def up(values):
        return permute(values, perm=[(i, i + PLANE) for i in range(ctx - PLANE)])

    def down(values):
        return permute(values, perm=[(i + PLANE, i) for i in range(ctx - PLANE)])

    def swap(values, distance):
        return permute(values, perm=[(i, i ^ distance) for i in range(ctx)])

    far = (reach + 1) * PLANE - (lanes - 1) * split
    far_pairs = [
        (i, i + far) for i in range(ctx - far) if i // split % lanes == lanes - 1
    ]

    streams = (gate_input, key_input, value_input, hyena_grad)
    *kv, inner, outer = pack_edges(key_heads, value_heads, streams, slots, split)
    inner = permute(inner, perm=[(i, i ^ 1) for i in range(ctx)])
    outer = permute(
        outer, perm=[(i, (i + 1 if i % 2 else i - 1)) for i in range(1, ctx - 1)]
    )

    def exchange(values, which):
        for distance in which:
            far_t, far_c = distance // split, distance % split
            perm = [
                (i * tp + t, (i ^ far_c) * tp + (t ^ far_t))
                for t in range(tp)
                for i in range(ctx)
            ]
            values[distance] = lax.ppermute(values[distance], ("ctx", "tp"), perm)

    pairwise = split > 1 and piece % 32 == 0
    if pairwise:
        kv[0], query_heads = lax.optimization_barrier((kv[0], query_heads))
        qg = list(pack_rows(query_heads, out_grad, slots, split))
        exchange(kv, range(1, slots))
        kv[0], qg[0] = lax.optimization_barrier((kv[0], qg[0]))
        own_kv = join(kv, split)
    else:
        kv = share(jnp.stack(kv)).reshape(tp, split, 2, piece, kv_local * HD)
        own_kv = kv.transpose(2, 1, 0, 3, 4).reshape(2, unit, kv_local * HD)
        cut = [part.reshape(piece, slots, -1) for part in (query_heads, out_grad)]
        laid = jnp.concatenate(cut, axis=2).transpose(1, 0, 2)
        qg = share(laid).reshape(tp, split, piece, -1).transpose(1, 0, 2, 3)
        qg = list(qg.reshape(split, tokens, -1))

    calls = [(split - 1, 0), (split // 2, split // 2 - 1)] if split > 1 else [(0,)]

    def rows_for(call):
        return [a * split + c for c in calls[call] for a in range(tp)]

    filters = (short_filter, long_filter)
    columns = [own_kv]
    if pairwise:
        first = [d for d in rows_for(0) if d]
        own_kv, *held = lax.optimization_barrier((own_kv,) + tuple(qg[d] for d in first))
        columns = [own_kv]
        for distance, value in zip(first, held):
            qg[distance] = value
        exchange(qg, first)
    for hop in range(reach):
        coming = up(columns[-1])
        if hop == reach - 1:
            inner, columns[-1] = lax.optimization_barrier((inner, columns[-1]))
            hyena_outs = hyena(streams, inner, outer, *filters, 0, 1)
            coming, first_out = lax.optimization_barrier((coming, hyena_outs[0]))
            hyena_outs = [first_out] + list(hyena_outs[1:])
        columns.append(coming)
    tail_kv = own_kv[:, unit - tail :]
    tail_kv, columns[1] = lax.optimization_barrier((tail_kv, columns[1]))
    tail_kv = permute(tail_kv, perm=far_pairs)
    pieces = [tail_kv]
    places = [jnp.int32(0)]
    for back in range(reach + 1):
        for distance in range(lanes):
            held = columns[back]
            pieces.append(held if distance == 0 else across(held, distance))
            places.append(tail + (reach - back) * plane + (lane ^ distance) * unit)
    origin = (level - reach) * plane - tail
    info = jnp.stack([origin] + places).astype(jnp.int32)

    owners = [None] * split
    terms = ()
    arrived = None
    for call, distances in enumerate(calls):
        if call:
            exchange(qg, rows_for(call))
        held = [qg[d] for d in rows_for(call)] if pairwise else qg
        outs, terms = attention(held, pieces, info, record_lengths, distances, most, terms)
        if arrived is not None:
            at = 1 + reach * lanes
            terms = list(terms)
            arrived, terms[at] = lax.optimization_barrier((arrived, terms[at]))
            owners[calls[0][0]] = arrived
        for distance, value in zip(distances, outs):
            owners[distance] = swap(value, distance) if distance else value
        if call == 0 and split > 1:
            arrived = owners[distances[0]]
    attn_out, grad_query = settle(owners)

    def plane_sum(back):
        at = 1 + back * lanes
        total = terms[at].astype(f32)
        for distance in range(1, lanes):
            total = total + across(terms[at + distance], distance).astype(f32)
        return total

    tail_term = permute(terms[0], perm=[(j, i) for i, j in far_pairs])
    running = plane_sum(reach).astype(bf16)
    for back in range(reach - 1, -1, -1):
        coming = down(running)
        if back >= reach - 2:
            inner, running = lax.optimization_barrier((inner, running))
            eighths = (1, 4) if back == reach - 1 else (5, 3)
            hyena_outs = hyena(streams, inner, outer, *filters, *eighths, hyena_outs)
            coming, first_out = lax.optimization_barrier((coming, hyena_outs[0]))
            hyena_outs = [first_out] + list(hyena_outs[1:])
        running = plane_sum(back) + coming.astype(f32)
        if back:
            running = running.astype(bf16)
    running, attn_out = lax.optimization_barrier((running, attn_out))
    owned = jnp.concatenate(
        [running[:, : unit - tail], running[:, unit - tail :] + tail_term.astype(f32)], axis=1
    ).astype(bf16)

    parts = []
    for distance in range(split):
        held = lax.dynamic_slice_in_dim(owned, (core ^ distance) * tokens, tokens, 1)
        parts.append(swap(held, distance) if distance else held)
    bit = 1
    while bit < split:
        parts = [
            jnp.where(core & bit != 0, parts[index ^ bit], parts[index]) for index in range(split)
        ]
        bit = 2 * bit
    grads = jnp.concatenate(parts, axis=2)
    return (attn_out, grad_query, grads[0], grads[1]) + tuple(hyena_outs)


def solution(mesh):
    rows = P(("ctx", "tp"), None)
    both = P("ctx", "tp")
    return jax.shard_map(
        body,
        mesh=mesh,
        in_specs=(P(), rows, rows, rows, rows, both, both, both, both)
        + (P(None, None, "tp"), P(None, "tp")),
        out_specs=(both,) * 8,
        check_vma=False,
    )
```

```python
import functools

import jax
import jax.numpy as jnp
import numpy as np
from jax import lax
from jax.experimental import pallas as pl
from jax.experimental.pallas import tpu as pltpu
from jax.sharding import PartitionSpec as P

HD = 128
QH = 64
KVH = 8
GROUP = 16
TAPS = 7
SHORT = 3
HALO = 8
PLANE = 4
KB = 256
NEG = -1e30
SCALE = HD ** (-0.5)
TO_EXP2 = SCALE * 1.4426950408889634
VMEM = 48 * 1024 * 1024
VMEM_PACK = 62 * 1024 * 1024


def hyena_kernel(
    first,
    gate_ref,
    key_ref,
    value_ref,
    grad_ref,
    inner_ref,
    outer_ref,
    short_ref,
    long_ref,
    *refs,
):
    out_ref, dgate_ref, dkey_ref, dvalue_ref, taps, shift = refs[-6:]
    tokens, width = gate_ref.shape
    own = pl.program_id(0)
    odd = lax.axis_index("ctx") % 2

    @pl.when(own == 0)
    def _():
        shape = (long_ref.shape[1], taps.shape[1])
        group = lax.broadcasted_iota(jnp.int32, shape, 0)
        channel = first + lax.broadcasted_iota(jnp.int32, shape, 1)
        taps[...] = jnp.dot(
            long_ref[...],
            (group == channel // GROUP).astype(jnp.float32),
            precision=lax.Precision.HIGHEST,
            preferred_element_type=jnp.float32,
        )

    rows = tokens + 2 * HALO

    def chunk(index, carry):
        lanes = pl.ds(pl.multiple_of(index * HD, HD), HD)
        inner = inner_ref[:, lanes].astype(jnp.float32)
        outer = outer_ref[:, lanes].astype(jnp.float32)
        before = jnp.where(odd == 1, inner, outer)
        after = jnp.where(odd == 1, outer, inner)

        long = taps[:, pl.ds(pl.multiple_of(own * width + index * HD, HD), HD)]

        def short(which, tap):
            return short_ref[which, tap : tap + 1, lanes]

        def hold(slot, values, first=0):
            shift[slot, first + HALO : first + HALO + values.shape[0]] = values

        def at(slot, first, count):
            return shift[slot, first + HALO : first + HALO + count]

        def padded(ref, which):
            part = slice(which * HALO, (which + 1) * HALO)
            return jnp.concatenate(
                [before[part], ref[:, lanes].astype(jnp.float32), after[part]], axis=0
            )

        def featurize(ref, which):
            values = padded(ref, which)
            hold(which, values)
            result = short(which, 0) * values
            for tap in range(1, SHORT):
                result = result + short(which, tap) * at(which, -tap, rows)
            return result

        def unfeaturize(grads, which):
            hold(which, grads, HALO)
            result = short(which, 0) * grads[:tokens]
            for tap in range(1, SHORT):
                result = result + short(which, tap) * at(which, HALO + tap, tokens)
            return result.astype(jnp.bfloat16)

        count = tokens + HALO
        key_f = featurize(key_ref, 1)
        value_f = featurize(value_ref, 2)
        mixed = key_f * value_f
        hold(3, mixed)
        conv = long[0:1] * mixed[HALO:]
        for tap in range(1, TAPS):
            conv = conv + long[tap : tap + 1] * at(3, HALO - tap, count)
        gate_f = featurize(gate_ref, 0)[HALO:]
        out_ref[:, lanes] = (gate_f * conv)[:tokens].astype(jnp.bfloat16)
        grad = padded(grad_ref, 3)[HALO:]
        dgate_ref[:, lanes] = unfeaturize(grad * conv, 0)
        dconv = grad * gate_f
        hold(4, dconv, HALO)
        dmixed = long[0:1] * dconv
        for tap in range(1, TAPS):
            dmixed = dmixed + long[tap : tap + 1] * at(4, HALO + tap, count)
        dkey_ref[:, lanes] = unfeaturize(dmixed * value_f[HALO:], 1)
        dvalue_ref[:, lanes] = unfeaturize(dmixed * key_f[HALO:], 2)
        return carry

    lax.fori_loop(0, width // HD, chunk, 0)


def hyena(streams, inner, outer, short_filter, long_filter, first, steps, filled=()):
    tokens, channels = streams[0].shape
    width = channels // 8
    own = steps * width
    block = pl.BlockSpec((tokens, width), lambda i: (0, first + i))
    edge = pl.BlockSpec((4 * HALO, width), lambda i: (0, first + i))
    return pl.pallas_call(
        functools.partial(hyena_kernel, first * width),
        grid=(steps,),
        in_specs=[block] * 4
        + [edge, edge]
        + [
            pl.BlockSpec((3, SHORT, width), lambda i: (0, 0, first + i)),
            pl.BlockSpec(long_filter.shape, lambda i: (0, 0)),
        ]
        + [pl.BlockSpec(memory_space=pl.ANY)] * len(filled),
        out_specs=[block] * 4,
        out_shape=[jax.ShapeDtypeStruct((tokens, channels), jnp.bfloat16)] * 4,
        scratch_shapes=[
            pltpu.VMEM((TAPS, own), jnp.float32),
            pltpu.VMEM((5, tokens + 4 * HALO, HD), jnp.float32),
        ],
        input_output_aliases={8 + i: i for i in range(len(filled))},
        compiler_params=pltpu.CompilerParams(vmem_limit_bytes=VMEM),
        cost_estimate=pl.CostEstimate(
            flops=(14000 if filled else 28000) * tokens * own, bytes_accessed=16 * tokens * own, transcendentals=0
        ),
        name="hyena",
    )(*streams, inner, outer, short_filter, long_filter, *filled)


def own_slot(split):
    return lax.axis_index("tp") * split + lax.axis_index("ctx") % split


def pack_edges_kernel(streams, split, k_ref, v_ref, *refs):
    first_refs, last_refs = refs[:streams], refs[streams : 2 * streams]
    kv_refs, (inner_ref, outer_ref) = refs[2 * streams : -2], refs[-2:]
    width = kv_refs[0].shape[2]
    own = own_slot(split) if split > 1 else 0
    for distance, ref in enumerate(kv_refs):
        part = pl.ds(pl.multiple_of((own ^ distance) * width, HD), width)
        ref[0] = k_ref[:, part]
        ref[1] = v_ref[:, part]
    f32 = jnp.float32
    odd = lax.axis_index("ctx") % 2

    def edge(refs, start, at):
        pair = [ref[...].astype(f32)[start : start + HALO] for ref in refs[at : at + 2]]
        return jnp.concatenate(pair, axis=0)

    for at in range(0, streams, 2):
        rows = slice(at * HALO, (at + 2) * HALO)
        head, tail = edge(first_refs, 0, at), edge(last_refs, HALO, at)
        inner_ref[rows] = jnp.where(odd == 1, head, tail).astype(inner_ref.dtype)
        outer_ref[rows] = jnp.where(odd == 1, tail, head).astype(outer_ref.dtype)


def pack_edges(keys, values, streams, slots, split):
    rows, columns = keys.shape
    tokens, channels = streams[0].shape
    edge = 2 * HALO
    count = len(streams)
    whole = pl.BlockSpec((rows, columns), lambda i: (0, 0))
    first = pl.BlockSpec((edge, channels), lambda i: (0, 0))
    last = pl.BlockSpec((edge, channels), lambda i: (tokens // edge - 1, 0))
    halo = (count * HALO, channels)
    laid = (2, rows, columns // slots)
    return pl.pallas_call(
        functools.partial(pack_edges_kernel, count, split),
        grid=(1,),
        in_specs=[whole] * 2 + [first] * count + [last] * count,
        out_specs=[pl.BlockSpec(laid, lambda i: (0, 0, 0))] * slots
        + [pl.BlockSpec(halo, lambda i: (0, 0))] * 2,
        out_shape=[jax.ShapeDtypeStruct(laid, keys.dtype)] * slots
        + [jax.ShapeDtypeStruct(halo, keys.dtype)] * 2,
        name="pack_edges",
    )(keys, values, *streams, *streams)


def join_kernel(split, *refs):
    parts, target = refs[:-1], refs[-1]
    piece = parts[0].shape[1]
    slot = own_slot(split)
    for distance, ref in enumerate(parts):
        held = slot ^ distance
        place = held % split * (len(parts) // split) + held // split
        target[:, pl.ds(pl.multiple_of(place * piece, 32), piece)] = ref[...]


def join(parts, split):
    pair, rows, width = parts[0].shape
    return pl.pallas_call(
        functools.partial(join_kernel, split),
        out_shape=jax.ShapeDtypeStruct((pair, rows * len(parts), width), parts[0].dtype),
        name="join",
    )(*parts)


def pack_rows_kernel(split, q_ref, g_ref, *refs):
    outs, sems = refs[:-1], refs[-1]
    width = outs[0].shape[1] // 2
    slot = own_slot(split)
    copies = []
    for distance, out in enumerate(outs):
        part = pl.ds(pl.multiple_of((slot ^ distance) * width, HD), width)
        for ref, first in ((q_ref, 0), (g_ref, width)):
            copies.append(
                pltpu.make_async_copy(
                    ref.at[:, part], out.at[:, first : first + width], sems.at[len(copies)]
                )
            )
    for copy in copies:
        copy.start()
    for copy in copies:
        copy.wait()


def pack_rows(queries, grads, slots, split):
    rows, columns = queries.shape
    shape = jax.ShapeDtypeStruct((rows, 2 * columns // slots), queries.dtype)
    return pl.pallas_call(
        functools.partial(pack_rows_kernel, split),
        in_specs=[pl.BlockSpec(memory_space=pltpu.VMEM)] * 2,
        out_specs=[pl.BlockSpec(memory_space=pltpu.HBM)] * slots,
        out_shape=[shape] * slots,
        scratch_shapes=[pltpu.SemaphoreType.DMA((2 * slots,))],
        compiler_params=pltpu.CompilerParams(vmem_limit_bytes=VMEM_PACK),
        name="pack_rows",
    )(queries, grads)


def attention_kernel(pieces, distances, groups, prior, *refs):
    (info_ref, lengths_ref), refs = refs[:2], refs[2:]
    steps = len(distances)
    qg_refs, refs = refs[: steps * groups], refs[steps * groups :]
    piece_refs, refs = refs[:pieces], refs[pieces:]
    prior_refs, refs = refs[: prior * pieces], refs[prior * pieces :]
    out_refs, refs = refs[:steps], refs[steps:]
    term_refs, refs = refs[:pieces], refs[pieces:]
    kv, k_t, v_t, dk_sum, dv_sum, scores, weights, dscores = refs[:8]
    q_rows, q_t, g_rows, g_t, peak8, total8, out_t, dq_t = refs[8:]
    step = pl.program_id(0)
    blocks = k_t.shape[0]
    run = qg_refs[0].shape[0]
    columns = qg_refs[0].shape[1] // 2
    heads = columns // HD
    size = groups * run
    rows = size * heads
    f32 = jnp.float32
    bf16 = jnp.bfloat16
    chunks = [slice(start, min(start + 256, rows)) for start in range(0, rows, 256)]
    ctx = lax.axis_index("ctx")
    own = lax.axis_index("tp") if groups > 1 else 0
    origin = info_ref[0]

    def record_start(position):
        ends = 0
        start = position * 0
        for record in range(lengths_ref.shape[0]):
            ends = ends + lengths_ref[record]
            start = jnp.where(position >= ends, ends, start)
        return start

    def rows_of(b):
        return pl.ds(pl.multiple_of(b * KB, KB), KB)

    def piece_rows(index):
        count = piece_refs[index].shape[1]
        return pl.ds(pl.multiple_of(info_ref[1 + index], 64), count)

    @pl.when(step == 0)
    def _():
        filled = sum(ref.shape[1] for ref in piece_refs)
        if filled < kv.shape[0]:
            kv[filled:] = jnp.zeros((kv.shape[0] - filled, 2 * HD), bf16)
        for index in range(pieces):
            kv[piece_rows(index), :HD] = piece_refs[index][0]
            kv[piece_rows(index), HD:] = piece_refs[index][1]
        dk_sum[...] = jnp.zeros(dk_sum.shape, f32)
        dv_sum[...] = jnp.zeros(dv_sum.shape, f32)

        def prepare(b, carry):
            k_t[b] = kv[rows_of(b), :HD].T
            v_t[b] = kv[rows_of(b), HD:].T
            return carry

        lax.fori_loop(0, blocks, prepare, 0)

    for which in range(steps):

        @pl.when(step == which)
        def _():
            for a in range(groups):
                ref = qg_refs[which * groups + a]
                for h in range(heads):
                    part = slice(h * size + a * run, h * size + (a + 1) * run)
                    q_rows[part] = ref[:, h * HD : (h + 1) * HD]
                    g_rows[part] = ref[:, columns + h * HD : columns + (h + 1) * HD]

    q_t[...] = q_rows[...].T
    g_t[...] = g_rows[...].T
    peak8[...] = jnp.full((8, rows), NEG, f32)
    total8[...] = jnp.zeros((8, rows), f32)
    out_t[...] = jnp.zeros((HD, rows), f32)
    dq_t[...] = jnp.zeros((HD, rows), f32)

    distance = distances[0]
    for which in range(1, steps):
        distance = jnp.where(step == which, distances[which], distance)
    q_first = (ctx ^ distance) * size
    low_first = record_start(q_first)
    low_last = record_start(q_first + (size - 1))
    token = lax.broadcasted_iota(jnp.int32, (1, rows), 1) % size
    if groups > 1:
        token = ((token // run) ^ own) * run + token % run
    pos = q_first + token
    low = record_start(pos)
    first = (low_first - origin) // KB
    last = (q_first + (size - 1) - origin) // KB + 1

    def fold(values, combine):
        result = values[0:8]
        for start in range(8, values.shape[0], 8):
            result = combine(result, values[start : start + 8])
        return result

    def score_pass(b, carry):
        base = origin + b * KB
        whole = (base + (KB - 1) <= q_first) & (base >= low_last)

        @pl.when(whole)
        def _():
            for part in chunks:
                s = jnp.dot(kv[rows_of(b), :HD], q_t[:, part], preferred_element_type=f32)
                scores[b - first, :, part] = s
                peak8[:, part] = jnp.maximum(peak8[:, part], fold(s, jnp.maximum))

        @pl.when(jnp.logical_not(whole))
        def _():
            for part in chunks:
                s = jnp.dot(kv[rows_of(b), :HD], q_t[:, part], preferred_element_type=f32)
                key_pos = base + lax.broadcasted_iota(jnp.int32, s.shape, 0)
                allowed = (key_pos <= pos[:, part]) & (key_pos >= low[:, part])
                s = jnp.where(allowed, s, NEG)
                scores[b - first, :, part] = s
                peak8[:, part] = jnp.maximum(peak8[:, part], fold(s, jnp.maximum))

        return carry

    lax.fori_loop(first, last, score_pass, 0)
    peak = jnp.max(peak8[...], axis=0, keepdims=True) * TO_EXP2

    def weight_pass(b, carry):
        for part in chunks:
            w = jnp.exp2(scores[b - first, :, part] * TO_EXP2 - peak[:, part])
            total8[:, part] += fold(w, jnp.add)
            w_b = w.astype(bf16)
            weights[b - first, :, part] = w_b
            out_t[:, part] += jnp.dot(v_t[b], w_b, preferred_element_type=f32)
        return carry

    lax.fori_loop(first, last, weight_pass, 0)
    inverse = 1.0 / jnp.sum(total8[...], axis=0, keepdims=True)
    out_b = (out_t[...] * inverse).astype(bf16)
    g_wide = g_t[...].astype(f32)
    delta = jnp.sum(g_wide * out_b.astype(f32), axis=0, keepdims=True) * inverse
    g_scaled = (g_wide * inverse).astype(bf16)
    g_t[...] = g_scaled
    g_rows[...] = g_scaled.T

    def give(wide, first):
        for which in range(steps):

            @pl.when(step == which)
            def _():
                for a in range(groups):
                    to = pl.ds(pl.multiple_of((own ^ a) * run, 16), run)
                    for h in range(heads):
                        start = h * size + a * run
                        out_refs[which][to, first + h * HD : first + (h + 1) * HD] = wide[
                            start : start + run
                        ]

    give(out_b.T, 0)

    def grad_pass(b, carry):
        for part in chunks:
            dp = jnp.dot(kv[rows_of(b), HD:], g_t[:, part], preferred_element_type=f32)
            w = weights[b - first, :, part].astype(f32)
            dscores[:, part] = (w * (dp - delta[:, part])).astype(bf16)
        dv_sum[rows_of(b)] += jnp.dot(weights[b - first], g_rows[...], preferred_element_type=f32)
        dk_sum[rows_of(b)] += jnp.dot(dscores[...], q_rows[...], preferred_element_type=f32)
        dq_t[...] += jnp.dot(k_t[b], dscores[...], preferred_element_type=f32)
        return carry

    lax.fori_loop(first, last, grad_pass, 0)
    give((dq_t[...] * SCALE).astype(bf16).T, heads * HD)

    @pl.when(step == steps - 1)
    def _():
        for index in range(pieces):
            dk = dk_sum[piece_rows(index)] * SCALE
            dv = dv_sum[piece_rows(index)]
            if prior:
                dk = dk + prior_refs[index][0].astype(f32)
                dv = dv + prior_refs[index][1].astype(f32)
            term_refs[index][0] = dk.astype(bf16)
            term_refs[index][1] = dv.astype(bf16)


def attention(qg_pieces, kv_pieces, info, lengths, distances, most, prior=()):
    run, columns = qg_pieces[0].shape
    steps = len(distances)
    groups = len(qg_pieces) // steps
    size = groups * run
    heads = columns // (2 * HD)
    rows = size * heads
    pieces = len(kv_pieces)
    keys = -(-sum(part.shape[1] for part in kv_pieces) // KB) * KB
    blocks = keys // KB
    live = min(blocks, (most + size - 3) // KB + 2)
    bf16 = jnp.bfloat16
    f32 = jnp.float32

    def still(shape):
        return pl.BlockSpec(shape, lambda i, *_: (0,) * len(shape))

    kv_specs = [still(part.shape) for part in kv_pieces]
    given = (size, columns)
    pairs = size * steps * heads * keys
    results = pl.pallas_call(
        functools.partial(attention_kernel, pieces, distances, groups, 1 if prior else 0),
        grid_spec=pltpu.PrefetchScalarGridSpec(
            num_scalar_prefetch=2,
            grid=(steps,),
            in_specs=[still((run, columns))] * len(qg_pieces)
            + kv_specs
            + (kv_specs if prior else []),
            out_specs=[still(given)] * steps + kv_specs,
            scratch_shapes=[
                pltpu.VMEM((keys, 2 * HD), bf16),
                pltpu.VMEM((blocks, HD, KB), bf16),
                pltpu.VMEM((blocks, HD, KB), bf16),
                pltpu.VMEM((keys, HD), f32),
                pltpu.VMEM((keys, HD), f32),
                pltpu.VMEM((live, KB, rows), f32),
                pltpu.VMEM((live, KB, rows), bf16),
                pltpu.VMEM((KB, rows), bf16),
                pltpu.VMEM((rows, HD), bf16),
                pltpu.VMEM((HD, rows), bf16),
                pltpu.VMEM((rows, HD), bf16),
                pltpu.VMEM((HD, rows), bf16),
                pltpu.VMEM((8, rows), f32),
                pltpu.VMEM((8, rows), f32),
                pltpu.VMEM((HD, rows), f32),
                pltpu.VMEM((HD, rows), f32),
            ],
        ),
        out_shape=[jax.ShapeDtypeStruct(given, bf16)] * steps
        + [jax.ShapeDtypeStruct(part.shape, bf16) for part in kv_pieces],
        compiler_params=pltpu.CompilerParams(vmem_limit_bytes=VMEM),
        cost_estimate=pl.CostEstimate(
            flops=48 * HD * pairs, bytes_accessed=32 * rows * HD * steps, transcendentals=pairs
        ),
        name="attention",
    )(info, lengths, *qg_pieces, *kv_pieces, *prior)
    return results[:steps], results[steps:]


def settle_kernel(split, *refs):
    piece_refs, (out_ref, dq_ref) = refs[:split], refs[split:]
    width = piece_refs[0].shape[1] // 2
    core = lax.axis_index("ctx") % split
    for distance in range(split):
        to = pl.ds(pl.multiple_of((core ^ distance) * width, HD), width)
        out_ref[:, to] = piece_refs[distance][:, :width]
        dq_ref[:, to] = piece_refs[distance][:, width:]


def settle(parts):
    split = len(parts)
    rows, width = parts[0].shape
    shape = jax.ShapeDtypeStruct((rows, width * split // 2), parts[0].dtype)
    return pl.pallas_call(
        functools.partial(settle_kernel, split),
        out_shape=[shape] * 2,
        compiler_params=pltpu.CompilerParams(vmem_limit_bytes=VMEM),
        name="settle",
    )(*parts)


def body(
    record_lengths,
    query_heads,
    key_heads,
    value_heads,
    out_grad,
    gate_input,
    key_input,
    value_input,
    hyena_grad,
    short_filter,
    long_filter,
):
    ctx = lax.axis_size("ctx")
    tp = lax.axis_size("tp")
    own_ctx = lax.axis_index("ctx")
    piece = query_heads.shape[0]
    tokens = piece * tp
    window = tokens * ctx
    most = window // 2 + 192
    split = PLANE if (KVH // tp) % PLANE == 0 else 1
    slots = tp * split
    kv_local = KVH // slots
    assert kv_local == 1 and tokens % 192 == 0
    unit = tokens * split
    lanes = PLANE // split
    plane = unit * lanes
    reach = (most - 1) // plane
    tail = -(-(most - 1 - reach * plane) // 192) * 192
    core = own_ctx % split
    lane = own_ctx // split % lanes
    level = own_ctx // PLANE
    f32 = jnp.float32
    bf16 = jnp.bfloat16

    members = [
        [t * ctx + n * split + c for t in range(tp) for c in range(split)]
        for n in range(ctx // split)
    ]

    def share(laid):
        return lax.all_to_all(
            laid, ("tp", "ctx"), 0, 0, axis_index_groups=members, tiled=True
        )

    permute = functools.partial(lax.ppermute, axis_name="ctx")

    def across(values, distance):
        return permute(values, perm=[(i, i ^ (distance * split)) for i in range(ctx)])

    def up(values):
        return permute(values, perm=[(i, i + PLANE) for i in range(ctx - PLANE)])

    def down(values):
        return permute(values, perm=[(i + PLANE, i) for i in range(ctx - PLANE)])

    def swap(values, distance):
        return permute(values, perm=[(i, i ^ distance) for i in range(ctx)])

    far = (reach + 1) * PLANE - (lanes - 1) * split
    far_pairs = [
        (i, i + far) for i in range(ctx - far) if i // split % lanes == lanes - 1
    ]

    streams = (gate_input, key_input, value_input, hyena_grad)
    *kv, inner, outer = pack_edges(key_heads, value_heads, streams, slots, split)
    inner = permute(inner, perm=[(i, i ^ 1) for i in range(ctx)])
    outer = permute(
        outer, perm=[(i, (i + 1 if i % 2 else i - 1)) for i in range(1, ctx - 1)]
    )

    def exchange(values, which):
        for distance in which:
            far_t, far_c = distance // split, distance % split
            perm = [
                (i * tp + t, (i ^ far_c) * tp + (t ^ far_t))
                for t in range(tp)
                for i in range(ctx)
            ]
            values[distance] = lax.ppermute(values[distance], ("ctx", "tp"), perm)

    pairwise = split > 1 and piece % 32 == 0
    if pairwise:
        kv[0], query_heads = lax.optimization_barrier((kv[0], query_heads))
        qg = list(pack_rows(query_heads, out_grad, slots, split))
        exchange(kv, range(1, slots))
        kv[0], qg[0] = lax.optimization_barrier((kv[0], qg[0]))
        own_kv = join(kv, split)
    else:
        kv = share(jnp.stack(kv)).reshape(tp, split, 2, piece, kv_local * HD)
        own_kv = kv.transpose(2, 1, 0, 3, 4).reshape(2, unit, kv_local * HD)
        cut = [part.reshape(piece, slots, -1) for part in (query_heads, out_grad)]
        laid = jnp.concatenate(cut, axis=2).transpose(1, 0, 2)
        qg = share(laid).reshape(tp, split, piece, -1).transpose(1, 0, 2, 3)
        qg = list(qg.reshape(split, tokens, -1))

    calls = [(split - 1, 0), (split // 2, split // 2 - 1)] if split > 1 else [(0,)]

    def rows_for(call):
        return [a * split + c for c in calls[call] for a in range(tp)]

    filters = (short_filter, long_filter)
    columns = [own_kv]
    if pairwise:
        first = [d for d in rows_for(0) if d]
        own_kv, *held = lax.optimization_barrier((own_kv,) + tuple(qg[d] for d in first))
        columns = [own_kv]
        for distance, value in zip(first, held):
            qg[distance] = value
        exchange(qg, first)
    for hop in range(reach):
        coming = up(columns[-1])
        if hop == reach - 1:
            inner, columns[-1] = lax.optimization_barrier((inner, columns[-1]))
            hyena_outs = hyena(streams, inner, outer, *filters, 0, 2)
            coming, first_out = lax.optimization_barrier((coming, hyena_outs[0]))
            hyena_outs = [first_out] + list(hyena_outs[1:])
        columns.append(coming)
    tail_kv = own_kv[:, unit - tail :]
    tail_kv, columns[1] = lax.optimization_barrier((tail_kv, columns[1]))
    tail_kv = permute(tail_kv, perm=far_pairs)
    pieces = [tail_kv]
    places = [jnp.int32(0)]
    for back in range(reach + 1):
        for distance in range(lanes):
            held = columns[back]
            pieces.append(held if distance == 0 else across(held, distance))
            places.append(tail + (reach - back) * plane + (lane ^ distance) * unit)
    origin = (level - reach) * plane - tail
    info = jnp.stack([origin] + places).astype(jnp.int32)

    owners = [None] * split
    terms = ()
    arrived = None
    for call, distances in enumerate(calls):
        if call:
            exchange(qg, rows_for(call))
        held = [qg[d] for d in rows_for(call)] if pairwise else qg
        outs, terms = attention(held, pieces, info, record_lengths, distances, most, terms)
        if arrived is not None:
            at = 1 + reach * lanes
            terms = list(terms)
            arrived, terms[at] = lax.optimization_barrier((arrived, terms[at]))
            owners[calls[0][0]] = arrived
        for distance, value in zip(distances, outs):
            owners[distance] = swap(value, distance) if distance else value
        if call == 0 and split > 1:
            arrived = owners[distances[0]]
    attn_out, grad_query = settle(owners)

    def plane_sum(back):
        at = 1 + back * lanes
        total = terms[at].astype(f32)
        for distance in range(1, lanes):
            total = total + across(terms[at + distance], distance).astype(f32)
        return total

    tail_term = permute(terms[0], perm=[(j, i) for i, j in far_pairs])
    running = plane_sum(reach).astype(bf16)
    for back in range(reach - 1, -1, -1):
        coming = down(running)
        if back >= reach - 2:
            inner, running = lax.optimization_barrier((inner, running))
            eighths = (2, 4) if back == reach - 1 else (6, 2)
            hyena_outs = hyena(streams, inner, outer, *filters, *eighths, hyena_outs)
            coming, first_out = lax.optimization_barrier((coming, hyena_outs[0]))
            hyena_outs = [first_out] + list(hyena_outs[1:])
        running = plane_sum(back) + coming.astype(f32)
        if back:
            running = running.astype(bf16)
    running, attn_out = lax.optimization_barrier((running, attn_out))
    owned = jnp.concatenate(
        [running[:, : unit - tail], running[:, unit - tail :] + tail_term.astype(f32)], axis=1
    ).astype(bf16)

    parts = []
    for distance in range(split):
        held = lax.dynamic_slice_in_dim(owned, (core ^ distance) * tokens, tokens, 1)
        parts.append(swap(held, distance) if distance else held)
    bit = 1
    while bit < split:
        parts = [
            jnp.where(core & bit != 0, parts[index ^ bit], parts[index]) for index in range(split)
        ]
        bit = 2 * bit
    grads = jnp.concatenate(parts, axis=2)
    return (attn_out, grad_query, grads[0], grads[1]) + tuple(hyena_outs)


def solution(mesh):
    rows = P(("ctx", "tp"), None)
    both = P("ctx", "tp")
    return jax.shard_map(
        body,
        mesh=mesh,
        in_specs=(P(), rows, rows, rows, rows, both, both, both, both)
        + (P(None, None, "tp"), P(None, "tp")),
        out_specs=(both,) * 8,
        check_vma=False,
    )
```

```python
import functools

import jax
import jax.numpy as jnp
import numpy as np
from jax import lax
from jax.experimental import pallas as pl
from jax.experimental.pallas import tpu as pltpu
from jax.sharding import PartitionSpec as P

HD = 128
QH = 64
KVH = 8
GROUP = 16
TAPS = 7
SHORT = 3
HALO = 8
PLANE = 4
KB = 256
NEG = -1e30
SCALE = HD ** (-0.5)
TO_EXP2 = SCALE * 1.4426950408889634
VMEM = 48 * 1024 * 1024
VMEM_PACK = 62 * 1024 * 1024


def hyena_kernel(
    first,
    gate_ref,
    key_ref,
    value_ref,
    grad_ref,
    inner_ref,
    outer_ref,
    short_ref,
    long_ref,
    *refs,
):
    out_ref, dgate_ref, dkey_ref, dvalue_ref, taps, shift = refs[-6:]
    tokens, width = gate_ref.shape
    own = pl.program_id(0)
    odd = lax.axis_index("ctx") % 2

    @pl.when(own == 0)
    def _():
        shape = (long_ref.shape[1], taps.shape[1])
        group = lax.broadcasted_iota(jnp.int32, shape, 0)
        channel = first + lax.broadcasted_iota(jnp.int32, shape, 1)
        taps[...] = jnp.dot(
            long_ref[...],
            (group == channel // GROUP).astype(jnp.float32),
            precision=lax.Precision.HIGHEST,
            preferred_element_type=jnp.float32,
        )

    rows = tokens + 2 * HALO

    def chunk(index, carry):
        lanes = pl.ds(pl.multiple_of(index * HD, HD), HD)
        inner = inner_ref[:, lanes].astype(jnp.float32)
        outer = outer_ref[:, lanes].astype(jnp.float32)
        before = jnp.where(odd == 1, inner, outer)
        after = jnp.where(odd == 1, outer, inner)

        long = taps[:, pl.ds(pl.multiple_of(own * width + index * HD, HD), HD)]

        def short(which, tap):
            return short_ref[which, tap : tap + 1, lanes]

        def hold(slot, values, first=0):
            shift[slot, first + HALO : first + HALO + values.shape[0]] = values

        def at(slot, first, count):
            return shift[slot, first + HALO : first + HALO + count]

        def padded(ref, which):
            part = slice(which * HALO, (which + 1) * HALO)
            return jnp.concatenate(
                [before[part], ref[:, lanes].astype(jnp.float32), after[part]], axis=0
            )

        def featurize(ref, which):
            values = padded(ref, which)
            hold(which, values)
            result = short(which, 0) * values
            for tap in range(1, SHORT):
                result = result + short(which, tap) * at(which, -tap, rows)
            return result

        def unfeaturize(grads, which):
            hold(which, grads, HALO)
            result = short(which, 0) * grads[:tokens]
            for tap in range(1, SHORT):
                result = result + short(which, tap) * at(which, HALO + tap, tokens)
            return result.astype(jnp.bfloat16)

        count = tokens + HALO
        key_f = featurize(key_ref, 1)
        value_f = featurize(value_ref, 2)
        mixed = key_f * value_f
        hold(3, mixed)
        conv = long[0:1] * mixed[HALO:]
        for tap in range(1, TAPS):
            conv = conv + long[tap : tap + 1] * at(3, HALO - tap, count)
        gate_f = featurize(gate_ref, 0)[HALO:]
        out_ref[:, lanes] = (gate_f * conv)[:tokens].astype(jnp.bfloat16)
        grad = padded(grad_ref, 3)[HALO:]
        dgate_ref[:, lanes] = unfeaturize(grad * conv, 0)
        dconv = grad * gate_f
        hold(4, dconv, HALO)
        dmixed = long[0:1] * dconv
        for tap in range(1, TAPS):
            dmixed = dmixed + long[tap : tap + 1] * at(4, HALO + tap, count)
        dkey_ref[:, lanes] = unfeaturize(dmixed * value_f[HALO:], 1)
        dvalue_ref[:, lanes] = unfeaturize(dmixed * key_f[HALO:], 2)
        return carry

    lax.fori_loop(0, width // HD, chunk, 0)


def hyena(streams, inner, outer, short_filter, long_filter, first, steps, filled=()):
    tokens, channels = streams[0].shape
    width = channels // 8
    own = steps * width
    block = pl.BlockSpec((tokens, width), lambda i: (0, first + i))
    edge = pl.BlockSpec((4 * HALO, width), lambda i: (0, first + i))
    return pl.pallas_call(
        functools.partial(hyena_kernel, first * width),
        grid=(steps,),
        in_specs=[block] * 4
        + [edge, edge]
        + [
            pl.BlockSpec((3, SHORT, width), lambda i: (0, 0, first + i)),
            pl.BlockSpec(long_filter.shape, lambda i: (0, 0)),
        ]
        + [pl.BlockSpec(memory_space=pl.ANY)] * len(filled),
        out_specs=[block] * 4,
        out_shape=[jax.ShapeDtypeStruct((tokens, channels), jnp.bfloat16)] * 4,
        scratch_shapes=[
            pltpu.VMEM((TAPS, own), jnp.float32),
            pltpu.VMEM((5, tokens + 4 * HALO, HD), jnp.float32),
        ],
        input_output_aliases={8 + i: i for i in range(len(filled))},
        compiler_params=pltpu.CompilerParams(vmem_limit_bytes=VMEM),
        cost_estimate=pl.CostEstimate(
            flops=14000 * tokens * own, bytes_accessed=16 * tokens * own, transcendentals=0
        ),
        name="hyena",
    )(*streams, inner, outer, short_filter, long_filter, *filled)


def own_slot(split):
    return lax.axis_index("tp") * split + lax.axis_index("ctx") % split


def pack_edges_kernel(streams, split, k_ref, v_ref, *refs):
    first_refs, last_refs = refs[:streams], refs[streams : 2 * streams]
    kv_refs, (inner_ref, outer_ref) = refs[2 * streams : -2], refs[-2:]
    width = kv_refs[0].shape[2]
    own = own_slot(split) if split > 1 else 0
    for distance, ref in enumerate(kv_refs):
        part = pl.ds(pl.multiple_of((own ^ distance) * width, HD), width)
        ref[0] = k_ref[:, part]
        ref[1] = v_ref[:, part]
    f32 = jnp.float32
    odd = lax.axis_index("ctx") % 2

    def edge(refs, start, at):
        pair = [ref[...].astype(f32)[start : start + HALO] for ref in refs[at : at + 2]]
        return jnp.concatenate(pair, axis=0)

    for at in range(0, streams, 2):
        rows = slice(at * HALO, (at + 2) * HALO)
        head, tail = edge(first_refs, 0, at), edge(last_refs, HALO, at)
        inner_ref[rows] = jnp.where(odd == 1, head, tail).astype(inner_ref.dtype)
        outer_ref[rows] = jnp.where(odd == 1, tail, head).astype(outer_ref.dtype)


def pack_edges(keys, values, streams, slots, split):
    rows, columns = keys.shape
    tokens, channels = streams[0].shape
    edge = 2 * HALO
    count = len(streams)
    whole = pl.BlockSpec((rows, columns), lambda i: (0, 0))
    first = pl.BlockSpec((edge, channels), lambda i: (0, 0))
    last = pl.BlockSpec((edge, channels), lambda i: (tokens // edge - 1, 0))
    halo = (count * HALO, channels)
    laid = (2, rows, columns // slots)
    return pl.pallas_call(
        functools.partial(pack_edges_kernel, count, split),
        grid=(1,),
        in_specs=[whole] * 2 + [first] * count + [last] * count,
        out_specs=[pl.BlockSpec(laid, lambda i: (0, 0, 0))] * slots
        + [pl.BlockSpec(halo, lambda i: (0, 0))] * 2,
        out_shape=[jax.ShapeDtypeStruct(laid, keys.dtype)] * slots
        + [jax.ShapeDtypeStruct(halo, keys.dtype)] * 2,
        name="pack_edges",
    )(keys, values, *streams, *streams)


def join_kernel(split, *refs):
    parts, target = refs[:-1], refs[-1]
    piece = parts[0].shape[1]
    slot = own_slot(split)
    for distance, ref in enumerate(parts):
        held = slot ^ distance
        place = held % split * (len(parts) // split) + held // split
        target[:, pl.ds(pl.multiple_of(place * piece, 32), piece)] = ref[...]


def join(parts, split):
    pair, rows, width = parts[0].shape
    return pl.pallas_call(
        functools.partial(join_kernel, split),
        out_shape=jax.ShapeDtypeStruct((pair, rows * len(parts), width), parts[0].dtype),
        name="join",
    )(*parts)


def pack_rows_kernel(split, q_ref, g_ref, *refs):
    outs, sems = refs[:-1], refs[-1]
    width = outs[0].shape[1] // 2
    slot = own_slot(split)
    copies = []
    for distance, out in enumerate(outs):
        part = pl.ds(pl.multiple_of((slot ^ distance) * width, HD), width)
        for ref, first in ((q_ref, 0), (g_ref, width)):
            copies.append(
                pltpu.make_async_copy(
                    ref.at[:, part], out.at[:, first : first + width], sems.at[len(copies)]
                )
            )
    for copy in copies:
        copy.start()
    for copy in copies:
        copy.wait()


def pack_rows(queries, grads, slots, split):
    rows, columns = queries.shape
    shape = jax.ShapeDtypeStruct((rows, 2 * columns // slots), queries.dtype)
    return pl.pallas_call(
        functools.partial(pack_rows_kernel, split),
        in_specs=[pl.BlockSpec(memory_space=pltpu.VMEM)] * 2,
        out_specs=[pl.BlockSpec(memory_space=pltpu.HBM)] * slots,
        out_shape=[shape] * slots,
        scratch_shapes=[pltpu.SemaphoreType.DMA((2 * slots,))],
        compiler_params=pltpu.CompilerParams(vmem_limit_bytes=VMEM_PACK),
        name="pack_rows",
    )(queries, grads)


def attention_kernel(pieces, distances, groups, prior, *refs):
    (info_ref, lengths_ref), refs = refs[:2], refs[2:]
    steps = len(distances)
    qg_refs, refs = refs[: steps * groups], refs[steps * groups :]
    piece_refs, refs = refs[:pieces], refs[pieces:]
    prior_refs, refs = refs[: prior * pieces], refs[prior * pieces :]
    out_refs, refs = refs[:steps], refs[steps:]
    term_refs, refs = refs[:pieces], refs[pieces:]
    kv, k_t, v_t, dk_sum, dv_sum, scores, weights, dscores = refs[:8]
    q_rows, q_t, g_rows, g_t, peak8, total8, out_t, dq_t = refs[8:]
    step = pl.program_id(0)
    blocks = k_t.shape[0]
    run = qg_refs[0].shape[0]
    columns = qg_refs[0].shape[1] // 2
    heads = columns // HD
    size = groups * run
    rows = size * heads
    f32 = jnp.float32
    bf16 = jnp.bfloat16
    chunks = [slice(start, min(start + 256, rows)) for start in range(0, rows, 256)]
    ctx = lax.axis_index("ctx")
    own = lax.axis_index("tp") if groups > 1 else 0
    origin = info_ref[0]

    def record_start(position):
        ends = 0
        start = position * 0
        for record in range(lengths_ref.shape[0]):
            ends = ends + lengths_ref[record]
            start = jnp.where(position >= ends, ends, start)
        return start

    def rows_of(b):
        return pl.ds(pl.multiple_of(b * KB, KB), KB)

    def piece_rows(index):
        count = piece_refs[index].shape[1]
        return pl.ds(pl.multiple_of(info_ref[1 + index], 64), count)

    @pl.when(step == 0)
    def _():
        filled = sum(ref.shape[1] for ref in piece_refs)
        if filled < kv.shape[0]:
            kv[filled:] = jnp.zeros((kv.shape[0] - filled, 2 * HD), bf16)
        for index in range(pieces):
            kv[piece_rows(index), :HD] = piece_refs[index][0]
            kv[piece_rows(index), HD:] = piece_refs[index][1]
        dk_sum[...] = jnp.zeros(dk_sum.shape, f32)
        dv_sum[...] = jnp.zeros(dv_sum.shape, f32)

        def prepare(b, carry):
            k_t[b] = kv[rows_of(b), :HD].T
            v_t[b] = kv[rows_of(b), HD:].T
            return carry

        lax.fori_loop(0, blocks, prepare, 0)

    for which in range(steps):

        @pl.when(step == which)
        def _():
            for a in range(groups):
                ref = qg_refs[which * groups + a]
                for h in range(heads):
                    part = slice(h * size + a * run, h * size + (a + 1) * run)
                    q_rows[part] = ref[:, h * HD : (h + 1) * HD]
                    g_rows[part] = ref[:, columns + h * HD : columns + (h + 1) * HD]

    q_t[...] = q_rows[...].T
    g_t[...] = g_rows[...].T
    peak8[...] = jnp.full((8, rows), NEG, f32)
    total8[...] = jnp.zeros((8, rows), f32)
    out_t[...] = jnp.zeros((HD, rows), f32)
    dq_t[...] = jnp.zeros((HD, rows), f32)

    distance = distances[0]
    for which in range(1, steps):
        distance = jnp.where(step == which, distances[which], distance)
    q_first = (ctx ^ distance) * size
    low_first = record_start(q_first)
    low_last = record_start(q_first + (size - 1))
    token = lax.broadcasted_iota(jnp.int32, (1, rows), 1) % size
    if groups > 1:
        token = ((token // run) ^ own) * run + token % run
    pos = q_first + token
    low = record_start(pos)
    first = (low_first - origin) // KB
    last = (q_first + (size - 1) - origin) // KB + 1

    def fold(values, combine):
        result = values[0:8]
        for start in range(8, values.shape[0], 8):
            result = combine(result, values[start : start + 8])
        return result

    def score_pass(b, carry):
        base = origin + b * KB
        whole = (base + (KB - 1) <= q_first) & (base >= low_last)

        @pl.when(whole)
        def _():
            for part in chunks:
                s = jnp.dot(kv[rows_of(b), :HD], q_t[:, part], preferred_element_type=f32)
                scores[b - first, :, part] = s
                peak8[:, part] = jnp.maximum(peak8[:, part], fold(s, jnp.maximum))

        @pl.when(jnp.logical_not(whole))
        def _():
            for part in chunks:
                s = jnp.dot(kv[rows_of(b), :HD], q_t[:, part], preferred_element_type=f32)
                key_pos = base + lax.broadcasted_iota(jnp.int32, s.shape, 0)
                allowed = (key_pos <= pos[:, part]) & (key_pos >= low[:, part])
                s = jnp.where(allowed, s, NEG)
                scores[b - first, :, part] = s
                peak8[:, part] = jnp.maximum(peak8[:, part], fold(s, jnp.maximum))

        return carry

    lax.fori_loop(first, last, score_pass, 0)
    peak = jnp.max(peak8[...], axis=0, keepdims=True) * TO_EXP2

    def weight_pass(b, carry):
        for part in chunks:
            w = jnp.exp2(scores[b - first, :, part] * TO_EXP2 - peak[:, part])
            total8[:, part] += fold(w, jnp.add)
            w_b = w.astype(bf16)
            weights[b - first, :, part] = w_b
            out_t[:, part] += jnp.dot(v_t[b], w_b, preferred_element_type=f32)
        return carry

    lax.fori_loop(first, last, weight_pass, 0)
    inverse = 1.0 / jnp.sum(total8[...], axis=0, keepdims=True)
    out_b = (out_t[...] * inverse).astype(bf16)
    g_wide = g_t[...].astype(f32)
    delta = jnp.sum(g_wide * out_b.astype(f32), axis=0, keepdims=True) * inverse
    g_scaled = (g_wide * inverse).astype(bf16)
    g_t[...] = g_scaled
    g_rows[...] = g_scaled.T

    def give(wide, first):
        for which in range(steps):

            @pl.when(step == which)
            def _():
                for a in range(groups):
                    to = pl.ds(pl.multiple_of((own ^ a) * run, 16), run)
                    for h in range(heads):
                        start = h * size + a * run
                        out_refs[which][to, first + h * HD : first + (h + 1) * HD] = wide[
                            start : start + run
                        ]

    give(out_b.T, 0)

    def grad_pass(b, carry):
        for part in chunks:
            dp = jnp.dot(kv[rows_of(b), HD:], g_t[:, part], preferred_element_type=f32)
            w = weights[b - first, :, part].astype(f32)
            dscores[:, part] = (w * (dp - delta[:, part])).astype(bf16)
        dv_sum[rows_of(b)] += jnp.dot(weights[b - first], g_rows[...], preferred_element_type=f32)
        dk_sum[rows_of(b)] += jnp.dot(dscores[...], q_rows[...], preferred_element_type=f32)
        dq_t[...] += jnp.dot(k_t[b], dscores[...], preferred_element_type=f32)
        return carry

    lax.fori_loop(first, last, grad_pass, 0)
    give((dq_t[...] * SCALE).astype(bf16).T, heads * HD)

    @pl.when(step == steps - 1)
    def _():
        for index in range(pieces):
            dk = dk_sum[piece_rows(index)] * SCALE
            dv = dv_sum[piece_rows(index)]
            if prior:
                dk = dk + prior_refs[index][0].astype(f32)
                dv = dv + prior_refs[index][1].astype(f32)
            term_refs[index][0] = dk.astype(bf16)
            term_refs[index][1] = dv.astype(bf16)


def attention(qg_pieces, kv_pieces, info, lengths, distances, most, prior=()):
    run, columns = qg_pieces[0].shape
    steps = len(distances)
    groups = len(qg_pieces) // steps
    size = groups * run
    heads = columns // (2 * HD)
    rows = size * heads
    pieces = len(kv_pieces)
    keys = -(-sum(part.shape[1] for part in kv_pieces) // KB) * KB
    blocks = keys // KB
    live = min(blocks, (most + size - 3) // KB + 2)
    bf16 = jnp.bfloat16
    f32 = jnp.float32

    def still(shape):
        return pl.BlockSpec(shape, lambda i, *_: (0,) * len(shape))

    kv_specs = [still(part.shape) for part in kv_pieces]
    given = (size, columns)
    pairs = size * steps * heads * keys
    results = pl.pallas_call(
        functools.partial(attention_kernel, pieces, distances, groups, 1 if prior else 0),
        grid_spec=pltpu.PrefetchScalarGridSpec(
            num_scalar_prefetch=2,
            grid=(steps,),
            in_specs=[still((run, columns))] * len(qg_pieces)
            + kv_specs
            + (kv_specs if prior else []),
            out_specs=[still(given)] * steps + kv_specs,
            scratch_shapes=[
                pltpu.VMEM((keys, 2 * HD), bf16),
                pltpu.VMEM((blocks, HD, KB), bf16),
                pltpu.VMEM((blocks, HD, KB), bf16),
                pltpu.VMEM((keys, HD), f32),
                pltpu.VMEM((keys, HD), f32),
                pltpu.VMEM((live, KB, rows), f32),
                pltpu.VMEM((live, KB, rows), bf16),
                pltpu.VMEM((KB, rows), bf16),
                pltpu.VMEM((rows, HD), bf16),
                pltpu.VMEM((HD, rows), bf16),
                pltpu.VMEM((rows, HD), bf16),
                pltpu.VMEM((HD, rows), bf16),
                pltpu.VMEM((8, rows), f32),
                pltpu.VMEM((8, rows), f32),
                pltpu.VMEM((HD, rows), f32),
                pltpu.VMEM((HD, rows), f32),
            ],
        ),
        out_shape=[jax.ShapeDtypeStruct(given, bf16)] * steps
        + [jax.ShapeDtypeStruct(part.shape, bf16) for part in kv_pieces],
        compiler_params=pltpu.CompilerParams(vmem_limit_bytes=VMEM),
        cost_estimate=pl.CostEstimate(
            flops=48 * HD * pairs, bytes_accessed=32 * rows * HD * steps, transcendentals=pairs
        ),
        name="attention",
    )(info, lengths, *qg_pieces, *kv_pieces, *prior)
    return results[:steps], results[steps:]


def settle_kernel(split, *refs):
    piece_refs, (out_ref, dq_ref) = refs[:split], refs[split:]
    width = piece_refs[0].shape[1] // 2
    core = lax.axis_index("ctx") % split
    for distance in range(split):
        to = pl.ds(pl.multiple_of((core ^ distance) * width, HD), width)
        out_ref[:, to] = piece_refs[distance][:, :width]
        dq_ref[:, to] = piece_refs[distance][:, width:]


def settle(parts):
    split = len(parts)
    rows, width = parts[0].shape
    shape = jax.ShapeDtypeStruct((rows, width * split // 2), parts[0].dtype)
    return pl.pallas_call(
        functools.partial(settle_kernel, split),
        out_shape=[shape] * 2,
        compiler_params=pltpu.CompilerParams(vmem_limit_bytes=VMEM),
        name="settle",
    )(*parts)


def body(
    record_lengths,
    query_heads,
    key_heads,
    value_heads,
    out_grad,
    gate_input,
    key_input,
    value_input,
    hyena_grad,
    short_filter,
    long_filter,
):
    ctx = lax.axis_size("ctx")
    tp = lax.axis_size("tp")
    own_ctx = lax.axis_index("ctx")
    piece = query_heads.shape[0]
    tokens = piece * tp
    window = tokens * ctx
    most = window // 2 + 192
    split = PLANE if (KVH // tp) % PLANE == 0 else 1
    slots = tp * split
    kv_local = KVH // slots
    assert kv_local == 1 and tokens % 192 == 0
    unit = tokens * split
    lanes = PLANE // split
    plane = unit * lanes
    reach = (most - 1) // plane
    tail = -(-(most - 1 - reach * plane) // 192) * 192
    core = own_ctx % split
    lane = own_ctx // split % lanes
    level = own_ctx // PLANE
    f32 = jnp.float32
    bf16 = jnp.bfloat16

    members = [
        [t * ctx + n * split + c for t in range(tp) for c in range(split)]
        for n in range(ctx // split)
    ]

    def share(laid):
        return lax.all_to_all(
            laid, ("tp", "ctx"), 0, 0, axis_index_groups=members, tiled=True
        )

    permute = functools.partial(lax.ppermute, axis_name="ctx")

    def across(values, distance):
        return permute(values, perm=[(i, i ^ (distance * split)) for i in range(ctx)])

    def up(values):
        return permute(values, perm=[(i, i + PLANE) for i in range(ctx - PLANE)])

    def down(values):
        return permute(values, perm=[(i + PLANE, i) for i in range(ctx - PLANE)])

    def swap(values, distance):
        return permute(values, perm=[(i, i ^ distance) for i in range(ctx)])

    far = (reach + 1) * PLANE - (lanes - 1) * split
    far_pairs = [
        (i, i + far) for i in range(ctx - far) if i // split % lanes == lanes - 1
    ]

    streams = (gate_input, key_input, value_input, hyena_grad)
    *kv, inner, outer = pack_edges(key_heads, value_heads, streams, slots, split)
    inner = permute(inner, perm=[(i, i ^ 1) for i in range(ctx)])
    outer = permute(
        outer, perm=[(i, (i + 1 if i % 2 else i - 1)) for i in range(1, ctx - 1)]
    )

    def exchange(values, which):
        for distance in which:
            far_t, far_c = distance // split, distance % split
            perm = [
                (i * tp + t, (i ^ far_c) * tp + (t ^ far_t))
                for t in range(tp)
                for i in range(ctx)
            ]
            values[distance] = lax.ppermute(values[distance], ("ctx", "tp"), perm)

    pairwise = split > 1 and piece % 32 == 0
    if pairwise:
        kv[0], query_heads = lax.optimization_barrier((kv[0], query_heads))
        qg = list(pack_rows(query_heads, out_grad, slots, split))
        exchange(kv, range(1, slots))
        kv[0], qg[0] = lax.optimization_barrier((kv[0], qg[0]))
        own_kv = join(kv, split)
    else:
        kv = share(jnp.stack(kv)).reshape(tp, split, 2, piece, kv_local * HD)
        own_kv = kv.transpose(2, 1, 0, 3, 4).reshape(2, unit, kv_local * HD)
        cut = [part.reshape(piece, slots, -1) for part in (query_heads, out_grad)]
        laid = jnp.concatenate(cut, axis=2).transpose(1, 0, 2)
        qg = share(laid).reshape(tp, split, piece, -1).transpose(1, 0, 2, 3)
        qg = list(qg.reshape(split, tokens, -1))

    calls = [(split - 1, 0), (split // 2, split // 2 - 1)] if split > 1 else [(0,)]

    def rows_for(call):
        return [a * split + c for c in calls[call] for a in range(tp)]

    filters = (short_filter, long_filter)
    columns = [own_kv]
    if pairwise:
        first = [d for d in rows_for(0) if d]
        own_kv, *held = lax.optimization_barrier((own_kv,) + tuple(qg[d] for d in first))
        columns = [own_kv]
        for distance, value in zip(first, held):
            qg[distance] = value
        exchange(qg, first)
    for hop in range(reach):
        coming = up(columns[-1])
        if hop == reach - 1:
            inner, columns[-1] = lax.optimization_barrier((inner, columns[-1]))
            hyena_outs = hyena(streams, inner, outer, *filters, 0, 4)
            coming, first_out = lax.optimization_barrier((coming, hyena_outs[0]))
            hyena_outs = [first_out] + list(hyena_outs[1:])
        columns.append(coming)
    tail_kv = own_kv[:, unit - tail :]
    tail_kv, columns[1] = lax.optimization_barrier((tail_kv, columns[1]))
    tail_kv = permute(tail_kv, perm=far_pairs)
    pieces = [tail_kv]
    places = [jnp.int32(0)]
    for back in range(reach + 1):
        for distance in range(lanes):
            held = columns[back]
            pieces.append(held if distance == 0 else across(held, distance))
            places.append(tail + (reach - back) * plane + (lane ^ distance) * unit)
    origin = (level - reach) * plane - tail
    info = jnp.stack([origin] + places).astype(jnp.int32)

    owners = [None] * split
    terms = ()
    arrived = None
    for call, distances in enumerate(calls):
        if call:
            exchange(qg, rows_for(call))
        held = [qg[d] for d in rows_for(call)] if pairwise else qg
        outs, terms = attention(held, pieces, info, record_lengths, distances, most, terms)
        if arrived is not None:
            at = 1 + reach * lanes
            terms = list(terms)
            arrived, terms[at] = lax.optimization_barrier((arrived, terms[at]))
            owners[calls[0][0]] = arrived
        for distance, value in zip(distances, outs):
            owners[distance] = swap(value, distance) if distance else value
        if call == 0 and split > 1:
            arrived = owners[distances[0]]
    attn_out, grad_query = settle(owners)

    def plane_sum(back):
        at = 1 + back * lanes
        total = terms[at].astype(f32)
        for distance in range(1, lanes):
            total = total + across(terms[at + distance], distance).astype(f32)
        return total

    tail_term = permute(terms[0], perm=[(j, i) for i, j in far_pairs])
    running = plane_sum(reach).astype(bf16)
    for back in range(reach - 1, -1, -1):
        coming = down(running)
        if back == reach - 1:
            inner, running = lax.optimization_barrier((inner, running))
            hyena_outs = hyena(streams, inner, outer, *filters, 4, 4, hyena_outs)
            coming, first_out = lax.optimization_barrier((coming, hyena_outs[0]))
            hyena_outs = [first_out] + list(hyena_outs[1:])
        running = plane_sum(back) + coming.astype(f32)
        if back:
            running = running.astype(bf16)
    running, attn_out = lax.optimization_barrier((running, attn_out))
    owned = jnp.concatenate(
        [running[:, : unit - tail], running[:, unit - tail :] + tail_term.astype(f32)], axis=1
    ).astype(bf16)

    parts = []
    for distance in range(split):
        held = lax.dynamic_slice_in_dim(owned, (core ^ distance) * tokens, tokens, 1)
        parts.append(swap(held, distance) if distance else held)
    bit = 1
    while bit < split:
        parts = [
            jnp.where(core & bit != 0, parts[index ^ bit], parts[index]) for index in range(split)
        ]
        bit = 2 * bit
    grads = jnp.concatenate(parts, axis=2)
    return (attn_out, grad_query, grads[0], grads[1]) + tuple(hyena_outs)


def solution(mesh):
    rows = P(("ctx", "tp"), None)
    both = P("ctx", "tp")
    return jax.shard_map(
        body,
        mesh=mesh,
        in_specs=(P(), rows, rows, rows, rows, both, both, both, both)
        + (P(None, None, "tp"), P(None, "tp")),
        out_specs=(both,) * 8,
        check_vma=False,
    )
```
